32 devices in a mesh: tile: 8 (over z, x), mp: 4 (over y, core).
Axes of the slice: x: 2, y: 2, z: 4, core: 2. Of those that a mesh axis runs over, the one named last changes fastest.
Arguments:
- latent: bfloat16 [96, 384], P('tile'), may hold values from -19 to 19, as said below
- reward_grad: float32 [96, 384], P('tile'), may hold values from -6 to 6
- curvature: float32 [96, 384], P('tile'), may hold values from 0.3 to 3
- offsets: int32 [16, 2], P('tile'), may hold values from 0 to 64, as said below
- counts: int32 [96, 96], P('tile'), may hold values from 1 to 4, as said below
- w_in: bfloat16 [16, 640], replicated, may hold values from -3.2 to 3.2, as said below
- w_value: bfloat16 [640, 2560], P(None, 'mp'), may hold values from -0.25 to 0.25
- w_gate: bfloat16 [640, 2560], P(None, 'mp'), may hold values from -0.25 to 0.25
- w_down: bfloat16 [2560, 640], P('mp'), may hold values from -0.125 to 0.125
- w_out: bfloat16 [640, 16], replicated, may hold values from -0.25 to 0.25
Outputs:
- blended: float32 [96, 384], P('tile')
- grad_in: float32 [16, 640], replicated
- grad_value: float32 [640, 2560], P(None, 'mp')
- grad_gate: float32 [640, 2560], P(None, 'mp')
- grad_down: float32 [2560, 640], P('mp')
- grad_out: float32 [640, 16], replicated
The draws below stay inside these ranges and needn't reach their ends.
Inputs may be any that keep to these rules, and one draw needn't show every extreme that they name: `offsets`: the corners are the points of a grid of 4 by 4 points spaced 24, each point taken by exactly one tile in a random order, each moved by at most 4 along each direction; the grid's first row and column stay at 0 and its last row and column are clamped to 64 and 64. The tiles cover every cell of the canvas. `counts`: the number of tiles whose 32 x 32 square holds the cell. `latent`: Real-valued. `w_in`: Real-valued.
All inputs are finite; a program needn't handle non-finite values.
Results may differ from the reference program's by a relative error of at most 0.003.
The reference program's roundings to bfloat16 on the way count: a program that leaves them out, or rounds other values in their place, can miss the bound.
Values may be sent and summed in bfloat16 or wider, within the bound.
No kernel may reach another device: no remote copies, remote signals or barrier semaphores. Data moves between devices by JAX's collectives and lax.ppermute only.
A program may use at most 64 MiB of HBM per device.

```python
import math
import jax
import jax.numpy as jnp
from jax import lax

C = 4
D = 640
FF = 2560
S = 32
SPACING = 24
JITTER = 4
F = 16
TT = 256
H = 96
W = 96
TILES = 16


def grid_corners(key):
    base_key = jax.random.fold_in(key, 11)
    row_key, col_key, order_key = jax.random.split(base_key, 3)
    grid_cols = W // SPACING
    row_jitter = jax.random.randint(row_key, (TILES,), -JITTER, JITTER + 1)
    col_jitter = jax.random.randint(col_key, (TILES,), -JITTER, JITTER + 1)
    grid_cells = jax.random.permutation(order_key, TILES)
    grid_row = grid_cells // grid_cols
    grid_col = grid_cells % grid_cols
    row_start = jnp.where(grid_row == 0, 0, jnp.clip(grid_row * SPACING + row_jitter, 0, H - S))
    col_start = jnp.where(grid_col == 0, 0, jnp.clip(grid_col * SPACING + col_jitter, 0, W - S))
    return jnp.stack([row_start, col_start], axis=1).astype(jnp.int32)


def draw_offsets(key, part):
    return grid_corners(key)


def draw_counts(key, part):
    corners = grid_corners(key)
    row_ids = jnp.arange(H, dtype=jnp.int32)
    col_ids = jnp.arange(W, dtype=jnp.int32)
    row_cover = ((row_ids[None, :] >= corners[:, 0:1]) & (row_ids[None, :] < corners[:, 0:1] + S)).astype(jnp.int32)
    col_cover = ((col_ids[None, :] >= corners[:, 1:2]) & (col_ids[None, :] < corners[:, 1:2] + S)).astype(jnp.int32)
    return jnp.sum(row_cover[:, :, None] * col_cover[:, None, :], axis=0).astype(jnp.int32)


def draw_latent(key, part):
    base_key, spread_key = jax.random.split(jax.random.fold_in(key, 23))
    spread = jnp.exp(jax.random.uniform(spread_key, (H, W * C), minval=-1.15, maxval=1.15))
    values = jnp.clip(jax.random.normal(base_key, (H, W * C)), -6.0, 6.0)
    return (values * spread).astype(jnp.float32).astype(jnp.bfloat16)


def draw_w_in(key, part):
    base_key, column_key = jax.random.split(jax.random.fold_in(key, 37), 2)
    column_scale = jnp.exp(jax.random.uniform(column_key, (1, D), minval=-1.15, maxval=1.15))
    values = jnp.clip(jax.random.normal(base_key, (F, D)), -4.0, 4.0)
    return (values * column_scale * F ** (-0.5)).astype(jnp.float32).astype(jnp.bfloat16)


def steps_of(own_key, dims, pieces, least, top_value):
    def one(axis_at, blocks):
        heights = jax.random.uniform(jax.random.fold_in(jax.random.fold_in(own_key, 6), axis_at), (blocks,), jnp.float32, least / len(pieces), top_value / len(pieces))
        return jnp.repeat(jnp.exp(heights), dims[axis_at] // blocks).reshape((-1,) + (1,) * (len(dims) - axis_at - 1))

    factor_of = one(*pieces[0])
    for cut in pieces[1:]:
        factor_of = factor_of * one(*cut)
    return factor_of


def bell_draw(stream_key, shape, width, bound, pieces=(), kind=jnp.bfloat16):
    result = jax.random.normal(stream_key, shape, jnp.float32) * width
    if len(pieces) > 0:
        result = steps_of(stream_key, shape, pieces, -0.22, 0.18) * result
    return jnp.clip(result, min=-bound, max=bound).astype(kind)


def setup_inputs(seed: int = 0) -> dict:
    splits = jax.random.split(jax.random.key(seed), 11)
    latent = draw_latent(jax.random.fold_in(splits[10], 71), 0)
    reward_grad = bell_draw(splits[1], (H, W * C), 1.0, 6.0, ((0, 8),), jnp.float32)
    curvature = jnp.clip(jnp.exp(math.log(3.0) - 2.3025851 * jax.random.uniform(splits[2], (H, W * C), jnp.float32) ** steps_of(splits[2], (H, W * C), ((0, 8),), -0.2, 0.2)), 0.3, 3.0)
    offsets = draw_offsets(jax.random.fold_in(splits[10], 71), 0)
    counts = draw_counts(jax.random.fold_in(splits[10], 71), 0)
    w_in = draw_w_in(jax.random.fold_in(splits[10], 71), 0)
    w_value = bell_draw(splits[6], (D, FF), D ** -0.5, 0.25, ((1, 4),))
    w_gate = bell_draw(splits[7], (D, FF), D ** -0.5, 0.25, ((1, 4),))
    w_down = bell_draw(splits[8], (FF, D), FF ** -0.5, 0.125, ((0, 4),))
    w_out = bell_draw(splits[9], (D, F), D ** -0.5, 0.25)
    return dict(latent=latent, reward_grad=reward_grad, curvature=curvature, offsets=offsets, counts=counts, w_in=w_in, w_value=w_value, w_gate=w_gate, w_down=w_down, w_out=w_out)


layer_eps = 1e-05
root_half = 0.7071067811865476
inv_root_two_pi = 0.3989422804014327

def product(left, right):
    return jnp.dot(left.astype(jnp.float32), right.astype(jnp.float32), preferred_element_type=jnp.float32)

def gelu_value(inputs):
    return 0.5 * inputs * (1.0 + lax.erf(inputs * root_half))

def gelu_slope(inputs):
    return 0.5 * (1.0 + lax.erf(inputs * root_half)) + inputs * jnp.exp(-0.5 * inputs * inputs) * inv_root_two_pi

def patchify(cropped, channels):
    half_side = cropped.shape[0] // 2
    return cropped.reshape(half_side, 2, half_side, 2 * channels).transpose(0, 2, 1, 3).reshape(half_side * half_side, 4 * channels)

def unpatch(tokens, tile_side, channels):
    half_side = tile_side // 2
    token_rows = tokens.shape[0] // half_side
    return tokens.reshape(token_rows, half_side, 2, 2 * channels).transpose(0, 2, 1, 3).reshape(2 * token_rows, tile_side * channels)

def layer_norm(hidden):
    values = hidden.astype(jnp.float32)
    center = values - lax.optimization_barrier(jnp.mean(values, axis=-1, keepdims=True))
    variance = lax.optimization_barrier(jnp.mean(center * center, axis=-1, keepdims=True))
    inv_scale = lax.rsqrt(variance + layer_eps)
    return (center * inv_scale, inv_scale)

def norm_backward(normed, inv_scale, d_unit):
    centered = d_unit - lax.optimization_barrier(jnp.mean(d_unit, axis=-1, keepdims=True))
    return inv_scale * (centered - normed * lax.optimization_barrier(jnp.mean(d_unit * normed, axis=-1, keepdims=True)))

def forward_tile(patches, weights):
    w_in, w_value, w_gate, w_down, w_out = weights
    hidden = product(patches, w_in).astype(jnp.bfloat16)
    normed, inv_scale = layer_norm(hidden)
    unit_in = normed.astype(jnp.bfloat16)
    value_proj = product(unit_in, w_value)
    gate_proj = product(unit_in, w_gate)
    active = (value_proj * gelu_value(gate_proj)).astype(jnp.bfloat16)
    ff_out = product(active, w_down)
    noise_pred = product(hidden, w_out) + jnp.dot(ff_out, w_out.astype(jnp.float32), precision=lax.Precision.HIGHEST)
    return (noise_pred, (hidden, normed, inv_scale, unit_in, value_proj, gate_proj, active, ff_out))

def backward_tile(patches, cot_tokens, saved, weights):
    w_in, w_value, w_gate, w_down, w_out = weights
    hidden, normed, inv_scale, unit_in, value_proj, gate_proj, active, ff_out = saved
    d_feat = product(cot_tokens, jnp.transpose(w_out))
    d_feat_b = d_feat.astype(jnp.bfloat16)
    d_active = product(d_feat_b, jnp.transpose(w_down))
    d_value = (d_active * gelu_value(gate_proj)).astype(jnp.bfloat16)
    d_gate = (d_active * value_proj * gelu_slope(gate_proj)).astype(jnp.bfloat16)
    d_unit = product(d_value, jnp.transpose(w_value)) + product(d_gate, jnp.transpose(w_gate))
    d_hidden = (d_feat + norm_backward(normed, inv_scale, d_unit)).astype(jnp.bfloat16)
    grad_in = product(jnp.transpose(patches), d_hidden)
    grad_value = product(jnp.transpose(unit_in), d_value)
    grad_gate = product(jnp.transpose(unit_in), d_gate)
    grad_down = product(jnp.transpose(active), d_feat_b)
    grad_out = product(jnp.transpose(hidden), cot_tokens) + jnp.dot(jnp.transpose(ff_out), cot_tokens.astype(jnp.float32), precision=lax.Precision.HIGHEST)
    return (grad_in, grad_value, grad_gate, grad_down, grad_out)

def reference(latent, reward_grad, curvature, offsets, counts, w_in, w_value, w_gate, w_down, w_out):
    weights = (w_in, w_value, w_gate, w_down, w_out)

    def crop_at(canvas, corner):
        return lax.dynamic_slice(canvas, (corner[0], corner[1] * C), (S, S * C))

    def predict(corner):
        patches = patchify(crop_at(latent, corner), C)
        noise_pred, saved = forward_tile(patches, weights)
        return unpatch(noise_pred, S, C)
    tile_noise = lax.map(predict, offsets)

    def place(canvas, item):
        corner, piece = item
        start = (corner[0], corner[1] * C)
        current = lax.dynamic_slice(canvas, start, (S, S * C))
        return (lax.dynamic_update_slice(canvas, current + piece, start), None)
    blend_total, unused = lax.scan(place, jnp.zeros((H, W * C), jnp.float32), (offsets, tile_noise))
    cover_count = jnp.repeat(counts, C, axis=1).astype(jnp.float32)
    blended = blend_total / cover_count
    scale_factor = 16.0 / math.sqrt(TILES * TT)
    cotangent = ((reward_grad - curvature * blended) / cover_count * scale_factor).astype(jnp.bfloat16)

    def accumulate(carry, corner):
        patches = patchify(crop_at(latent, corner), C)
        noise_pred, saved = forward_tile(patches, weights)
        cot_tokens = patchify(crop_at(cotangent, corner), C)
        terms = backward_tile(patches, cot_tokens, saved, weights)
        return (tuple((first + second for first, second in zip(carry, terms))), None)
    initial = (jnp.zeros((F, D), jnp.float32), jnp.zeros((D, FF), jnp.float32), jnp.zeros((D, FF), jnp.float32), jnp.zeros((FF, D), jnp.float32), jnp.zeros((D, F), jnp.float32))
    totals, unused_two = lax.scan(accumulate, initial, offsets)
    grad_in, grad_value, grad_gate, grad_down, grad_out = totals
    return (blended, grad_in, grad_value, grad_gate, grad_down, grad_out)
```

```python
import functools
import math

import jax
import jax.numpy as jnp
from jax import lax
from jax.experimental import pallas as pl
from jax.experimental.pallas import tpu as pltpu
from jax.sharding import PartitionSpec as P

S = 32
SPACING = 24


layer_eps = 1e-05
root_half = 0.7071067811865476
inv_root_two_pi = 0.3989422804014327
highest = lax.Precision.HIGHEST


def passed_along(shard, axis, by):
    peers = lax.axis_size(axis)
    pairs = [(i, i + by) for i in range(peers) if 0 <= i + by < peers]
    return lax.ppermute(shard, axis, pairs)


def gelu_value(inputs):
    return 0.5 * inputs * (1.0 + lax.erf(inputs * root_half))


def gelu_slope(inputs):
    return (
        0.5 * (1.0 + lax.erf(inputs * root_half))
        + inputs * jnp.exp(-0.5 * inputs * inputs) * inv_root_two_pi
    )


def patchify(cropped, channels):
    half_side = cropped.shape[0] // 2
    return (
        cropped.reshape(half_side, 2, half_side, 2 * channels)
        .transpose(0, 2, 1, 3)
        .reshape(half_side * half_side, 4 * channels)
    )


def unpatch(tokens, tile_side, channels):
    half_side = tile_side // 2
    token_rows = tokens.shape[0] // half_side
    return (
        tokens.reshape(token_rows, half_side, 2, 2 * channels)
        .transpose(0, 2, 1, 3)
        .reshape(2 * token_rows, tile_side * channels)
    )


def layer_norm(hidden):
    values = hidden.astype(jnp.float32)
    center = values - jnp.mean(values, axis=-1, keepdims=True)
    variance = jnp.mean(center * center, axis=-1, keepdims=True)
    inv_scale = lax.rsqrt(variance + layer_eps)
    return (center * inv_scale, inv_scale)


def norm_backward(normed, inv_scale, d_unit):
    centered = d_unit - jnp.mean(d_unit, axis=-1, keepdims=True)
    return inv_scale * (centered - normed * jnp.mean(d_unit * normed, axis=-1, keepdims=True))


def contract_rows(left, right):
    return lax.dot_general(
        left, right, (((0,), (0,)), ((), ())), preferred_element_type=jnp.float32
    )


def contract_rows_exact(left, right):
    return lax.dot_general(
        left, right, (((0,), (0,)), ((), ())), precision=highest, preferred_element_type=jnp.float32
    )


def contract_cols(left, right):
    return lax.dot_general(
        left, right, (((1,), (1,)), ((), ())), preferred_element_type=jnp.float32
    )


def crop_tiles(source, corners, row_base, tile_side, channels):

    def crop_one(corner):
        cropped = lax.dynamic_slice(
            source, (corner[0] - row_base, corner[1] * channels), (tile_side, tile_side * channels)
        )
        return patchify(cropped, channels)

    return jax.vmap(crop_one)(corners)


def place_tiles(canvas, pieces, corners, row_shift, channels):
    piece_rows = pieces.shape[1]
    piece_cols = pieces.shape[2]

    def add_tile(tile_index, current):
        corner = corners[tile_index]
        start_row = corner[0] + row_shift
        start_col = corner[1] * channels
        existing = lax.dynamic_slice(current, (start_row, start_col), (piece_rows, piece_cols))
        return lax.dynamic_update_slice(
            current, existing + pieces[tile_index], (start_row, start_col)
        )

    return lax.fori_loop(0, pieces.shape[0], add_tile, canvas)


def per_device_sharded(
    latent, reward_grad, curvature, offsets, counts, w_in, w_value, w_gate, w_down, w_out
):
    channels = w_in.shape[0] // 4
    model_width = w_in.shape[1]
    tile_side = S
    half_side = tile_side // 2
    token_count = half_side * half_side
    tiles_here = offsets.shape[0]
    slab_rows = latent.shape[0]
    canvas_cols = latent.shape[1]
    tile_devices = lax.axis_size("tile")
    model_devices = lax.axis_size("mp")
    tile_pos = lax.axis_index("tile")
    model_pos = lax.axis_index("mp")
    share_tokens = token_count // model_devices
    share_pixels = tile_side // model_devices
    scale_factor = 16.0 / math.sqrt(tiles_here * tile_devices * token_count)
    w_out_wide = w_out.astype(jnp.float32)
    cover_count = jnp.repeat(counts, channels, axis=1).astype(jnp.float32)
    placed_row = model_pos * share_pixels
    every_corner = lax.all_gather(offsets, "tile", axis=0, tiled=True)
    grid_cols = canvas_cols // (channels * SPACING)
    grid_cells = (every_corner[:, 0] + SPACING // 2) // SPACING * grid_cols + (
        every_corner[:, 1] + SPACING // 2
    ) // SPACING
    wanted = (
        tile_pos // 2 * grid_cols
        + tile_pos % 2 * tiles_here
        + jnp.arange(tiles_here, dtype=jnp.int32)
    )
    matched = (grid_cells[None, :] == wanted[:, None]).astype(jnp.int32)
    corners = jnp.sum(matched[:, :, None] * every_corner[None, :, :], axis=1)
    row_base = (tile_pos - 2) * slab_rows
    latent_parts = []
    for shift_by in (2, 1, 0, -1, -2):
        if shift_by == 0:
            latent_parts.append(latent)
        else:
            latent_parts.append(passed_along(latent, "tile", shift_by))
    latent_source = jnp.concatenate(latent_parts, axis=0)
    patches = crop_tiles(latent_source, corners, row_base, tile_side, channels)
    flat_patches = jnp.transpose(patches, (1, 0, 2)).reshape(token_count * tiles_here, 4 * channels)
    hidden = jnp.dot(flat_patches, w_in, preferred_element_type=jnp.float32).astype(jnp.bfloat16)
    normed, inv_scale = layer_norm(hidden)
    unit_in = normed.astype(jnp.bfloat16)
    value_proj = jnp.dot(unit_in, w_value, preferred_element_type=jnp.float32)
    gate_proj = jnp.dot(unit_in, w_gate, preferred_element_type=jnp.float32)
    active = (value_proj * gelu_value(gate_proj)).astype(jnp.bfloat16)
    active_grid = active.reshape(token_count, tiles_here, active.shape[1])

    def take_share(values):
        grid = values.reshape(token_count, tiles_here, values.shape[-1])
        picked = lax.dynamic_slice_in_dim(grid, model_pos * share_tokens, share_tokens, 0)
        return picked.reshape(share_tokens * tiles_here, values.shape[-1])

    hidden_share = take_share(hidden)
    row_block = active_grid.reshape(
        lax.axis_size("mp") * share_tokens * tiles_here, active_grid.shape[2]
    )
    ff_share = lax.psum_scatter(
        jnp.dot(row_block, w_down, preferred_element_type=jnp.float32).reshape(
            lax.axis_size("mp") * share_tokens, tiles_here, model_width
        ),
        "mp",
        scatter_dimension=0,
        tiled=True,
    ).reshape(share_tokens * tiles_here, model_width)
    noise_share = jnp.dot(hidden_share, w_out, preferred_element_type=jnp.float32) + jnp.dot(
        ff_share, w_out_wide, precision=highest, preferred_element_type=jnp.float32
    )
    noise_tiles = jnp.transpose(
        noise_share.reshape(share_tokens, tiles_here, w_out.shape[1]), (1, 0, 2)
    )

    def unpatch_share(tokens):
        return unpatch(tokens, tile_side, channels)

    noise_pieces = jax.vmap(unpatch_share)(noise_tiles)
    window_term = place_tiles(
        jnp.zeros((5 * slab_rows, canvas_cols), jnp.float32),
        noise_pieces,
        corners,
        placed_row - row_base,
        channels,
    )
    slab_sum = window_term[2 * slab_rows : 3 * slab_rows]
    for shift_by in (-2, -1, 1, 2):
        outgoing = window_term[(shift_by + 2) * slab_rows : (shift_by + 3) * slab_rows]
        slab_sum = slab_sum + passed_along(outgoing, "tile", shift_by)
    blend_total = lax.psum(slab_sum, "mp")
    blended = blend_total / cover_count
    cotangent = ((reward_grad - curvature * blended) / cover_count * scale_factor).astype(
        jnp.bfloat16
    )
    cot_parts = []
    for shift_by in (2, 1, 0, -1, -2):
        if shift_by == 0:
            cot_parts.append(cotangent)
        else:
            cot_parts.append(passed_along(cotangent, "tile", shift_by))
    cot_source = jnp.concatenate(cot_parts, axis=0)
    cot_patches = crop_tiles(cot_source, corners, row_base, tile_side, channels)
    cot_flat = jnp.transpose(cot_patches, (1, 0, 2)).reshape(token_count * tiles_here, 4 * channels)
    cot_share = take_share(cot_flat)
    d_feat = contract_cols(cot_flat, w_out)
    d_feat_b = d_feat.astype(jnp.bfloat16)
    d_active = contract_cols(d_feat_b, w_down)
    down_term = contract_rows(active, d_feat_b)
    d_value = (d_active * gelu_value(gate_proj)).astype(jnp.bfloat16)
    d_gate = (d_active * value_proj * gelu_slope(gate_proj)).astype(jnp.bfloat16)
    value_term = contract_rows(unit_in, d_value)
    gate_term = contract_rows(unit_in, d_gate)
    d_value_grid = d_value.reshape(token_count, tiles_here, d_value.shape[1])
    d_gate_grid = d_gate.reshape(token_count, tiles_here, d_gate.shape[1])
    value_block = d_value_grid.reshape(
        share_tokens * lax.axis_size("mp") * tiles_here, d_value.shape[1]
    )
    gate_block = d_gate_grid.reshape(
        share_tokens * lax.axis_size("mp") * tiles_here, d_gate.shape[1]
    )
    summed = contract_cols(value_block, w_value) + contract_cols(gate_block, w_gate)
    d_unit_share = (
        lax.psum_scatter(
            summed.reshape(share_tokens * lax.axis_size("mp"), tiles_here, model_width).astype(
                jnp.bfloat16
            ),
            "mp",
            scatter_dimension=0,
            tiled=True,
        )
        .astype(jnp.float32)
        .reshape(share_tokens * tiles_here, model_width)
    )
    d_hidden = (
        take_share(d_feat) + norm_backward(take_share(normed), take_share(inv_scale), d_unit_share)
    ).astype(jnp.bfloat16)
    in_term = contract_rows(take_share(flat_patches), d_hidden)
    out_term = contract_rows(hidden_share, cot_share) + contract_rows_exact(
        ff_share, cot_share.astype(jnp.float32)
    )
    grad_in, grad_out = lax.psum((in_term, out_term), ("tile", "mp"))
    grad_value, grad_gate, grad_down = lax.psum((value_term, gate_term, down_term), "tile")
    return (blended, grad_in, grad_value, grad_gate, grad_down, grad_out)


def dot_lanes(left, right):
    return lax.dot_general(
        left, right, (((1,), (1,)), ((), ())), preferred_element_type=jnp.float32
    )


def dot_plain(left, right):
    return lax.dot_general(
        left, right, (((1,), (0,)), ((), ())), preferred_element_type=jnp.float32
    )


def split_two(values):
    high = values.astype(jnp.bfloat16)
    low = (values - high.astype(jnp.float32)).astype(jnp.bfloat16)
    return high, low


def split_three(values):
    high = values.astype(jnp.bfloat16)
    rest = values - high.astype(jnp.float32)
    middle = rest.astype(jnp.bfloat16)
    low = (rest - middle.astype(jnp.float32)).astype(jnp.bfloat16)
    return high, middle, low


def fold_matrix(features, half_side):
    run = features // 2
    wide = 2 * half_side * run
    feature = lax.broadcasted_iota(jnp.int32, (features, wide), 0)
    place = lax.broadcasted_iota(jnp.int32, (features, wide), 1)
    own = place // (half_side * run) * run + place % run
    return jnp.where(feature == own, 1.0, 0.0).astype(jnp.bfloat16)


def column_mask(features, half_side):
    run = features // 2
    wide = 2 * half_side * run
    token = lax.broadcasted_iota(jnp.int32, (half_side * half_side, wide), 0)
    place = lax.broadcasted_iota(jnp.int32, (half_side * half_side, wide), 1)
    return token % half_side == place // run % half_side


def spread_tile(canvas_ref, row, col, half_side, features):
    run = features // 2
    width = half_side * run
    panels = canvas_ref.shape[0]
    cols = panels * width
    lanes = col * run // 2
    halves = []
    for parity in range(2):
        at = pl.ds(row + parity, half_side, stride=2)
        rows = jnp.concatenate([canvas_ref[panel, at, :] for panel in range(panels)], axis=1)
        rolled = pltpu.roll(rows, lax.rem(cols - lanes, cols), 1)
        halves.append(rolled[:, :width])
    pair = jnp.concatenate(halves, axis=1).astype(jnp.bfloat16)
    token = lax.broadcasted_iota(jnp.int32, (half_side * half_side, half_side), 0)
    patch_row = lax.broadcasted_iota(jnp.int32, (half_side * half_side, half_side), 1)
    repeat = jnp.where(token // half_side == patch_row, 1.0, 0.0).astype(jnp.bfloat16)
    repeated = dot_plain(repeat, pair)
    return jnp.where(column_mask(features, half_side), repeated, 0.0).astype(jnp.bfloat16)


def forward_kernel(
    half_side,
    corner_ref,
    latent_ref,
    w_in_ref,
    w_value_ref,
    w_gate_ref,
    w_down_ref,
    w_out_ref,
    canvas_ref,
    cover_ref,
    value_ref,
    gate_ref,
    normal_ref,
    unit_ref,
    active_ref,
    hidden_ref,
    patch_ref,
    scale_ref,
    latent_wide,
    w_in_spread,
    w_both,
    w_noise,
):
    tile = pl.program_id(0)
    features, model_width = w_in_ref.shape
    units = w_value_ref.shape[1]
    slabs, slab_rows, cols = latent_ref.shape
    panels, rows, width = canvas_ref.shape
    own_rows = rows // slabs

    @pl.when(tile == 0)
    def _prepare():
        for slab in range(slabs):
            own = latent_ref[slab].astype(jnp.float32)[:own_rows]
            for panel in range(panels):
                latent_wide[panel, slab * own_rows : (slab + 1) * own_rows, :] = own[
                    :, panel * width : (panel + 1) * width
                ]
        fold = fold_matrix(features, half_side)
        w_in_spread[...] = lax.dot_general(
            w_in_ref[...], fold, (((0,), (0,)), ((), ())), preferred_element_type=jnp.float32
        ).astype(jnp.bfloat16)
        w_both[:units, :] = w_value_ref[...].T
        w_both[units:, :] = w_gate_ref[...].T
        both = lax.dot_general(
            w_out_ref[...],
            w_down_ref[...],
            (((0,), (1,)), ((), ())),
            preferred_element_type=jnp.float32,
        )
        high, low = split_two(both)
        w_noise[:features, :] = high
        w_noise[features:, :] = low
        canvas_ref[...] = jnp.zeros_like(canvas_ref)
        cover_ref[...] = jnp.zeros_like(cover_ref)

    row = corner_ref[tile, 0]
    col = corner_ref[tile, 1]
    spread = spread_tile(latent_wide, row, col, half_side, features)
    fold = fold_matrix(features, half_side)
    patch_ref[0] = dot_lanes(fold, spread).astype(jnp.bfloat16)
    hidden_b = dot_lanes(w_in_spread[...], spread).astype(jnp.bfloat16)
    hidden_ref[0] = hidden_b
    hidden = hidden_b.astype(jnp.float32)
    center = hidden - jnp.mean(hidden, axis=0, keepdims=True)
    variance = jnp.mean(center * center, axis=0, keepdims=True)
    inv_scale = lax.rsqrt(variance + layer_eps)
    scale_ref[0] = inv_scale
    unit = (center * inv_scale).astype(jnp.bfloat16)
    unit_ref[0] = unit
    both = dot_plain(w_both[...], unit)
    value = both[:units]
    gate = both[units:]
    value_ref[0] = value
    gate_ref[0] = gate
    normal = 0.5 * (1.0 + lax.erf(gate * root_half))
    normal_ref[0] = normal
    active = (value * (gate * normal)).astype(jnp.bfloat16)
    active_ref[0] = active
    parts = dot_plain(w_noise[...], active)
    noise = parts[:features] + parts[features:]
    add_noise(canvas_ref, noise, row, col, half_side, features)

    @pl.when(lax.rem(tile, lax.axis_size("mp")) == lax.axis_index("mp"))
    def _direct():
        direct = lax.dot_general(
            w_out_ref[...], hidden_b, (((0,), (0,)), ((), ())), preferred_element_type=jnp.float32
        )
        add_noise(canvas_ref, direct, row, col, half_side, features)

    shape = cover_ref.shape
    row_at = lax.broadcasted_iota(jnp.int32, shape, 1) - row
    col_at = (
        lax.broadcasted_iota(jnp.int32, shape, 0) * width
        + lax.broadcasted_iota(jnp.int32, shape, 2)
        - col * (features // 4)
    )
    inside = (
        (row_at >= 0)
        & (row_at < 2 * half_side)
        & (col_at >= 0)
        & (col_at < half_side * features // 2)
    )
    cover_ref[...] += jnp.where(inside, 1.0, 0.0)


def add_noise(canvas_ref, noise, row, col, half_side, features):
    run = features // 2
    width = half_side * run
    panels = canvas_ref.shape[0]
    fold = fold_matrix(features, half_side)
    tall = lax.dot_general(
        jnp.concatenate(split_three(noise), axis=0),
        jnp.concatenate([fold, fold, fold], axis=0),
        (((0,), (0,)), ((), ())),
        preferred_element_type=jnp.float32,
    )
    kept = jnp.where(column_mask(features, half_side), tall, 0.0)
    pair = jnp.sum(kept.reshape(half_side, half_side, 2 * width), axis=1)
    blank = jnp.zeros((half_side, (panels - 1) * width), jnp.float32)
    for parity in range(2):
        placed = jnp.concatenate([pair[:, parity * width : (parity + 1) * width], blank], axis=1)
        placed = pltpu.roll(placed, col * run // 2, 1)
        at = pl.ds(row + parity, half_side, stride=2)
        for panel in range(panels):
            own = placed[:, panel * width : (panel + 1) * width]
            canvas_ref[panel, at, :] = canvas_ref[panel, at, :] + own


def backward_kernel(
    half_side,
    scale_factor,
    corner_ref,
    sum_ref,
    other_ref,
    reward_ref,
    cover_ref,
    w_value_ref,
    w_gate_ref,
    w_down_ref,
    w_out_ref,
    value_ref,
    gate_ref,
    normal_ref,
    unit_ref,
    active_ref,
    hidden_ref,
    patch_ref,
    scale_ref,
    blended_ref,
    grad_value_ref,
    grad_gate_ref,
    grad_down_ref,
    small_ref,
    cot_wide,
    w_out_spread,
    scaled_sum,
    mean_sum,
    active_sum,
    hidden_sum,
    patch_sum,
):
    tile = pl.program_id(0)
    model_width, features = w_out_ref.shape
    units = w_down_ref.shape[0]
    slabs, two_slabs, cols = reward_ref.shape
    slab_rows = two_slabs // 2
    panels, rows, width = sum_ref.shape

    @pl.when(tile == 0)
    def _prepare():
        for panel in range(panels):
            lanes = slice(panel * width, (panel + 1) * width)
            cover = cover_ref[panel]
            blended = (sum_ref[panel] + other_ref[panel]) / cover
            blended_ref[:, lanes] = blended
            reward = jnp.concatenate(
                [reward_ref[slab, :slab_rows, lanes] for slab in range(slabs)], axis=0
            )
            curvature = jnp.concatenate(
                [reward_ref[slab, slab_rows:, lanes] for slab in range(slabs)], axis=0
            )
            cot_wide[panel] = (
                ((reward - curvature * blended) / cover * scale_factor)
                .astype(jnp.bfloat16)
                .astype(jnp.float32)
            )
        w_out_spread[...] = dot_plain(w_out_ref[...], fold_matrix(features, half_side)).astype(
            jnp.bfloat16
        )
        for ref in (
            grad_value_ref,
            grad_gate_ref,
            scaled_sum,
            mean_sum,
            active_sum,
            hidden_sum,
            patch_sum,
        ):
            ref[...] = jnp.zeros_like(ref)

    spread = spread_tile(cot_wide, corner_ref[tile, 0], corner_ref[tile, 1], half_side, features)
    cot = dot_lanes(fold_matrix(features, half_side), spread).astype(jnp.bfloat16)
    d_feat_b = dot_lanes(w_out_spread[...], spread).astype(jnp.bfloat16)
    d_active = dot_plain(w_down_ref[...], d_feat_b)
    value = value_ref[0]
    gate = gate_ref[0]
    normal = normal_ref[0]
    unit = unit_ref[0]
    slope = normal + gate * jnp.exp(-0.5 * gate * gate) * inv_root_two_pi
    d_value = (d_active * (gate * normal)).astype(jnp.bfloat16)
    d_gate = (d_active * value * slope).astype(jnp.bfloat16)
    along = jnp.sum(
        d_value.astype(jnp.float32) * value + d_gate.astype(jnp.float32) * gate,
        axis=0,
        keepdims=True,
    ) * (1.0 / model_width)
    scaled = patch_ref[0].astype(jnp.float32) * scale_ref[0]
    left = jnp.concatenate([unit, *split_two(scaled)], axis=0)
    grads = dot_lanes(left, jnp.concatenate([d_value, d_gate], axis=0))
    grad_value_ref[...] += grads[:model_width, :units]
    grad_gate_ref[...] += grads[:model_width, units:]
    scaled_sum[...] += grads[model_width:]
    mean_sum[...] += dot_lanes(jnp.concatenate(split_two(scaled * along), axis=0), unit)
    active_sum[...] += dot_lanes(cot, active_ref[0])

    @pl.when(lax.rem(tile, lax.axis_size("mp")) == lax.axis_index("mp"))
    def _direct():
        hidden_sum[...] += dot_lanes(cot, hidden_ref[0])
        patch_sum[...] += dot_lanes(patch_ref[0], cot)

    @pl.when(tile == pl.num_programs(0) - 1)
    def _finish():
        active_two = jnp.concatenate(split_two(active_sum[...]), axis=0)
        w_out_two = jnp.concatenate([w_out_ref[...], w_out_ref[...]], axis=1)
        grad_down_ref[...] = lax.dot_general(
            active_two, w_out_two, (((0,), (1,)), ((), ())), preferred_element_type=jnp.float32
        )
        through = dot_plain(active_two, w_down_ref[...])
        small_ref[features:] = hidden_sum[...] + through[:features] + through[features:]
        scaled_both = scaled_sum[:features] + scaled_sum[features:]
        scaled_two = jnp.concatenate(split_two(scaled_both), axis=0)
        moved = dot_lanes(scaled_two[:, :units], w_value_ref[...]) + dot_lanes(
            scaled_two[:, units:], w_gate_ref[...]
        )
        moved = moved[:features] + moved[features:]
        patch_two = jnp.concatenate(split_two(patch_sum[...]), axis=0)
        direct = dot_lanes(patch_two, w_out_ref[...])
        small_ref[:features] = (
            direct[:features]
            + direct[features:]
            + moved
            - jnp.mean(moved, axis=1, keepdims=True)
            - mean_sum[:features]
            - mean_sum[features:]
        )


def whole(shape):
    return pl.BlockSpec(shape, lambda *_: (0,) * len(shape))


def one_tile(shape):
    return pl.BlockSpec((1,) + shape, lambda tile, *_: (tile,) + (0,) * len(shape))


def over_mp(values):
    peers = lax.axis_size("mp")
    by = 1
    total = values
    other = None
    while by < peers:
        if other is not None:
            total = total + other
        other = lax.ppermute(total, "mp", [(i, i ^ by) for i in range(peers)])
        by *= 2
    return total, other


def per_device_replicated(
    latent, reward_grad, curvature, offsets, counts, w_in, w_value, w_gate, w_down, w_out
):
    features, model_width = w_in.shape
    units = w_value.shape[1]
    half_side = S // 2
    token_count = half_side * half_side
    slab_rows, cols = latent.shape
    tiles_here = offsets.shape[0]
    slabs = lax.axis_size("tile")
    tiles = tiles_here * slabs
    rows = slab_rows * slabs
    digits = jnp.stack([offsets // 256, offsets % 256]).reshape(1, -1).astype(latent.dtype)
    digit_row = jnp.pad(digits, ((0, 0), (0, cols - digits.shape[1])))
    spare = -(slab_rows + 1) % 16
    packed = jnp.pad(jnp.concatenate([latent, digit_row], axis=0), ((0, spare), (0, 0)))

    def to_all(values):
        return lax.all_to_all(
            jnp.broadcast_to(values[None], (slabs,) + values.shape), "tile", 0, 0
        )

    latents = to_all(packed)
    rewards = to_all(jnp.concatenate([reward_grad, curvature], axis=0))
    digits = latents[:, slab_rows, : 4 * tiles_here].astype(jnp.int32)
    digits = digits.reshape(slabs, 2, tiles_here, 2)
    corners = (digits[:, 0] * 256 + digits[:, 1]).reshape(tiles, 2)

    wide = 2 * half_side * features // 2
    f32 = jnp.float32
    b16 = jnp.bfloat16

    def saved(kind, height):
        return jax.ShapeDtypeStruct((tiles, height, token_count), kind)

    kept = [
        saved(f32, units),
        saved(f32, units),
        saved(f32, units),
        saved(b16, model_width),
        saved(b16, units),
        saved(b16, model_width),
        saved(b16, features),
        saved(f32, 1),
    ]
    width = half_side * features // 2
    panels = cols // width
    canvas = jax.ShapeDtypeStruct((panels, rows, width), f32)
    params = pltpu.CompilerParams(
        dimension_semantics=("arbitrary",), vmem_limit_bytes=52 * 2**20
    )
    weights = [w_in, w_value, w_gate, w_down, w_out]
    sums, cover, *stored = pl.pallas_call(
        functools.partial(forward_kernel, half_side),
        out_shape=[canvas, canvas, *kept],
        grid_spec=pltpu.PrefetchScalarGridSpec(
            num_scalar_prefetch=1,
            grid=(tiles,),
            in_specs=[whole(latents.shape)] + [whole(w.shape) for w in weights],
            out_specs=[whole(canvas.shape)] * 2 + [one_tile(k.shape[1:]) for k in kept],
            scratch_shapes=[
                pltpu.VMEM(canvas.shape, f32),
                pltpu.VMEM((model_width, wide), b16),
                pltpu.VMEM((2 * units, model_width), b16),
                pltpu.VMEM((2 * features, units), b16),
            ],
        ),
        compiler_params=params,
        name="forward",
    )(corners, latents, *weights)
    total, other = over_mp(sums)
    scale_factor = 16.0 / math.sqrt(tiles * token_count)
    weights = [w_value, w_gate, w_down, w_out]
    blended, grad_value, grad_gate, grad_down, small = pl.pallas_call(
        functools.partial(backward_kernel, half_side, scale_factor),
        out_shape=[
            jax.ShapeDtypeStruct((rows, cols), f32),
            jax.ShapeDtypeStruct((model_width, units), f32),
            jax.ShapeDtypeStruct((model_width, units), f32),
            jax.ShapeDtypeStruct((units, model_width), f32),
            jax.ShapeDtypeStruct((2 * features, model_width), f32),
        ],
        grid_spec=pltpu.PrefetchScalarGridSpec(
            num_scalar_prefetch=1,
            grid=(tiles,),
            in_specs=[whole(canvas.shape)] * 2
            + [whole(rewards.shape), whole(canvas.shape)]
            + [whole(w.shape) for w in weights]
            + [one_tile(k.shape[1:]) for k in kept],
            out_specs=[
                whole((rows, cols)),
                whole((model_width, units)),
                whole((model_width, units)),
                whole((units, model_width)),
                whole((2 * features, model_width)),
            ],
            scratch_shapes=[
                pltpu.VMEM(canvas.shape, f32),
                pltpu.VMEM((model_width, wide), b16),
                pltpu.VMEM((2 * features, 2 * units), f32),
                pltpu.VMEM((2 * features, model_width), f32),
                pltpu.VMEM((features, units), f32),
                pltpu.VMEM((features, model_width), f32),
                pltpu.VMEM((features, features), f32),
            ],
        ),
        compiler_params=params,
        name="backward",
    )(corners, total, other, rewards, cover, *weights, *stored)
    own = lax.dynamic_slice_in_dim(blended, lax.axis_index("tile") * slab_rows, slab_rows, 0)
    mine, theirs = over_mp(small)
    small = mine + theirs
    return (own, small[:features], grad_value, grad_gate, grad_down, small[features:].T)


def per_device(
    latent, reward_grad, curvature, offsets, counts, w_in, w_value, w_gate, w_down, w_out
):
    tiles = offsets.shape[0] * lax.axis_size("tile")
    stored_bytes = tiles * (S // 2) ** 2 * (14 * w_value.shape[1] + 4 * w_in.shape[1])
    peers = lax.axis_size("mp")
    replicate = stored_bytes <= 48 * 2**20 and peers > 1 and peers & (peers - 1) == 0
    plan = per_device_replicated if replicate else per_device_sharded
    return plan(
        latent, reward_grad, curvature, offsets, counts, w_in, w_value, w_gate, w_down, w_out
    )


def solution(mesh):
    return jax.shard_map(
        per_device,
        mesh=mesh,
        in_specs=(
            P("tile", None),
            P("tile", None),
            P("tile", None),
            P("tile", None),
            P("tile", None),
            P(),
            P(None, "mp"),
            P(None, "mp"),
            P("mp", None),
            P(),
        ),
        out_specs=(P("tile", None), P(), P(None, "mp"), P(None, "mp"), P("mp", None), P()),
        check_vma=False,
    )
```

```python
import functools
import math

import jax
import jax.numpy as jnp
from jax import lax
from jax.experimental import pallas as pl
from jax.experimental.pallas import tpu as pltpu
from jax.sharding import PartitionSpec as P

S = 32
SPACING = 24


layer_eps = 1e-05
root_half = 0.7071067811865476
inv_root_two_pi = 0.3989422804014327
highest = lax.Precision.HIGHEST


def passed_along(shard, axis, by):
    peers = lax.axis_size(axis)
    pairs = [(i, i + by) for i in range(peers) if 0 <= i + by < peers]
    return lax.ppermute(shard, axis, pairs)


def gelu_value(inputs):
    return 0.5 * inputs * (1.0 + lax.erf(inputs * root_half))


def gelu_slope(inputs):
    return (
        0.5 * (1.0 + lax.erf(inputs * root_half))
        + inputs * jnp.exp(-0.5 * inputs * inputs) * inv_root_two_pi
    )


def patchify(cropped, channels):
    half_side = cropped.shape[0] // 2
    return (
        cropped.reshape(half_side, 2, half_side, 2 * channels)
        .transpose(0, 2, 1, 3)
        .reshape(half_side * half_side, 4 * channels)
    )


def unpatch(tokens, tile_side, channels):
    half_side = tile_side // 2
    token_rows = tokens.shape[0] // half_side
    return (
        tokens.reshape(token_rows, half_side, 2, 2 * channels)
        .transpose(0, 2, 1, 3)
        .reshape(2 * token_rows, tile_side * channels)
    )


def layer_norm(hidden):
    values = hidden.astype(jnp.float32)
    center = values - jnp.mean(values, axis=-1, keepdims=True)
    variance = jnp.mean(center * center, axis=-1, keepdims=True)
    inv_scale = lax.rsqrt(variance + layer_eps)
    return (center * inv_scale, inv_scale)


def norm_backward(normed, inv_scale, d_unit):
    centered = d_unit - jnp.mean(d_unit, axis=-1, keepdims=True)
    return inv_scale * (centered - normed * jnp.mean(d_unit * normed, axis=-1, keepdims=True))


def contract_rows(left, right):
    return lax.dot_general(
        left, right, (((0,), (0,)), ((), ())), preferred_element_type=jnp.float32
    )


def contract_rows_exact(left, right):
    return lax.dot_general(
        left, right, (((0,), (0,)), ((), ())), precision=highest, preferred_element_type=jnp.float32
    )


def contract_cols(left, right):
    return lax.dot_general(
        left, right, (((1,), (1,)), ((), ())), preferred_element_type=jnp.float32
    )


def crop_tiles(source, corners, row_base, tile_side, channels):

    def crop_one(corner):
        cropped = lax.dynamic_slice(
            source, (corner[0] - row_base, corner[1] * channels), (tile_side, tile_side * channels)
        )
        return patchify(cropped, channels)

    return jax.vmap(crop_one)(corners)


def place_tiles(canvas, pieces, corners, row_shift, channels):
    piece_rows = pieces.shape[1]
    piece_cols = pieces.shape[2]

    def add_tile(tile_index, current):
        corner = corners[tile_index]
        start_row = corner[0] + row_shift
        start_col = corner[1] * channels
        existing = lax.dynamic_slice(current, (start_row, start_col), (piece_rows, piece_cols))
        return lax.dynamic_update_slice(
            current, existing + pieces[tile_index], (start_row, start_col)
        )

    return lax.fori_loop(0, pieces.shape[0], add_tile, canvas)


def per_device_sharded(
    latent, reward_grad, curvature, offsets, counts, w_in, w_value, w_gate, w_down, w_out
):
    channels = w_in.shape[0] // 4
    model_width = w_in.shape[1]
    tile_side = S
    half_side = tile_side // 2
    token_count = half_side * half_side
    tiles_here = offsets.shape[0]
    slab_rows = latent.shape[0]
    canvas_cols = latent.shape[1]
    tile_devices = lax.axis_size("tile")
    model_devices = lax.axis_size("mp")
    tile_pos = lax.axis_index("tile")
    model_pos = lax.axis_index("mp")
    share_tokens = token_count // model_devices
    share_pixels = tile_side // model_devices
    scale_factor = 16.0 / math.sqrt(tiles_here * tile_devices * token_count)
    w_out_wide = w_out.astype(jnp.float32)
    cover_count = jnp.repeat(counts, channels, axis=1).astype(jnp.float32)
    placed_row = model_pos * share_pixels
    every_corner = lax.all_gather(offsets, "tile", axis=0, tiled=True)
    grid_cols = canvas_cols // (channels * SPACING)
    grid_cells = (every_corner[:, 0] + SPACING // 2) // SPACING * grid_cols + (
        every_corner[:, 1] + SPACING // 2
    ) // SPACING
    wanted = (
        tile_pos // 2 * grid_cols
        + tile_pos % 2 * tiles_here
        + jnp.arange(tiles_here, dtype=jnp.int32)
    )
    matched = (grid_cells[None, :] == wanted[:, None]).astype(jnp.int32)
    corners = jnp.sum(matched[:, :, None] * every_corner[None, :, :], axis=1)
    row_base = (tile_pos - 2) * slab_rows
    latent_parts = []
    for shift_by in (2, 1, 0, -1, -2):
        if shift_by == 0:
            latent_parts.append(latent)
        else:
            latent_parts.append(passed_along(latent, "tile", shift_by))
    latent_source = jnp.concatenate(latent_parts, axis=0)
    patches = crop_tiles(latent_source, corners, row_base, tile_side, channels)
    flat_patches = jnp.transpose(patches, (1, 0, 2)).reshape(token_count * tiles_here, 4 * channels)
    hidden = jnp.dot(flat_patches, w_in, preferred_element_type=jnp.float32).astype(jnp.bfloat16)
    normed, inv_scale = layer_norm(hidden)
    unit_in = normed.astype(jnp.bfloat16)
    value_proj = jnp.dot(unit_in, w_value, preferred_element_type=jnp.float32)
    gate_proj = jnp.dot(unit_in, w_gate, preferred_element_type=jnp.float32)
    active = (value_proj * gelu_value(gate_proj)).astype(jnp.bfloat16)
    active_grid = active.reshape(token_count, tiles_here, active.shape[1])

    def take_share(values):
        grid = values.reshape(token_count, tiles_here, values.shape[-1])
        picked = lax.dynamic_slice_in_dim(grid, model_pos * share_tokens, share_tokens, 0)
        return picked.reshape(share_tokens * tiles_here, values.shape[-1])

    hidden_share = take_share(hidden)
    row_block = active_grid.reshape(
        lax.axis_size("mp") * share_tokens * tiles_here, active_grid.shape[2]
    )
    ff_share = lax.psum_scatter(
        jnp.dot(row_block, w_down, preferred_element_type=jnp.float32).reshape(
            lax.axis_size("mp") * share_tokens, tiles_here, model_width
        ),
        "mp",
        scatter_dimension=0,
        tiled=True,
    ).reshape(share_tokens * tiles_here, model_width)
    noise_share = jnp.dot(hidden_share, w_out, preferred_element_type=jnp.float32) + jnp.dot(
        ff_share, w_out_wide, precision=highest, preferred_element_type=jnp.float32
    )
    noise_tiles = jnp.transpose(
        noise_share.reshape(share_tokens, tiles_here, w_out.shape[1]), (1, 0, 2)
    )

    def unpatch_share(tokens):
        return unpatch(tokens, tile_side, channels)

    noise_pieces = jax.vmap(unpatch_share)(noise_tiles)
    window_term = place_tiles(
        jnp.zeros((5 * slab_rows, canvas_cols), jnp.float32),
        noise_pieces,
        corners,
        placed_row - row_base,
        channels,
    )
    slab_sum = window_term[2 * slab_rows : 3 * slab_rows]
    for shift_by in (-2, -1, 1, 2):
        outgoing = window_term[(shift_by + 2) * slab_rows : (shift_by + 3) * slab_rows]
        slab_sum = slab_sum + passed_along(outgoing, "tile", shift_by)
    blend_total = lax.psum(slab_sum, "mp")
    blended = blend_total / cover_count
    cotangent = ((reward_grad - curvature * blended) / cover_count * scale_factor).astype(
        jnp.bfloat16
    )
    cot_parts = []
    for shift_by in (2, 1, 0, -1, -2):
        if shift_by == 0:
            cot_parts.append(cotangent)
        else:
            cot_parts.append(passed_along(cotangent, "tile", shift_by))
    cot_source = jnp.concatenate(cot_parts, axis=0)
    cot_patches = crop_tiles(cot_source, corners, row_base, tile_side, channels)
    cot_flat = jnp.transpose(cot_patches, (1, 0, 2)).reshape(token_count * tiles_here, 4 * channels)
    cot_share = take_share(cot_flat)
    d_feat = contract_cols(cot_flat, w_out)
    d_feat_b = d_feat.astype(jnp.bfloat16)
    d_active = contract_cols(d_feat_b, w_down)
    down_term = contract_rows(active, d_feat_b)
    d_value = (d_active * gelu_value(gate_proj)).astype(jnp.bfloat16)
    d_gate = (d_active * value_proj * gelu_slope(gate_proj)).astype(jnp.bfloat16)
    value_term = contract_rows(unit_in, d_value)
    gate_term = contract_rows(unit_in, d_gate)
    d_value_grid = d_value.reshape(token_count, tiles_here, d_value.shape[1])
    d_gate_grid = d_gate.reshape(token_count, tiles_here, d_gate.shape[1])
    value_block = d_value_grid.reshape(
        share_tokens * lax.axis_size("mp") * tiles_here, d_value.shape[1]
    )
    gate_block = d_gate_grid.reshape(
        share_tokens * lax.axis_size("mp") * tiles_here, d_gate.shape[1]
    )
    summed = contract_cols(value_block, w_value) + contract_cols(gate_block, w_gate)
    d_unit_share = (
        lax.psum_scatter(
            summed.reshape(share_tokens * lax.axis_size("mp"), tiles_here, model_width).astype(
                jnp.bfloat16
            ),
            "mp",
            scatter_dimension=0,
            tiled=True,
        )
        .astype(jnp.float32)
        .reshape(share_tokens * tiles_here, model_width)
    )
    d_hidden = (
        take_share(d_feat) + norm_backward(take_share(normed), take_share(inv_scale), d_unit_share)
    ).astype(jnp.bfloat16)
    in_term = contract_rows(take_share(flat_patches), d_hidden)
    out_term = contract_rows(hidden_share, cot_share) + contract_rows_exact(
        ff_share, cot_share.astype(jnp.float32)
    )
    grad_in, grad_out = lax.psum((in_term, out_term), ("tile", "mp"))
    grad_value, grad_gate, grad_down = lax.psum((value_term, gate_term, down_term), "tile")
    return (blended, grad_in, grad_value, grad_gate, grad_down, grad_out)


def dot_lanes(left, right):
    return lax.dot_general(
        left, right, (((1,), (1,)), ((), ())), preferred_element_type=jnp.float32
    )


def dot_plain(left, right):
    return lax.dot_general(
        left, right, (((1,), (0,)), ((), ())), preferred_element_type=jnp.float32
    )


def split_two(values):
    high = values.astype(jnp.bfloat16)
    low = (values - high.astype(jnp.float32)).astype(jnp.bfloat16)
    return high, low


def split_three(values):
    high = values.astype(jnp.bfloat16)
    rest = values - high.astype(jnp.float32)
    middle = rest.astype(jnp.bfloat16)
    low = (rest - middle.astype(jnp.float32)).astype(jnp.bfloat16)
    return high, middle, low


def fold_matrix(features, half_side):
    run = features // 2
    wide = 2 * half_side * run
    feature = lax.broadcasted_iota(jnp.int32, (features, wide), 0)
    place = lax.broadcasted_iota(jnp.int32, (features, wide), 1)
    own = place // (half_side * run) * run + place % run
    return jnp.where(feature == own, 1.0, 0.0).astype(jnp.bfloat16)


def column_mask(features, half_side):
    run = features // 2
    wide = 2 * half_side * run
    token = lax.broadcasted_iota(jnp.int32, (half_side * half_side, wide), 0)
    place = lax.broadcasted_iota(jnp.int32, (half_side * half_side, wide), 1)
    return token % half_side == place // run % half_side


def spread_tile(canvas_ref, row, col, half_side, features):
    run = features // 2
    width = half_side * run
    panels = canvas_ref.shape[0]
    cols = panels * width
    lanes = col * run // 2
    halves = []
    for parity in range(2):
        at = pl.ds(row + parity, half_side, stride=2)
        rows = jnp.concatenate([canvas_ref[panel, at, :] for panel in range(panels)], axis=1)
        rolled = pltpu.roll(rows, lax.rem(cols - lanes, cols), 1)
        halves.append(rolled[:, :width])
    pair = jnp.concatenate(halves, axis=1).astype(jnp.bfloat16)
    token = lax.broadcasted_iota(jnp.int32, (half_side * half_side, half_side), 0)
    patch_row = lax.broadcasted_iota(jnp.int32, (half_side * half_side, half_side), 1)
    repeat = jnp.where(token // half_side == patch_row, 1.0, 0.0).astype(jnp.bfloat16)
    repeated = dot_plain(repeat, pair)
    return jnp.where(column_mask(features, half_side), repeated, 0.0).astype(jnp.bfloat16)


def token_at(tile, tokens):
    return pl.ds(pl.multiple_of(tile * tokens, tokens), tokens)


def forward_kernel(
    half_side,
    corner_ref,
    latent_ref,
    w_in_ref,
    w_value_ref,
    w_gate_ref,
    w_down_ref,
    w_out_ref,
    canvas_ref,
    cover_ref,
    value_ref,
    gate_ref,
    left_ref,
    patch_ref,
    hidden_ref,
    latent_wide,
    w_in_spread,
    w_both,
    w_noise,
    hidden_all,
    active,
    noise,
):
    step = pl.program_id(0)
    features, model_width = w_in_ref.shape
    units = w_value_ref.shape[1]
    slabs, slab_rows, cols = latent_ref.shape
    panels, rows, width = canvas_ref.shape
    own_rows = rows // slabs
    tokens = half_side * half_side
    tiles_here = active.shape[1] // tokens

    @pl.when(step == 0)
    def _prepare():
        for slab in range(slabs):
            own = latent_ref[slab].astype(jnp.float32)[:own_rows]
            for panel in range(panels):
                latent_wide[panel, slab * own_rows : (slab + 1) * own_rows, :] = own[
                    :, panel * width : (panel + 1) * width
                ]
        fold = fold_matrix(features, half_side)
        w_in_spread[...] = lax.dot_general(
            w_in_ref[...], fold, (((0,), (0,)), ((), ())), preferred_element_type=jnp.float32
        ).astype(jnp.bfloat16)
        w_both[:units, :] = w_value_ref[...].T
        w_both[units:, :] = w_gate_ref[...].T
        both = lax.dot_general(
            w_out_ref[...],
            w_down_ref[...],
            (((0,), (1,)), ((), ())),
            preferred_element_type=jnp.float32,
        )
        high, low = split_two(both)
        w_noise[:features, :] = high
        w_noise[features:, :] = low
        canvas_ref[...] = jnp.zeros_like(canvas_ref)
        cover_ref[...] = jnp.zeros_like(cover_ref)
        noise[...] = jnp.zeros_like(noise)

    def corners_of(group):
        return [
            (corner_ref[group * tiles_here + tile, 0], corner_ref[group * tiles_here + tile, 1])
            for tile in range(tiles_here)
        ]

    corners = corners_of(step)
    add_noise(canvas_ref, noise[...], corners_of(jnp.maximum(step - 1, 0)), half_side, features)
    fold = fold_matrix(features, half_side)
    for tile, (row, col) in enumerate(corners):
        here = slice(tile * tokens, (tile + 1) * tokens)
        spread = spread_tile(latent_wide, row, col, half_side, features)
        patch = dot_lanes(fold, spread)
        patch_ref[:, here] = patch.astype(jnp.bfloat16)
        hidden_all[:, here] = dot_lanes(w_in_spread[...], spread).astype(jnp.bfloat16)
        total = jnp.zeros((chunk_rows, tokens), jnp.float32)
        for at in range(0, model_width, chunk_rows):
            total = total + hidden_all[at : at + chunk_rows, here].astype(jnp.float32)
        mean = jnp.sum(total, axis=0, keepdims=True) * (1.0 / model_width)
        total = jnp.zeros((chunk_rows, tokens), jnp.float32)
        for at in range(0, model_width, chunk_rows):
            center = hidden_all[at : at + chunk_rows, here].astype(jnp.float32) - mean
            total = total + center * center
        variance = jnp.sum(total, axis=0, keepdims=True) * (1.0 / model_width)
        inv_scale = lax.rsqrt(variance + layer_eps)
        for at in range(0, model_width, chunk_rows):
            center = hidden_all[at : at + chunk_rows, here].astype(jnp.float32) - mean
            left_ref[at : at + chunk_rows, here] = (center * inv_scale).astype(jnp.bfloat16)
        high, low = split_two(patch * inv_scale)
        left_ref[model_width : model_width + features, here] = high
        left_ref[model_width + features :, here] = low
    for tile in range(tiles_here):
        here = slice(tile * tokens, (tile + 1) * tokens)
        unit = left_ref[:model_width, here]
        value_ref[:, here] = dot_plain(w_both[:units, :], unit)
        gate_ref[:, here] = dot_plain(w_both[units:, :], unit)
        for at in range(0, units, chunk_rows):
            value = value_ref[at : at + chunk_rows, here]
            gate = gate_ref[at : at + chunk_rows, here]
            normal = 0.5 * (1.0 + lax.erf(gate * root_half))
            active[at : at + chunk_rows, here] = (value * (gate * normal)).astype(jnp.bfloat16)
    parts = dot_plain(w_noise[...], active[...])
    noise[...] = parts[:features] + parts[features:]
    peers = lax.axis_size("mp")
    for group in range(tiles_here // peers):
        own = token_at(group * peers + lax.axis_index("mp"), tokens)
        hidden = hidden_all[:, own]
        hidden_ref[:, group * tokens : (group + 1) * tokens] = hidden
        noise[:, own] = noise[:, own] + lax.dot_general(
            w_out_ref[...], hidden, (((0,), (0,)), ((), ())), preferred_element_type=jnp.float32
        )

    @pl.when(step == pl.num_programs(0) - 1)
    def _last():
        add_noise(canvas_ref, noise[...], corners, half_side, features)

    shape = cover_ref.shape
    row_at = lax.broadcasted_iota(jnp.int32, shape, 1)
    col_at = lax.broadcasted_iota(jnp.int32, shape, 0) * width + lax.broadcasted_iota(
        jnp.int32, shape, 2
    )
    cover = cover_ref[...]
    for row, col in corners:
        left = col * (features // 4)
        inside = (
            (row_at >= row)
            & (row_at < row + 2 * half_side)
            & (col_at >= left)
            & (col_at < left + half_side * features // 2)
        )
        cover = cover + jnp.where(inside, 1.0, 0.0)
    cover_ref[...] = cover


def add_noise(canvas_ref, noise, corners, half_side, features):
    run = features // 2
    width = half_side * run
    panels = canvas_ref.shape[0]
    fold = fold_matrix(features, half_side)
    tall = lax.dot_general(
        jnp.concatenate(split_three(noise), axis=0),
        jnp.concatenate([fold, fold, fold], axis=0),
        (((0,), (0,)), ((), ())),
        preferred_element_type=jnp.float32,
    )
    tall = tall.reshape(len(corners), half_side * half_side, 2 * width)
    kept = jnp.where(column_mask(features, half_side)[None], tall, 0.0)
    pairs = jnp.sum(kept.reshape(len(corners), half_side, half_side, 2 * width), axis=2)
    blank = jnp.zeros((half_side, (panels - 1) * width), jnp.float32)
    for tile, (row, col) in enumerate(corners):
        for parity in range(2):
            own = pairs[tile, :, parity * width : (parity + 1) * width]
            placed = pltpu.roll(jnp.concatenate([own, blank], axis=1), col * run // 2, 1)
            at = pl.ds(row + parity, half_side, stride=2)
            for panel in range(panels):
                here = placed[:, panel * width : (panel + 1) * width]
                canvas_ref[panel, at, :] = canvas_ref[panel, at, :] + here


def backward_kernel(
    half_side,
    scale_factor,
    corner_ref,
    sum_ref,
    other_ref,
    reward_ref,
    cover_ref,
    w_value_ref,
    w_gate_ref,
    w_down_ref,
    w_out_ref,
    value_ref,
    gate_ref,
    left_ref,
    patch_ref,
    hidden_ref,
    blended_ref,
    grad_value_ref,
    grad_gate_ref,
    grad_down_ref,
    small_ref,
    cot_wide,
    w_through,
    scaled_sum,
    mean_sum,
    active_sum,
    hidden_sum,
    patch_sum,
    cot,
    d_active,
    d_both,
    active,
    along_scaled,
):
    step = pl.program_id(0)
    model_width, features = w_out_ref.shape
    units = w_down_ref.shape[0]
    slabs, two_slabs, cols = reward_ref.shape
    slab_rows = two_slabs // 2
    panels, rows, width = sum_ref.shape
    tokens = half_side * half_side
    tiles_here = active.shape[1] // tokens

    @pl.when(step == 0)
    def _prepare():
        for panel in range(panels):
            lanes = slice(panel * width, (panel + 1) * width)
            cover = cover_ref[panel]
            blended = (sum_ref[panel] + other_ref[panel]) / cover
            blended_ref[:, lanes] = blended
            reward = jnp.concatenate(
                [reward_ref[slab, :slab_rows, lanes] for slab in range(slabs)], axis=0
            )
            curvature = jnp.concatenate(
                [reward_ref[slab, slab_rows:, lanes] for slab in range(slabs)], axis=0
            )
            cot_wide[panel] = (
                ((reward - curvature * blended) / cover * scale_factor)
                .astype(jnp.bfloat16)
                .astype(jnp.float32)
            )
        w_through[...] = jnp.concatenate(
            split_two(dot_plain(w_down_ref[...], w_out_ref[...])), axis=1
        )
        for ref in (
            grad_value_ref,
            grad_gate_ref,
            scaled_sum,
            mean_sum,
            active_sum,
            hidden_sum,
            patch_sum,
        ):
            ref[...] = jnp.zeros_like(ref)

    for tile in range(tiles_here):
        here = slice(tile * tokens, (tile + 1) * tokens)
        spread = spread_tile(
            cot_wide,
            corner_ref[step * tiles_here + tile, 0],
            corner_ref[step * tiles_here + tile, 1],
            half_side,
            features,
        )
        cots = dot_lanes(fold_matrix(features, half_side), spread).astype(jnp.bfloat16)
        cot[:, here] = cots
        d_active[:, here] = dot_plain(w_through[...], jnp.concatenate([cots, cots], axis=0))
    for tile in range(tiles_here):
        here = slice(tile * tokens, (tile + 1) * tokens)
        total = jnp.zeros((chunk_rows, tokens), jnp.float32)
        for at in range(0, units, chunk_rows):
            chunk = slice(at, at + chunk_rows)
            value = value_ref[chunk, here]
            gate = gate_ref[chunk, here]
            passed = d_active[chunk, here]
            normal = 0.5 * (1.0 + lax.erf(gate * root_half))
            slope = normal + gate * jnp.exp(-0.5 * gate * gate) * inv_root_two_pi
            active[chunk, here] = (value * (gate * normal)).astype(jnp.bfloat16)
            d_value = (passed * (gate * normal)).astype(jnp.bfloat16)
            d_gate = (passed * value * slope).astype(jnp.bfloat16)
            d_both[chunk, here] = d_value
            d_both[units + at : units + at + chunk_rows, here] = d_gate
            total = total + d_value.astype(jnp.float32) * value
            total = total + d_gate.astype(jnp.float32) * gate
        along = jnp.sum(total, axis=0, keepdims=True) * (1.0 / model_width)
        scaled = left_ref[model_width:, here].astype(jnp.float32)
        high, low = split_two((scaled[:features] + scaled[features:]) * along)
        along_scaled[:features, here] = high
        along_scaled[features:, here] = low
    grads = dot_lanes(left_ref[...], d_both[...])
    grad_value_ref[...] += grads[:model_width, :units]
    grad_gate_ref[...] += grads[:model_width, units:]
    scaled_sum[...] += grads[model_width:]
    mean_sum[...] += dot_lanes(left_ref[:model_width, :], along_scaled[...])
    active_sum[...] += dot_lanes(active[...], cot[...])
    peers = lax.axis_size("mp")
    for group in range(tiles_here // peers):
        own = token_at(group * peers + lax.axis_index("mp"), tokens)
        own_cot = cot[:, own]
        hidden_sum[...] += dot_lanes(
            own_cot, hidden_ref[:, group * tokens : (group + 1) * tokens]
        )
        patch_sum[...] += dot_lanes(patch_ref[:, own], own_cot)

    @pl.when(step == pl.num_programs(0) - 1)
    def _finish():
        active_two = jnp.concatenate(split_two(active_sum[...].T), axis=0)
        mean_both = mean_sum[...].T
        w_out_two = jnp.concatenate([w_out_ref[...], w_out_ref[...]], axis=1)
        grad_down_ref[...] = lax.dot_general(
            active_two, w_out_two, (((0,), (1,)), ((), ())), preferred_element_type=jnp.float32
        )
        through = dot_plain(active_two, w_down_ref[...])
        small_ref[features:] = hidden_sum[...] + through[:features] + through[features:]
        scaled_both = scaled_sum[:features] + scaled_sum[features:]
        scaled_two = jnp.concatenate(split_two(scaled_both), axis=0)
        moved = dot_lanes(scaled_two[:, :units], w_value_ref[...]) + dot_lanes(
            scaled_two[:, units:], w_gate_ref[...]
        )
        moved = moved[:features] + moved[features:]
        patch_two = jnp.concatenate(split_two(patch_sum[...]), axis=0)
        direct = dot_lanes(patch_two, w_out_ref[...])
        small_ref[:features] = (
            direct[:features]
            + direct[features:]
            + moved
            - jnp.mean(moved, axis=1, keepdims=True)
            - mean_both[:features]
            - mean_both[features:]
        )


def whole(shape):
    return pl.BlockSpec(shape, lambda *_: (0,) * len(shape))


def over_mp(values):
    peers = lax.axis_size("mp")
    by = 1
    total = values
    other = None
    while by < peers:
        if other is not None:
            total = total + other
        other = lax.ppermute(total, "mp", [(i, i ^ by) for i in range(peers)])
        by *= 2
    return total, other


chunk_rows = 32


def some_tokens(height, tokens):
    return pl.BlockSpec((height, tokens), lambda step, *_: (0, step))


def step_tiles(tiles):
    peers = lax.axis_size("mp")
    return max(peers * count for count in (1,) if tiles % (peers * count) == 0)


def saved_arrays(tiles, token_count, features, model_width, units):
    every = tiles * token_count
    shapes = [
        ((units, every), jnp.float32),
        ((units, every), jnp.float32),
        ((model_width + 2 * features, every), jnp.bfloat16),
        ((features, every), jnp.bfloat16),
        ((model_width, every // lax.axis_size("mp")), jnp.bfloat16),
    ]
    return [jax.ShapeDtypeStruct(shape, kind) for shape, kind in shapes]


kernel_params = pltpu.CompilerParams(
    dimension_semantics=("arbitrary",), vmem_limit_bytes=52 * 2**20
)


def run_forward(corners, latents, weights, half_side, rows):
    features, model_width = weights[0].shape
    units = weights[1].shape[1]
    tiles = corners.shape[0]
    cols = latents.shape[2]
    steps = tiles // step_tiles(tiles)
    tokens = step_tiles(tiles) * half_side * half_side
    width = half_side * features // 2
    f32 = jnp.float32
    b16 = jnp.bfloat16
    canvas = jax.ShapeDtypeStruct((cols // width, rows, width), f32)
    kept = saved_arrays(tiles, half_side * half_side, features, model_width, units)
    return pl.pallas_call(
        functools.partial(forward_kernel, half_side),
        out_shape=[canvas, canvas, *kept],
        grid_spec=pltpu.PrefetchScalarGridSpec(
            num_scalar_prefetch=1,
            grid=(steps,),
            in_specs=[whole(latents.shape)] + [whole(w.shape) for w in weights],
            out_specs=[whole(canvas.shape)] * 2 + [some_tokens(k.shape[0], k.shape[1] // steps) for k in kept],
            scratch_shapes=[
                pltpu.VMEM(canvas.shape, f32),
                pltpu.VMEM((model_width, 2 * width), b16),
                pltpu.VMEM((2 * units, model_width), b16),
                pltpu.VMEM((2 * features, units), b16),
                pltpu.VMEM((model_width, tokens), b16),
                pltpu.VMEM((units, tokens), b16),
                pltpu.VMEM((features, tokens), f32),
            ],
        ),
        compiler_params=kernel_params,
        name="forward",
    )(corners, latents, *weights)


def run_backward(corners, total, other, rewards, cover, weights, stored, half_side):
    features, model_width = weights[0].shape
    units = weights[1].shape[1]
    tiles = corners.shape[0]
    token_count = half_side * half_side
    steps = tiles // step_tiles(tiles)
    tokens = step_tiles(tiles) * token_count
    panels, rows, width = total.shape
    f32 = jnp.float32
    scale_factor = 16.0 / math.sqrt(tiles * token_count)
    return pl.pallas_call(
        functools.partial(backward_kernel, half_side, scale_factor),
        out_shape=[
            jax.ShapeDtypeStruct((rows, panels * width), f32),
            jax.ShapeDtypeStruct((model_width, units), f32),
            jax.ShapeDtypeStruct((model_width, units), f32),
            jax.ShapeDtypeStruct((units, model_width), f32),
            jax.ShapeDtypeStruct((2 * features, model_width), f32),
        ],
        grid_spec=pltpu.PrefetchScalarGridSpec(
            num_scalar_prefetch=1,
            grid=(steps,),
            in_specs=[whole(total.shape)] * 2
            + [whole(rewards.shape), whole(cover.shape)]
            + [whole(w.shape) for w in weights[1:]]
            + [some_tokens(k.shape[0], k.shape[1] // steps) for k in stored],
            out_specs=[
                whole((rows, panels * width)),
                whole((model_width, units)),
                whole((model_width, units)),
                whole((units, model_width)),
                whole((2 * features, model_width)),
            ],
            scratch_shapes=[
                pltpu.VMEM(total.shape, f32),
                pltpu.VMEM((units, 2 * features), jnp.bfloat16),
                pltpu.VMEM((2 * features, 2 * units), f32),
                pltpu.VMEM((model_width, 2 * features), f32),
                pltpu.VMEM((units, features), f32),
                pltpu.VMEM((features, model_width), f32),
                pltpu.VMEM((features, features), f32),
                pltpu.VMEM((features, tokens), jnp.bfloat16),
                pltpu.VMEM((units, tokens), f32),
                pltpu.VMEM((2 * units, tokens), jnp.bfloat16),
                pltpu.VMEM((units, tokens), jnp.bfloat16),
                pltpu.VMEM((2 * features, tokens), jnp.bfloat16),
            ],
        ),
        compiler_params=kernel_params,
        name="backward",
    )(corners, total, other, rewards, cover, *weights[1:], *stored)


def per_device_replicated(
    latent, reward_grad, curvature, offsets, counts, w_in, w_value, w_gate, w_down, w_out
):
    features, model_width = w_in.shape
    units = w_value.shape[1]
    half_side = S // 2
    token_count = half_side * half_side
    slab_rows, cols = latent.shape
    tiles_here = offsets.shape[0]
    slabs = lax.axis_size("tile")
    tiles = tiles_here * slabs
    rows = slab_rows * slabs
    digits = jnp.stack([offsets // 256, offsets % 256]).reshape(1, -1).astype(latent.dtype)
    digit_row = jnp.pad(digits, ((0, 0), (0, cols - digits.shape[1])))
    spare = -(slab_rows + 1) % 16
    packed = jnp.pad(jnp.concatenate([latent, digit_row], axis=0), ((0, spare), (0, 0)))

    def to_all(values):
        return lax.all_to_all(
            jnp.broadcast_to(values[None], (slabs,) + values.shape), "tile", 0, 0
        )

    latents = to_all(packed)
    rewards = to_all(jnp.concatenate([reward_grad, curvature], axis=0))
    digits = latents[:, slab_rows, : 4 * tiles_here].astype(jnp.int32)
    digits = digits.reshape(slabs, 2, tiles_here, 2)
    corners = (digits[:, 0] * 256 + digits[:, 1]).reshape(tiles, 2)

    weights = (w_in, w_value, w_gate, w_down, w_out)
    sums, cover, *stored = run_forward(corners, latents, weights, half_side, rows)
    total, other = over_mp(sums)
    blended, grad_value, grad_gate, grad_down, small = run_backward(
        corners, total, other, rewards, cover, weights, stored, half_side
    )
    own = lax.dynamic_slice_in_dim(blended, lax.axis_index("tile") * slab_rows, slab_rows, 0)
    mine, theirs = over_mp(small)
    small = mine + theirs
    return (own, small[:features], grad_value, grad_gate, grad_down, small[features:].T)


def per_device(
    latent, reward_grad, curvature, offsets, counts, w_in, w_value, w_gate, w_down, w_out
):
    tiles = offsets.shape[0] * lax.axis_size("tile")
    stored_bytes = tiles * (S // 2) ** 2 * (8 * w_value.shape[1] + 3 * w_in.shape[1])
    peers = lax.axis_size("mp")
    pairs = peers > 1 and peers & (peers - 1) == 0 and tiles % peers == 0
    replicate = pairs and stored_bytes <= 40 * 2**20
    plan = per_device_replicated if replicate else per_device_sharded
    return plan(
        latent, reward_grad, curvature, offsets, counts, w_in, w_value, w_gate, w_down, w_out
    )


def solution(mesh):
    return jax.shard_map(
        per_device,
        mesh=mesh,
        in_specs=(
            P("tile", None),
            P("tile", None),
            P("tile", None),
            P("tile", None),
            P("tile", None),
            P(),
            P(None, "mp"),
            P(None, "mp"),
            P("mp", None),
            P(),
        ),
        out_specs=(P("tile", None), P(), P(None, "mp"), P(None, "mp"), P("mp", None), P()),
        check_vma=False,
    )
```

```python
import functools
import math

import jax
import jax.numpy as jnp
from jax import lax
from jax.experimental import pallas as pl
from jax.experimental.pallas import tpu as pltpu
from jax.sharding import PartitionSpec as P

S = 32
SPACING = 24


layer_eps = 1e-05
root_half = 0.7071067811865476
inv_root_two_pi = 0.3989422804014327
highest = lax.Precision.HIGHEST


def passed_along(shard, axis, by):
    peers = lax.axis_size(axis)
    pairs = [(i, i + by) for i in range(peers) if 0 <= i + by < peers]
    return lax.ppermute(shard, axis, pairs)


def gelu_value(inputs):
    return 0.5 * inputs * (1.0 + lax.erf(inputs * root_half))


def gelu_slope(inputs):
    return (
        0.5 * (1.0 + lax.erf(inputs * root_half))
        + inputs * jnp.exp(-0.5 * inputs * inputs) * inv_root_two_pi
    )


def patchify(cropped, channels):
    half_side = cropped.shape[0] // 2
    return (
        cropped.reshape(half_side, 2, half_side, 2 * channels)
        .transpose(0, 2, 1, 3)
        .reshape(half_side * half_side, 4 * channels)
    )


def unpatch(tokens, tile_side, channels):
    half_side = tile_side // 2
    token_rows = tokens.shape[0] // half_side
    return (
        tokens.reshape(token_rows, half_side, 2, 2 * channels)
        .transpose(0, 2, 1, 3)
        .reshape(2 * token_rows, tile_side * channels)
    )


def layer_norm(hidden):
    values = hidden.astype(jnp.float32)
    center = values - jnp.mean(values, axis=-1, keepdims=True)
    variance = jnp.mean(center * center, axis=-1, keepdims=True)
    inv_scale = lax.rsqrt(variance + layer_eps)
    return (center * inv_scale, inv_scale)


def norm_backward(normed, inv_scale, d_unit):
    centered = d_unit - jnp.mean(d_unit, axis=-1, keepdims=True)
    return inv_scale * (centered - normed * jnp.mean(d_unit * normed, axis=-1, keepdims=True))


def contract_rows(left, right):
    return lax.dot_general(
        left, right, (((0,), (0,)), ((), ())), preferred_element_type=jnp.float32
    )


def contract_rows_exact(left, right):
    return lax.dot_general(
        left, right, (((0,), (0,)), ((), ())), precision=highest, preferred_element_type=jnp.float32
    )


def contract_cols(left, right):
    return lax.dot_general(
        left, right, (((1,), (1,)), ((), ())), preferred_element_type=jnp.float32
    )


def crop_tiles(source, corners, row_base, tile_side, channels):

    def crop_one(corner):
        cropped = lax.dynamic_slice(
            source, (corner[0] - row_base, corner[1] * channels), (tile_side, tile_side * channels)
        )
        return patchify(cropped, channels)

    return jax.vmap(crop_one)(corners)


def place_tiles(canvas, pieces, corners, row_shift, channels):
    piece_rows = pieces.shape[1]
    piece_cols = pieces.shape[2]

    def add_tile(tile_index, current):
        corner = corners[tile_index]
        start_row = corner[0] + row_shift
        start_col = corner[1] * channels
        existing = lax.dynamic_slice(current, (start_row, start_col), (piece_rows, piece_cols))
        return lax.dynamic_update_slice(
            current, existing + pieces[tile_index], (start_row, start_col)
        )

    return lax.fori_loop(0, pieces.shape[0], add_tile, canvas)


def per_device_sharded(
    latent, reward_grad, curvature, offsets, counts, w_in, w_value, w_gate, w_down, w_out
):
    channels = w_in.shape[0] // 4
    model_width = w_in.shape[1]
    tile_side = S
    half_side = tile_side // 2
    token_count = half_side * half_side
    tiles_here = offsets.shape[0]
    slab_rows = latent.shape[0]
    canvas_cols = latent.shape[1]
    tile_devices = lax.axis_size("tile")
    model_devices = lax.axis_size("mp")
    tile_pos = lax.axis_index("tile")
    model_pos = lax.axis_index("mp")
    share_tokens = token_count // model_devices
    share_pixels = tile_side // model_devices
    scale_factor = 16.0 / math.sqrt(tiles_here * tile_devices * token_count)
    w_out_wide = w_out.astype(jnp.float32)
    cover_count = jnp.repeat(counts, channels, axis=1).astype(jnp.float32)
    placed_row = model_pos * share_pixels
    every_corner = lax.all_gather(offsets, "tile", axis=0, tiled=True)
    grid_cols = canvas_cols // (channels * SPACING)
    grid_cells = (every_corner[:, 0] + SPACING // 2) // SPACING * grid_cols + (
        every_corner[:, 1] + SPACING // 2
    ) // SPACING
    wanted = (
        tile_pos // 2 * grid_cols
        + tile_pos % 2 * tiles_here
        + jnp.arange(tiles_here, dtype=jnp.int32)
    )
    matched = (grid_cells[None, :] == wanted[:, None]).astype(jnp.int32)
    corners = jnp.sum(matched[:, :, None] * every_corner[None, :, :], axis=1)
    row_base = (tile_pos - 2) * slab_rows
    latent_parts = []
    for shift_by in (2, 1, 0, -1, -2):
        if shift_by == 0:
            latent_parts.append(latent)
        else:
            latent_parts.append(passed_along(latent, "tile", shift_by))
    latent_source = jnp.concatenate(latent_parts, axis=0)
    patches = crop_tiles(latent_source, corners, row_base, tile_side, channels)
    flat_patches = jnp.transpose(patches, (1, 0, 2)).reshape(token_count * tiles_here, 4 * channels)
    hidden = jnp.dot(flat_patches, w_in, preferred_element_type=jnp.float32).astype(jnp.bfloat16)
    normed, inv_scale = layer_norm(hidden)
    unit_in = normed.astype(jnp.bfloat16)
    value_proj = jnp.dot(unit_in, w_value, preferred_element_type=jnp.float32)
    gate_proj = jnp.dot(unit_in, w_gate, preferred_element_type=jnp.float32)
    active = (value_proj * gelu_value(gate_proj)).astype(jnp.bfloat16)
    active_grid = active.reshape(token_count, tiles_here, active.shape[1])

    def take_share(values):
        grid = values.reshape(token_count, tiles_here, values.shape[-1])
        picked = lax.dynamic_slice_in_dim(grid, model_pos * share_tokens, share_tokens, 0)
        return picked.reshape(share_tokens * tiles_here, values.shape[-1])

    hidden_share = take_share(hidden)
    row_block = active_grid.reshape(
        lax.axis_size("mp") * share_tokens * tiles_here, active_grid.shape[2]
    )
    ff_share = lax.psum_scatter(
        jnp.dot(row_block, w_down, preferred_element_type=jnp.float32).reshape(
            lax.axis_size("mp") * share_tokens, tiles_here, model_width
        ),
        "mp",
        scatter_dimension=0,
        tiled=True,
    ).reshape(share_tokens * tiles_here, model_width)
    noise_share = jnp.dot(hidden_share, w_out, preferred_element_type=jnp.float32) + jnp.dot(
        ff_share, w_out_wide, precision=highest, preferred_element_type=jnp.float32
    )
    noise_tiles = jnp.transpose(
        noise_share.reshape(share_tokens, tiles_here, w_out.shape[1]), (1, 0, 2)
    )

    def unpatch_share(tokens):
        return unpatch(tokens, tile_side, channels)

    noise_pieces = jax.vmap(unpatch_share)(noise_tiles)
    window_term = place_tiles(
        jnp.zeros((5 * slab_rows, canvas_cols), jnp.float32),
        noise_pieces,
        corners,
        placed_row - row_base,
        channels,
    )
    slab_sum = window_term[2 * slab_rows : 3 * slab_rows]
    for shift_by in (-2, -1, 1, 2):
        outgoing = window_term[(shift_by + 2) * slab_rows : (shift_by + 3) * slab_rows]
        slab_sum = slab_sum + passed_along(outgoing, "tile", shift_by)
    blend_total = lax.psum(slab_sum, "mp")
    blended = blend_total / cover_count
    cotangent = ((reward_grad - curvature * blended) / cover_count * scale_factor).astype(
        jnp.bfloat16
    )
    cot_parts = []
    for shift_by in (2, 1, 0, -1, -2):
        if shift_by == 0:
            cot_parts.append(cotangent)
        else:
            cot_parts.append(passed_along(cotangent, "tile", shift_by))
    cot_source = jnp.concatenate(cot_parts, axis=0)
    cot_patches = crop_tiles(cot_source, corners, row_base, tile_side, channels)
    cot_flat = jnp.transpose(cot_patches, (1, 0, 2)).reshape(token_count * tiles_here, 4 * channels)
    cot_share = take_share(cot_flat)
    d_feat = contract_cols(cot_flat, w_out)
    d_feat_b = d_feat.astype(jnp.bfloat16)
    d_active = contract_cols(d_feat_b, w_down)
    down_term = contract_rows(active, d_feat_b)
    d_value = (d_active * gelu_value(gate_proj)).astype(jnp.bfloat16)
    d_gate = (d_active * value_proj * gelu_slope(gate_proj)).astype(jnp.bfloat16)
    value_term = contract_rows(unit_in, d_value)
    gate_term = contract_rows(unit_in, d_gate)
    d_value_grid = d_value.reshape(token_count, tiles_here, d_value.shape[1])
    d_gate_grid = d_gate.reshape(token_count, tiles_here, d_gate.shape[1])
    value_block = d_value_grid.reshape(
        share_tokens * lax.axis_size("mp") * tiles_here, d_value.shape[1]
    )
    gate_block = d_gate_grid.reshape(
        share_tokens * lax.axis_size("mp") * tiles_here, d_gate.shape[1]
    )
    summed = contract_cols(value_block, w_value) + contract_cols(gate_block, w_gate)
    d_unit_share = (
        lax.psum_scatter(
            summed.reshape(share_tokens * lax.axis_size("mp"), tiles_here, model_width).astype(
                jnp.bfloat16
            ),
            "mp",
            scatter_dimension=0,
            tiled=True,
        )
        .astype(jnp.float32)
        .reshape(share_tokens * tiles_here, model_width)
    )
    d_hidden = (
        take_share(d_feat) + norm_backward(take_share(normed), take_share(inv_scale), d_unit_share)
    ).astype(jnp.bfloat16)
    in_term = contract_rows(take_share(flat_patches), d_hidden)
    out_term = contract_rows(hidden_share, cot_share) + contract_rows_exact(
        ff_share, cot_share.astype(jnp.float32)
    )
    grad_in, grad_out = lax.psum((in_term, out_term), ("tile", "mp"))
    grad_value, grad_gate, grad_down = lax.psum((value_term, gate_term, down_term), "tile")
    return (blended, grad_in, grad_value, grad_gate, grad_down, grad_out)


def dot_lanes(left, right):
    return lax.dot_general(
        left, right, (((1,), (1,)), ((), ())), preferred_element_type=jnp.float32
    )


def dot_plain(left, right):
    return lax.dot_general(
        left, right, (((1,), (0,)), ((), ())), preferred_element_type=jnp.float32
    )


def split_two(values):
    high = values.astype(jnp.bfloat16)
    low = (values - high.astype(jnp.float32)).astype(jnp.bfloat16)
    return high, low


def split_three(values):
    high = values.astype(jnp.bfloat16)
    rest = values - high.astype(jnp.float32)
    middle = rest.astype(jnp.bfloat16)
    low = (rest - middle.astype(jnp.float32)).astype(jnp.bfloat16)
    return high, middle, low


def fold_matrix(features, half_side):
    run = features // 2
    wide = 2 * half_side * run
    feature = lax.broadcasted_iota(jnp.int32, (features, wide), 0)
    place = lax.broadcasted_iota(jnp.int32, (features, wide), 1)
    own = place // (half_side * run) * run + place % run
    return jnp.where(feature == own, 1.0, 0.0).astype(jnp.bfloat16)


def column_mask(features, half_side):
    run = features // 2
    wide = 2 * half_side * run
    token = lax.broadcasted_iota(jnp.int32, (half_side * half_side, wide), 0)
    place = lax.broadcasted_iota(jnp.int32, (half_side * half_side, wide), 1)
    return token % half_side == place // run % half_side


def spread_tile(canvas_ref, row, col, half_side, features):
    run = features // 2
    width = half_side * run
    panels = canvas_ref.shape[0]
    cols = panels * width
    lanes = col * run // 2
    halves = []
    for parity in range(2):
        at = pl.ds(row + parity, half_side, stride=2)
        rows = jnp.concatenate([canvas_ref[panel, at, :] for panel in range(panels)], axis=1)
        rolled = pltpu.roll(rows, lax.rem(cols - lanes, cols), 1)
        halves.append(rolled[:, :width])
    pair = jnp.concatenate(halves, axis=1).astype(jnp.bfloat16)
    token = lax.broadcasted_iota(jnp.int32, (half_side * half_side, half_side), 0)
    patch_row = lax.broadcasted_iota(jnp.int32, (half_side * half_side, half_side), 1)
    repeat = jnp.where(token // half_side == patch_row, 1.0, 0.0).astype(jnp.bfloat16)
    repeated = dot_plain(repeat, pair)
    return jnp.where(column_mask(features, half_side), repeated, 0.0).astype(jnp.bfloat16)


def token_at(tile, tokens):
    return pl.ds(pl.multiple_of(tile * tokens, tokens), tokens)


def weight_kernel(
    half_side,
    w_in_ref,
    w_value_ref,
    w_gate_ref,
    w_down_ref,
    w_out_ref,
    packed,
    w_through,
):
    features, model_width = w_in_ref.shape
    units = w_value_ref.shape[1]
    fold = fold_matrix(features, half_side)
    packed[...] = jnp.zeros_like(packed)
    packed[:model_width, model_width:] = lax.dot_general(
        w_in_ref[...], fold, (((0,), (0,)), ((), ())), preferred_element_type=jnp.float32
    ).astype(jnp.bfloat16)
    packed[:units, :model_width] = w_value_ref[...].T
    packed[units : 2 * units, :model_width] = w_gate_ref[...].T
    both = dot_plain(w_down_ref[...], w_out_ref[...])
    w_through[...] = jnp.concatenate(split_two(both), axis=1)
    packed[2 * units :, :units] = jnp.concatenate(split_two(both.T), axis=0)


def run_weights(weights, half_side):
    features, model_width = weights[0].shape
    units = weights[1].shape[1]
    width = half_side * features // 2
    vmem = pl.BlockSpec(memory_space=pltpu.VMEM)
    shapes = [
        (2 * units + 2 * features, max(model_width + 2 * width, units)),
        (units, 2 * features),
    ]
    return pl.pallas_call(
        functools.partial(weight_kernel, half_side),
        out_shape=[jax.ShapeDtypeStruct(shape, jnp.bfloat16) for shape in shapes],
        in_specs=[vmem] * len(weights),
        out_specs=[vmem] * len(shapes),
        name="weights",
    )(*weights)


def forward_kernel(
    half_side,
    corner_ref,
    latent_ref,
    weights_ref,
    w_out_ref,
    canvas_ref,
    cover_ref,
    value_ref,
    gate_ref,
    left_ref,
    patch_ref,
    hidden_ref,
    latent_wide,
    spread,
    hidden_all,
    active,
    noise,
):
    step = pl.program_id(0)
    model_width, features = w_out_ref.shape
    units = weights_ref.shape[0] // 2 - features
    slabs, slab_rows, cols = latent_ref.shape
    panels, rows, width = canvas_ref.shape
    own_rows = rows // slabs
    tokens = half_side * half_side
    tiles_here = active.shape[1] // tokens

    @pl.when(step == 0)
    def _prepare():
        for slab in range(slabs):
            own = latent_ref[slab].astype(jnp.float32)[:own_rows]
            for panel in range(panels):
                latent_wide[panel, slab * own_rows : (slab + 1) * own_rows, :] = own[
                    :, panel * width : (panel + 1) * width
                ]
        canvas_ref[...] = jnp.zeros_like(canvas_ref)
        cover_ref[...] = jnp.zeros_like(cover_ref)
        noise[...] = jnp.zeros_like(noise)

    def corners_of(group):
        return [
            (corner_ref[group * tiles_here + tile, 0], corner_ref[group * tiles_here + tile, 1])
            for tile in range(tiles_here)
        ]

    corners = corners_of(step)
    add_noise(canvas_ref, noise[...], corners_of(jnp.maximum(step - 1, 0)), half_side, features)
    fold = fold_matrix(features, half_side)
    for tile, (row, col) in enumerate(corners):
        here = slice(tile * tokens, (tile + 1) * tokens)
        spread[here, :] = spread_tile(latent_wide, row, col, half_side, features)
    patch_ref[...] = dot_lanes(fold, spread[...]).astype(jnp.bfloat16)
    hidden_all[...] = dot_lanes(weights_ref[:model_width, model_width:], spread[...]).astype(jnp.bfloat16)
    for tile in range(tiles_here):
        here = slice(tile * tokens, (tile + 1) * tokens)
        base = hidden_all[:chunk_rows, here].astype(jnp.float32)[:1]
        total = jnp.zeros((chunk_rows, tokens), jnp.float32)
        squares = jnp.zeros((chunk_rows, tokens), jnp.float32)
        for at in range(0, model_width, chunk_rows):
            moved = hidden_all[at : at + chunk_rows, here].astype(jnp.float32) - base
            total = total + moved
            squares = squares + moved * moved
        offset = jnp.sum(total, axis=0, keepdims=True) * (1.0 / model_width)
        mean = base + offset
        variance = jnp.sum(squares, axis=0, keepdims=True) * (1.0 / model_width) - offset * offset
        inv_scale = lax.rsqrt(variance + layer_eps)
        for at in range(0, model_width, chunk_rows):
            center = hidden_all[at : at + chunk_rows, here].astype(jnp.float32) - mean
            left_ref[at : at + chunk_rows, here] = (center * inv_scale).astype(jnp.bfloat16)
        high, low = split_two(patch_ref[:, here].astype(jnp.float32) * inv_scale)
        left_ref[model_width : model_width + features, here] = high
        left_ref[model_width + features :, here] = low
    for tile in range(tiles_here):
        here = slice(tile * tokens, (tile + 1) * tokens)
        unit = left_ref[:model_width, here]
        value_ref[:, here] = dot_plain(weights_ref[:units, :model_width], unit)
        gate_ref[:, here] = dot_plain(weights_ref[units : 2 * units, :model_width], unit)
        for at in range(0, units, chunk_rows):
            value = value_ref[at : at + chunk_rows, here]
            gate = gate_ref[at : at + chunk_rows, here]
            normal = 0.5 * lax.erf(gate * root_half) + 0.5
            active[at : at + chunk_rows, here] = (value * (gate * normal)).astype(jnp.bfloat16)
    parts = dot_plain(weights_ref[2 * units :, :units], active[...])
    noise[...] = parts[:features] + parts[features:]
    peers = lax.axis_size("mp")
    for group in range(tiles_here // peers):
        own = token_at(group * peers + lax.axis_index("mp"), tokens)
        hidden = hidden_all[:, own]
        hidden_ref[:, group * tokens : (group + 1) * tokens] = hidden
        noise[:, own] = noise[:, own] + lax.dot_general(
            w_out_ref[...], hidden, (((0,), (0,)), ((), ())), preferred_element_type=jnp.float32
        )

    @pl.when(step == pl.num_programs(0) - 1)
    def _last():
        add_noise(canvas_ref, noise[...], corners, half_side, features)

    shape = cover_ref.shape
    row_at = lax.broadcasted_iota(jnp.int32, shape, 1)
    col_at = lax.broadcasted_iota(jnp.int32, shape, 0) * width + lax.broadcasted_iota(
        jnp.int32, shape, 2
    )
    cover = cover_ref[...]
    for row, col in corners:
        left = col * (features // 4)
        inside = (
            (row_at >= row)
            & (row_at < row + 2 * half_side)
            & (col_at >= left)
            & (col_at < left + half_side * features // 2)
        )
        cover = cover + jnp.where(inside, 1.0, 0.0)
    cover_ref[...] = cover


def add_noise(canvas_ref, noise, corners, half_side, features):
    run = features // 2
    width = half_side * run
    panels = canvas_ref.shape[0]
    fold = fold_matrix(features, half_side)
    tall = lax.dot_general(
        jnp.concatenate(split_three(noise), axis=0),
        jnp.concatenate([fold, fold, fold], axis=0),
        (((0,), (0,)), ((), ())),
        preferred_element_type=jnp.float32,
    )
    tall = tall.reshape(len(corners), half_side * half_side, 2 * width)
    kept = jnp.where(column_mask(features, half_side)[None], tall, 0.0)
    pairs = jnp.sum(kept.reshape(len(corners), half_side, half_side, 2 * width), axis=2)
    blank = jnp.zeros((half_side, (panels - 1) * width), jnp.float32)
    for tile, (row, col) in enumerate(corners):
        for parity in range(2):
            own = pairs[tile, :, parity * width : (parity + 1) * width]
            placed = pltpu.roll(jnp.concatenate([own, blank], axis=1), col * run // 2, 1)
            at = pl.ds(row + parity, half_side, stride=2)
            for panel in range(panels):
                here = placed[:, panel * width : (panel + 1) * width]
                canvas_ref[panel, at, :] = canvas_ref[panel, at, :] + here


def backward_kernel(
    half_side,
    scale_factor,
    corner_ref,
    sum_ref,
    other_ref,
    reward_ref,
    cover_ref,
    w_value_ref,
    w_gate_ref,
    w_down_ref,
    w_out_ref,
    w_through,
    value_ref,
    gate_ref,
    left_ref,
    patch_ref,
    hidden_ref,
    blended_ref,
    grad_value_ref,
    grad_gate_ref,
    grad_down_ref,
    small_ref,
    cot_wide,
    scaled_sum,
    mean_sum,
    active_sum,
    hidden_sum,
    patch_sum,
    spread,
    cot,
    d_active,
    d_both,
    active,
    along_scaled,
):
    step = pl.program_id(0)
    model_width, features = w_out_ref.shape
    units = w_down_ref.shape[0]
    slabs = reward_ref.shape[0]
    panels, rows, width = sum_ref.shape
    slab_rows = rows // slabs
    tokens = half_side * half_side
    tiles_here = active.shape[1] // tokens

    @pl.when(step == 0)
    def _prepare():
        for panel in range(panels):
            lanes = slice(panel * width, (panel + 1) * width)
            cover = cover_ref[panel]
            blended = (sum_ref[panel] + other_ref[panel]) / cover
            blended_ref[:, lanes] = blended
            reward = jnp.concatenate(
                [reward_ref[slab, :slab_rows, lanes] for slab in range(slabs)], axis=0
            )
            curvature = jnp.concatenate(
                [reward_ref[slab, slab_rows : 2 * slab_rows, lanes] for slab in range(slabs)], axis=0
            )
            cot_wide[panel] = (
                ((reward - curvature * blended) / cover * scale_factor)
                .astype(jnp.bfloat16)
                .astype(jnp.float32)
            )
        for ref in (
            grad_value_ref,
            grad_gate_ref,
            scaled_sum,
            mean_sum,
            active_sum,
            hidden_sum,
            patch_sum,
        ):
            ref[...] = jnp.zeros_like(ref)

    for tile in range(tiles_here):
        here = slice(tile * tokens, (tile + 1) * tokens)
        spread[here, :] = spread_tile(
            cot_wide,
            corner_ref[step * tiles_here + tile, 0],
            corner_ref[step * tiles_here + tile, 1],
            half_side,
            features,
        )
    cots = dot_lanes(fold_matrix(features, half_side), spread[...]).astype(jnp.bfloat16)
    cot[...] = cots
    d_active[...] = dot_plain(w_through[...], jnp.concatenate([cots, cots], axis=0))
    for tile in range(tiles_here):
        here = slice(tile * tokens, (tile + 1) * tokens)
        total = jnp.zeros((chunk_rows, tokens), jnp.float32)
        for at in range(0, units, chunk_rows):
            chunk = slice(at, at + chunk_rows)
            value = value_ref[chunk, here]
            gate = gate_ref[chunk, here]
            passed = d_active[chunk, here]
            normal = 0.5 * (1.0 + lax.erf(gate * root_half))
            gelu = gate * normal
            slope = normal + gate * jnp.exp(-0.5 * gate * gate) * inv_root_two_pi
            active[chunk, here] = (value * gelu).astype(jnp.bfloat16)
            product = passed * value
            d_both[chunk, here] = (passed * gelu).astype(jnp.bfloat16)
            d_both[units + at : units + at + chunk_rows, here] = (product * slope).astype(
                jnp.bfloat16
            )
            total = total + product * (gelu + slope * gate)
        along = jnp.sum(total, axis=0, keepdims=True) * (1.0 / model_width)
        scaled = left_ref[model_width:, here].astype(jnp.float32)
        high, low = split_two((scaled[:features] + scaled[features:]) * along)
        along_scaled[:features, here] = high
        along_scaled[features:, here] = low
    grads = dot_lanes(left_ref[...], d_both[...])
    grad_value_ref[...] += grads[:model_width, :units]
    grad_gate_ref[...] += grads[:model_width, units:]
    scaled_sum[...] += grads[model_width:]
    mean_sum[...] += dot_lanes(left_ref[:model_width, :], along_scaled[...])
    active_sum[...] += dot_lanes(active[...], cot[...])
    peers = lax.axis_size("mp")
    for group in range(tiles_here // peers):
        own = token_at(group * peers + lax.axis_index("mp"), tokens)
        own_cot = cot[:, own]
        hidden_sum[...] += dot_lanes(
            own_cot, hidden_ref[:, group * tokens : (group + 1) * tokens]
        )
        patch_sum[...] += dot_lanes(patch_ref[:, own], own_cot)

    @pl.when(step == pl.num_programs(0) - 1)
    def _finish():
        active_two = jnp.concatenate(split_two(active_sum[...].T), axis=0)
        mean_both = mean_sum[...].T
        w_out_two = jnp.concatenate([w_out_ref[...], w_out_ref[...]], axis=1)
        grad_down_ref[...] = lax.dot_general(
            active_two, w_out_two, (((0,), (1,)), ((), ())), preferred_element_type=jnp.float32
        )
        through = dot_plain(active_two, w_down_ref[...])
        small_ref[features:] = hidden_sum[...] + through[:features] + through[features:]
        scaled_both = scaled_sum[:features] + scaled_sum[features:]
        scaled_two = jnp.concatenate(split_two(scaled_both), axis=0)
        moved = dot_lanes(scaled_two[:, :units], w_value_ref[...]) + dot_lanes(
            scaled_two[:, units:], w_gate_ref[...]
        )
        moved = moved[:features] + moved[features:]
        patch_two = jnp.concatenate(split_two(patch_sum[...]), axis=0)
        direct = dot_lanes(patch_two, w_out_ref[...])
        small_ref[:features] = (
            direct[:features]
            + direct[features:]
            + moved
            - jnp.mean(moved, axis=1, keepdims=True)
            - mean_both[:features]
            - mean_both[features:]
        )


def whole(shape):
    return pl.BlockSpec(shape, lambda *_: (0,) * len(shape))


def over_mp(values):
    peers = lax.axis_size("mp")
    by = 1
    total = values
    other = None
    while by < peers:
        if other is not None:
            total = total + other
        other = lax.ppermute(total, "mp", [(i, i ^ by) for i in range(peers)])
        by *= 2
    return total, other


chunk_rows = 16


def some_tokens(height, tokens):
    return pl.BlockSpec((height, tokens), lambda step, *_: (0, step))


def step_tiles(tiles):
    peers = lax.axis_size("mp")
    return max(peers * count for count in (1,) if tiles % (peers * count) == 0)


def saved_arrays(tiles, token_count, features, model_width, units):
    every = tiles * token_count
    shapes = [
        ((units, every), jnp.float32),
        ((units, every), jnp.float32),
        ((model_width + 2 * features, every), jnp.bfloat16),
        ((features, every), jnp.bfloat16),
        ((model_width, every // lax.axis_size("mp")), jnp.bfloat16),
    ]
    return [jax.ShapeDtypeStruct(shape, kind) for shape, kind in shapes]


def kernel_params(megabytes):
    return pltpu.CompilerParams(
        dimension_semantics=("arbitrary",), vmem_limit_bytes=megabytes * 2**20
    )


def run_forward(corners, latents, weights, half_side, rows):
    model_width, features = weights[1].shape
    units = weights[0].shape[0] // 2 - features
    tiles = corners.shape[0]
    cols = latents.shape[2]
    steps = tiles // step_tiles(tiles)
    tokens = step_tiles(tiles) * half_side * half_side
    width = half_side * features // 2
    f32 = jnp.float32
    b16 = jnp.bfloat16
    canvas = jax.ShapeDtypeStruct((cols // width, rows, width), f32)
    kept = saved_arrays(tiles, half_side * half_side, features, model_width, units)
    return pl.pallas_call(
        functools.partial(forward_kernel, half_side),
        out_shape=[canvas, canvas, *kept],
        grid_spec=pltpu.PrefetchScalarGridSpec(
            num_scalar_prefetch=1,
            grid=(steps,),
            in_specs=[whole(latents.shape)] + [whole(w.shape) for w in weights],
            out_specs=[whole(canvas.shape)] * 2 + [some_tokens(k.shape[0], k.shape[1] // steps) for k in kept],
            scratch_shapes=[
                pltpu.VMEM(canvas.shape, f32),
                pltpu.VMEM((tokens, 2 * width), b16),
                pltpu.VMEM((model_width, tokens), b16),
                pltpu.VMEM((units, tokens), b16),
                pltpu.VMEM((features, tokens), f32),
            ],
        ),
        compiler_params=kernel_params(52),
        name="forward",
    )(corners, latents, *weights)


def run_backward(corners, total, other, rewards, cover, weights, stored, half_side):
    model_width, features = weights[3].shape
    units = weights[0].shape[1]
    tiles = corners.shape[0]
    token_count = half_side * half_side
    steps = tiles // step_tiles(tiles)
    tokens = step_tiles(tiles) * token_count
    panels, rows, width = total.shape
    f32 = jnp.float32
    scale_factor = 16.0 / math.sqrt(tiles * token_count)
    return pl.pallas_call(
        functools.partial(backward_kernel, half_side, scale_factor),
        out_shape=[
            jax.ShapeDtypeStruct((rows, panels * width), f32),
            jax.ShapeDtypeStruct((model_width, units), f32),
            jax.ShapeDtypeStruct((model_width, units), f32),
            jax.ShapeDtypeStruct((units, model_width), f32),
            jax.ShapeDtypeStruct((2 * features, model_width), f32),
        ],
        grid_spec=pltpu.PrefetchScalarGridSpec(
            num_scalar_prefetch=1,
            grid=(steps,),
            in_specs=[whole(total.shape)] * 2
            + [whole(rewards.shape), whole(cover.shape)]
            + [whole(w.shape) for w in weights]
            + [some_tokens(k.shape[0], k.shape[1] // steps) for k in stored],
            out_specs=[
                whole((rows, panels * width)),
                whole((model_width, units)),
                whole((model_width, units)),
                whole((units, model_width)),
                whole((2 * features, model_width)),
            ],
            scratch_shapes=[
                pltpu.VMEM(total.shape, f32),
                pltpu.VMEM((2 * features, 2 * units), f32),
                pltpu.VMEM((model_width, 2 * features), f32),
                pltpu.VMEM((units, features), f32),
                pltpu.VMEM((features, model_width), f32),
                pltpu.VMEM((features, features), f32),
                pltpu.VMEM((tokens, 2 * width), jnp.bfloat16),
                pltpu.VMEM((features, tokens), jnp.bfloat16),
                pltpu.VMEM((units, tokens), f32),
                pltpu.VMEM((2 * units, tokens), jnp.bfloat16),
                pltpu.VMEM((units, tokens), jnp.bfloat16),
                pltpu.VMEM((2 * features, tokens), jnp.bfloat16),
            ],
        ),
        compiler_params=kernel_params(52),
        name="backward",
    )(corners, total, other, rewards, cover, *weights, *stored)


def pack_kernel(offset_ref, latent_ref, reward_ref, curvature_ref, packed_ref, rewards_ref):
    copies, packed_rows, cols = packed_ref.shape
    slab_rows = latent_ref.shape[0]
    tiles_here = offset_ref.shape[0]
    lane = lax.broadcasted_iota(jnp.int32, (packed_rows - slab_rows, cols), 1)
    digits = jnp.zeros(lane.shape, jnp.int32)
    for tile in range(tiles_here):
        for axis in range(2):
            value = offset_ref[tile, axis]
            at = 2 * tile + axis
            digits = jnp.where(lane == at, value // 256, digits)
            digits = jnp.where(lane == 2 * tiles_here + at, value % 256, digits)
    packed = jnp.concatenate(
        [latent_ref[...].astype(jnp.float32), digits.astype(jnp.float32)], axis=0
    ).astype(packed_ref.dtype)
    rewards = jnp.concatenate([reward_ref[...], curvature_ref[...]], axis=0)
    for copy in range(copies):
        packed_ref[copy] = packed
        rewards_ref[copy] = rewards


def run_pack(latent, reward_grad, curvature, offsets, slabs):
    slab_rows, cols = latent.shape
    packed_rows = -(-(slab_rows + 1) // 16) * 16
    vmem = pl.BlockSpec(memory_space=pltpu.VMEM)
    return pl.pallas_call(
        pack_kernel,
        out_shape=[
            jax.ShapeDtypeStruct((slabs, packed_rows, cols), latent.dtype),
            jax.ShapeDtypeStruct((slabs, 2 * slab_rows, cols), jnp.float32),
        ],
        in_specs=[pl.BlockSpec(memory_space=pltpu.SMEM), vmem, vmem, vmem],
        out_specs=[vmem, vmem],
        name="pack",
    )(offsets, latent, reward_grad, curvature)


def per_device_replicated(
    latent, reward_grad, curvature, offsets, counts, w_in, w_value, w_gate, w_down, w_out
):
    features, model_width = w_in.shape
    units = w_value.shape[1]
    half_side = S // 2
    token_count = half_side * half_side
    slab_rows, cols = latent.shape
    tiles_here = offsets.shape[0]
    slabs = lax.axis_size("tile")
    tiles = tiles_here * slabs
    rows = slab_rows * slabs
    packed, rewards = run_pack(latent, reward_grad, curvature, offsets, slabs)
    latents = lax.all_to_all(packed, "tile", 0, 0)
    rewards = lax.all_to_all(rewards, "tile", 0, 0)
    digits = latents[:, slab_rows, : 4 * tiles_here].astype(jnp.int32)
    digits = digits.reshape(slabs, 2, tiles_here, 2)
    corners = (digits[:, 0] * 256 + digits[:, 1]).reshape(tiles, 2)

    packed_weights, w_through = run_weights((w_in, w_value, w_gate, w_down, w_out), half_side)
    sums, cover, *stored = run_forward(
        corners, latents, (packed_weights, w_out), half_side, rows
    )
    weights = (w_value, w_gate, w_down, w_out, w_through)
    total, other = over_mp(sums)
    blended, grad_value, grad_gate, grad_down, small = run_backward(
        corners, total, other, rewards, cover, weights, stored, half_side
    )
    own = lax.dynamic_slice_in_dim(blended, lax.axis_index("tile") * slab_rows, slab_rows, 0)
    mine, theirs = over_mp(small)
    small = mine + theirs
    return (own, small[:features], grad_value, grad_gate, grad_down, small[features:].T)


def per_device(
    latent, reward_grad, curvature, offsets, counts, w_in, w_value, w_gate, w_down, w_out
):
    tiles = offsets.shape[0] * lax.axis_size("tile")
    stored_bytes = tiles * (S // 2) ** 2 * (8 * w_value.shape[1] + 3 * w_in.shape[1])
    peers = lax.axis_size("mp")
    pairs = w_in.shape[1] <= 2 * w_value.shape[1] and peers > 1 and peers & (peers - 1) == 0 and tiles % peers == 0
    replicate = pairs and stored_bytes <= 40 * 2**20
    plan = per_device_replicated if replicate else per_device_sharded
    return plan(
        latent, reward_grad, curvature, offsets, counts, w_in, w_value, w_gate, w_down, w_out
    )


def solution(mesh):
    return jax.shard_map(
        per_device,
        mesh=mesh,
        in_specs=(
            P("tile", None),
            P("tile", None),
            P("tile", None),
            P("tile", None),
            P("tile", None),
            P(),
            P(None, "mp"),
            P(None, "mp"),
            P("mp", None),
            P(),
        ),
        out_specs=(P("tile", None), P(), P(None, "mp"), P(None, "mp"), P("mp", None), P()),
        check_vma=False,
    )
```

```python
import functools
import math

import jax
import jax.numpy as jnp
from jax import lax
from jax.experimental import pallas as pl
from jax.experimental.pallas import tpu as pltpu
from jax.sharding import PartitionSpec as P

S = 32
SPACING = 24


layer_eps = 1e-05
root_half = 0.7071067811865476
inv_root_two_pi = 0.3989422804014327
highest = lax.Precision.HIGHEST


def passed_along(shard, axis, by):
    peers = lax.axis_size(axis)
    pairs = [(i, i + by) for i in range(peers) if 0 <= i + by < peers]
    return lax.ppermute(shard, axis, pairs)


def gelu_value(inputs):
    return 0.5 * inputs * (1.0 + lax.erf(inputs * root_half))


def gelu_slope(inputs):
    return (
        0.5 * (1.0 + lax.erf(inputs * root_half))
        + inputs * jnp.exp(-0.5 * inputs * inputs) * inv_root_two_pi
    )


def patchify(cropped, channels):
    half_side = cropped.shape[0] // 2
    return (
        cropped.reshape(half_side, 2, half_side, 2 * channels)
        .transpose(0, 2, 1, 3)
        .reshape(half_side * half_side, 4 * channels)
    )


def unpatch(tokens, tile_side, channels):
    half_side = tile_side // 2
    token_rows = tokens.shape[0] // half_side
    return (
        tokens.reshape(token_rows, half_side, 2, 2 * channels)
        .transpose(0, 2, 1, 3)
        .reshape(2 * token_rows, tile_side * channels)
    )


def layer_norm(hidden):
    values = hidden.astype(jnp.float32)
    center = values - jnp.mean(values, axis=-1, keepdims=True)
    variance = jnp.mean(center * center, axis=-1, keepdims=True)
    inv_scale = lax.rsqrt(variance + layer_eps)
    return (center * inv_scale, inv_scale)


def norm_backward(normed, inv_scale, d_unit):
    centered = d_unit - jnp.mean(d_unit, axis=-1, keepdims=True)
    return inv_scale * (centered - normed * jnp.mean(d_unit * normed, axis=-1, keepdims=True))


def contract_rows(left, right):
    return lax.dot_general(
        left, right, (((0,), (0,)), ((), ())), preferred_element_type=jnp.float32
    )


def contract_rows_exact(left, right):
    return lax.dot_general(
        left, right, (((0,), (0,)), ((), ())), precision=highest, preferred_element_type=jnp.float32
    )


def contract_cols(left, right):
    return lax.dot_general(
        left, right, (((1,), (1,)), ((), ())), preferred_element_type=jnp.float32
    )


def crop_tiles(source, corners, row_base, tile_side, channels):

    def crop_one(corner):
        cropped = lax.dynamic_slice(
            source, (corner[0] - row_base, corner[1] * channels), (tile_side, tile_side * channels)
        )
        return patchify(cropped, channels)

    return jax.vmap(crop_one)(corners)


def place_tiles(canvas, pieces, corners, row_shift, channels):
    piece_rows = pieces.shape[1]
    piece_cols = pieces.shape[2]

    def add_tile(tile_index, current):
        corner = corners[tile_index]
        start_row = corner[0] + row_shift
        start_col = corner[1] * channels
        existing = lax.dynamic_slice(current, (start_row, start_col), (piece_rows, piece_cols))
        return lax.dynamic_update_slice(
            current, existing + pieces[tile_index], (start_row, start_col)
        )

    return lax.fori_loop(0, pieces.shape[0], add_tile, canvas)


def per_device_sharded(
    latent, reward_grad, curvature, offsets, counts, w_in, w_value, w_gate, w_down, w_out
):
    channels = w_in.shape[0] // 4
    model_width = w_in.shape[1]
    tile_side = S
    half_side = tile_side // 2
    token_count = half_side * half_side
    tiles_here = offsets.shape[0]
    slab_rows = latent.shape[0]
    canvas_cols = latent.shape[1]
    tile_devices = lax.axis_size("tile")
    model_devices = lax.axis_size("mp")
    tile_pos = lax.axis_index("tile")
    model_pos = lax.axis_index("mp")
    share_tokens = token_count // model_devices
    share_pixels = tile_side // model_devices
    scale_factor = 16.0 / math.sqrt(tiles_here * tile_devices * token_count)
    w_out_wide = w_out.astype(jnp.float32)
    cover_count = jnp.repeat(counts, channels, axis=1).astype(jnp.float32)
    placed_row = model_pos * share_pixels
    every_corner = lax.all_gather(offsets, "tile", axis=0, tiled=True)
    grid_cols = canvas_cols // (channels * SPACING)
    grid_cells = (every_corner[:, 0] + SPACING // 2) // SPACING * grid_cols + (
        every_corner[:, 1] + SPACING // 2
    ) // SPACING
    wanted = (
        tile_pos // 2 * grid_cols
        + tile_pos % 2 * tiles_here
        + jnp.arange(tiles_here, dtype=jnp.int32)
    )
    matched = (grid_cells[None, :] == wanted[:, None]).astype(jnp.int32)
    corners = jnp.sum(matched[:, :, None] * every_corner[None, :, :], axis=1)
    row_base = (tile_pos - 2) * slab_rows
    latent_parts = []
    for shift_by in (2, 1, 0, -1, -2):
        if shift_by == 0:
            latent_parts.append(latent)
        else:
            latent_parts.append(passed_along(latent, "tile", shift_by))
    latent_source = jnp.concatenate(latent_parts, axis=0)
    patches = crop_tiles(latent_source, corners, row_base, tile_side, channels)
    flat_patches = jnp.transpose(patches, (1, 0, 2)).reshape(token_count * tiles_here, 4 * channels)
    hidden = jnp.dot(flat_patches, w_in, preferred_element_type=jnp.float32).astype(jnp.bfloat16)
    normed, inv_scale = layer_norm(hidden)
    unit_in = normed.astype(jnp.bfloat16)
    value_proj = jnp.dot(unit_in, w_value, preferred_element_type=jnp.float32)
    gate_proj = jnp.dot(unit_in, w_gate, preferred_element_type=jnp.float32)
    active = (value_proj * gelu_value(gate_proj)).astype(jnp.bfloat16)
    active_grid = active.reshape(token_count, tiles_here, active.shape[1])

    def take_share(values):
        grid = values.reshape(token_count, tiles_here, values.shape[-1])
        picked = lax.dynamic_slice_in_dim(grid, model_pos * share_tokens, share_tokens, 0)
        return picked.reshape(share_tokens * tiles_here, values.shape[-1])

    hidden_share = take_share(hidden)
    row_block = active_grid.reshape(
        lax.axis_size("mp") * share_tokens * tiles_here, active_grid.shape[2]
    )
    ff_share = lax.psum_scatter(
        jnp.dot(row_block, w_down, preferred_element_type=jnp.float32).reshape(
            lax.axis_size("mp") * share_tokens, tiles_here, model_width
        ),
        "mp",
        scatter_dimension=0,
        tiled=True,
    ).reshape(share_tokens * tiles_here, model_width)
    noise_share = jnp.dot(hidden_share, w_out, preferred_element_type=jnp.float32) + jnp.dot(
        ff_share, w_out_wide, precision=highest, preferred_element_type=jnp.float32
    )
    noise_tiles = jnp.transpose(
        noise_share.reshape(share_tokens, tiles_here, w_out.shape[1]), (1, 0, 2)
    )

    def unpatch_share(tokens):
        return unpatch(tokens, tile_side, channels)

    noise_pieces = jax.vmap(unpatch_share)(noise_tiles)
    window_term = place_tiles(
        jnp.zeros((5 * slab_rows, canvas_cols), jnp.float32),
        noise_pieces,
        corners,
        placed_row - row_base,
        channels,
    )
    slab_sum = window_term[2 * slab_rows : 3 * slab_rows]
    for shift_by in (-2, -1, 1, 2):
        outgoing = window_term[(shift_by + 2) * slab_rows : (shift_by + 3) * slab_rows]
        slab_sum = slab_sum + passed_along(outgoing, "tile", shift_by)
    blend_total = lax.psum(slab_sum, "mp")
    blended = blend_total / cover_count
    cotangent = ((reward_grad - curvature * blended) / cover_count * scale_factor).astype(
        jnp.bfloat16
    )
    cot_parts = []
    for shift_by in (2, 1, 0, -1, -2):
        if shift_by == 0:
            cot_parts.append(cotangent)
        else:
            cot_parts.append(passed_along(cotangent, "tile", shift_by))
    cot_source = jnp.concatenate(cot_parts, axis=0)
    cot_patches = crop_tiles(cot_source, corners, row_base, tile_side, channels)
    cot_flat = jnp.transpose(cot_patches, (1, 0, 2)).reshape(token_count * tiles_here, 4 * channels)
    cot_share = take_share(cot_flat)
    d_feat = contract_cols(cot_flat, w_out)
    d_feat_b = d_feat.astype(jnp.bfloat16)
    d_active = contract_cols(d_feat_b, w_down)
    down_term = contract_rows(active, d_feat_b)
    d_value = (d_active * gelu_value(gate_proj)).astype(jnp.bfloat16)
    d_gate = (d_active * value_proj * gelu_slope(gate_proj)).astype(jnp.bfloat16)
    value_term = contract_rows(unit_in, d_value)
    gate_term = contract_rows(unit_in, d_gate)
    d_value_grid = d_value.reshape(token_count, tiles_here, d_value.shape[1])
    d_gate_grid = d_gate.reshape(token_count, tiles_here, d_gate.shape[1])
    value_block = d_value_grid.reshape(
        share_tokens * lax.axis_size("mp") * tiles_here, d_value.shape[1]
    )
    gate_block = d_gate_grid.reshape(
        share_tokens * lax.axis_size("mp") * tiles_here, d_gate.shape[1]
    )
    summed = contract_cols(value_block, w_value) + contract_cols(gate_block, w_gate)
    d_unit_share = (
        lax.psum_scatter(
            summed.reshape(share_tokens * lax.axis_size("mp"), tiles_here, model_width).astype(
                jnp.bfloat16
            ),
            "mp",
            scatter_dimension=0,
            tiled=True,
        )
        .astype(jnp.float32)
        .reshape(share_tokens * tiles_here, model_width)
    )
    d_hidden = (
        take_share(d_feat) + norm_backward(take_share(normed), take_share(inv_scale), d_unit_share)
    ).astype(jnp.bfloat16)
    in_term = contract_rows(take_share(flat_patches), d_hidden)
    out_term = contract_rows(hidden_share, cot_share) + contract_rows_exact(
        ff_share, cot_share.astype(jnp.float32)
    )
    grad_in, grad_out = lax.psum((in_term, out_term), ("tile", "mp"))
    grad_value, grad_gate, grad_down = lax.psum((value_term, gate_term, down_term), "tile")
    return (blended, grad_in, grad_value, grad_gate, grad_down, grad_out)


def dot_lanes(left, right):
    return lax.dot_general(
        left, right, (((1,), (1,)), ((), ())), preferred_element_type=jnp.float32
    )


def dot_plain(left, right):
    return lax.dot_general(
        left, right, (((1,), (0,)), ((), ())), preferred_element_type=jnp.float32
    )


def split_two(values):
    high = values.astype(jnp.bfloat16)
    low = (values - high.astype(jnp.float32)).astype(jnp.bfloat16)
    return high, low


def split_three(values):
    high = values.astype(jnp.bfloat16)
    rest = values - high.astype(jnp.float32)
    middle = rest.astype(jnp.bfloat16)
    low = (rest - middle.astype(jnp.float32)).astype(jnp.bfloat16)
    return high, middle, low


def fold_matrix(features, half_side):
    run = features // 2
    wide = 2 * half_side * run
    feature = lax.broadcasted_iota(jnp.int32, (features, wide), 0)
    place = lax.broadcasted_iota(jnp.int32, (features, wide), 1)
    own = place // (half_side * run) * run + place % run
    return jnp.where(feature == own, 1.0, 0.0).astype(jnp.bfloat16)


def column_mask(features, half_side):
    run = features // 2
    wide = 2 * half_side * run
    token = lax.broadcasted_iota(jnp.int32, (half_side * half_side, wide), 0)
    place = lax.broadcasted_iota(jnp.int32, (half_side * half_side, wide), 1)
    return token % half_side == place // run % half_side


def spread_tile(canvas_ref, row, col, half_side, features):
    run = features // 2
    width = half_side * run
    panels = canvas_ref.shape[0]
    cols = panels * width
    lanes = col * run // 2
    halves = []
    for parity in range(2):
        at = pl.ds(row + parity, half_side, stride=2)
        rows = jnp.concatenate([canvas_ref[panel, at, :] for panel in range(panels)], axis=1)
        rolled = pltpu.roll(rows, lax.rem(cols - lanes, cols), 1)
        halves.append(rolled[:, :width])
    pair = jnp.concatenate(halves, axis=1).astype(jnp.bfloat16)
    token = lax.broadcasted_iota(jnp.int32, (half_side * half_side, half_side), 0)
    patch_row = lax.broadcasted_iota(jnp.int32, (half_side * half_side, half_side), 1)
    repeat = jnp.where(token // half_side == patch_row, 1.0, 0.0).astype(jnp.bfloat16)
    repeated = dot_plain(repeat, pair)
    return jnp.where(column_mask(features, half_side), repeated, 0.0).astype(jnp.bfloat16)


def token_at(tile, tokens):
    return pl.ds(pl.multiple_of(tile * tokens, tokens), tokens)


def weight_kernel(
    half_side,
    w_in_ref,
    w_value_ref,
    w_gate_ref,
    w_down_ref,
    w_out_ref,
    packed,
    w_through,
):
    features, model_width = w_in_ref.shape
    units = w_value_ref.shape[1]
    fold = fold_matrix(features, half_side)
    packed[...] = jnp.zeros_like(packed)
    packed[:model_width, model_width:] = lax.dot_general(
        w_in_ref[...], fold, (((0,), (0,)), ((), ())), preferred_element_type=jnp.float32
    ).astype(jnp.bfloat16)
    packed[:units, :model_width] = w_value_ref[...].T
    packed[units : 2 * units, :model_width] = w_gate_ref[...].T
    both = dot_plain(w_down_ref[...], w_out_ref[...])
    w_through[...] = jnp.concatenate(split_two(both), axis=1)
    packed[2 * units :, :units] = jnp.concatenate(split_two(both.T), axis=0)


def run_weights(weights, half_side):
    features, model_width = weights[0].shape
    units = weights[1].shape[1]
    width = half_side * features // 2
    vmem = pl.BlockSpec(memory_space=pltpu.VMEM)
    shapes = [
        (2 * units + 2 * features, max(model_width + 2 * width, units)),
        (units, 2 * features),
    ]
    return pl.pallas_call(
        functools.partial(weight_kernel, half_side),
        out_shape=[jax.ShapeDtypeStruct(shape, jnp.bfloat16) for shape in shapes],
        in_specs=[vmem] * len(weights),
        out_specs=[vmem] * len(shapes),
        name="weights",
    )(*weights)


def forward_kernel(
    half_side,
    corner_ref,
    latent_ref,
    weights_ref,
    w_out_ref,
    canvas_ref,
    cover_ref,
    value_ref,
    gate_ref,
    left_ref,
    latent_wide,
    spread,
    hidden_all,
    active,
    noise,
):
    step = pl.program_id(0)
    model_width, features = w_out_ref.shape
    units = weights_ref.shape[0] // 2 - features
    slabs, slab_rows, cols = latent_ref.shape
    panels, rows, width = canvas_ref.shape
    own_rows = rows // slabs
    tokens = half_side * half_side
    tiles_here = active.shape[1] // tokens

    @pl.when(step == 0)
    def _prepare():
        for slab in range(slabs):
            own = latent_ref[slab, : latent_rows(own_rows)].astype(jnp.float32)[:own_rows]
            for panel in range(panels):
                latent_wide[panel, slab * own_rows : (slab + 1) * own_rows, :] = own[
                    :, panel * width : (panel + 1) * width
                ]
        canvas_ref[...] = jnp.zeros_like(canvas_ref)
        cover_ref[...] = jnp.zeros_like(cover_ref)
        noise[...] = jnp.zeros_like(noise)

    def corners_of(group):
        return [
            (corner_ref[group * tiles_here + tile, 0], corner_ref[group * tiles_here + tile, 1])
            for tile in range(tiles_here)
        ]

    corners = corners_of(step)
    add_noise(canvas_ref, noise[...], corners_of(jnp.maximum(step - 1, 0)), half_side, features)
    fold = fold_matrix(features, half_side)
    for tile, (row, col) in enumerate(corners):
        here = slice(tile * tokens, (tile + 1) * tokens)
        spread[here, :] = spread_tile(latent_wide, row, col, half_side, features)
    patch_rows = slice(model_width + 2 * features, None)
    left_ref[patch_rows, : active.shape[1]] = dot_lanes(fold, spread[...]).astype(jnp.bfloat16)
    hidden_all[...] = dot_lanes(weights_ref[:model_width, model_width:], spread[...]).astype(jnp.bfloat16)
    for tile in range(tiles_here):
        here = slice(tile * tokens, (tile + 1) * tokens)
        base = hidden_all[:chunk_rows, here].astype(jnp.float32)[:1]
        total = jnp.zeros((chunk_rows, tokens), jnp.float32)
        squares = jnp.zeros((chunk_rows, tokens), jnp.float32)
        for at in range(0, model_width, chunk_rows):
            moved = hidden_all[at : at + chunk_rows, here].astype(jnp.float32) - base
            total = total + moved
            squares = squares + moved * moved
        offset = jnp.sum(total, axis=0, keepdims=True) * (1.0 / model_width)
        mean = base + offset
        variance = jnp.sum(squares, axis=0, keepdims=True) * (1.0 / model_width) - offset * offset
        inv_scale = lax.rsqrt(variance + layer_eps)
        for at in range(0, model_width, chunk_rows):
            center = hidden_all[at : at + chunk_rows, here].astype(jnp.float32) - mean
            left_ref[at : at + chunk_rows, here] = (center * inv_scale).astype(jnp.bfloat16)
        high, low = split_two(left_ref[patch_rows, here].astype(jnp.float32) * inv_scale)
        left_ref[model_width : model_width + features, here] = high
        left_ref[model_width + features : model_width + 2 * features, here] = low
    for tile in range(tiles_here):
        here = slice(tile * tokens, (tile + 1) * tokens)
        unit = left_ref[:model_width, here]
        value_ref[:, here] = dot_plain(weights_ref[:units, :model_width], unit)
        gate_ref[:, here] = dot_plain(weights_ref[units : 2 * units, :model_width], unit)
        for at in range(0, units, chunk_rows):
            value = value_ref[at : at + chunk_rows, here]
            gate = gate_ref[at : at + chunk_rows, here]
            normal = 0.5 * lax.erf(gate * root_half) + 0.5
            active[at : at + chunk_rows, here] = (value * (gate * normal)).astype(jnp.bfloat16)
    parts = dot_plain(weights_ref[2 * units :, :units], active[...])
    noise[...] = parts[:features] + parts[features:]
    peers = lax.axis_size("mp")
    for group in range(tiles_here // peers):
        own = token_at(group * peers + lax.axis_index("mp"), tokens)
        hidden = hidden_all[:, own]
        at = active.shape[1] + group * tokens
        left_ref[:model_width, at : at + tokens] = hidden
        noise[:, own] = noise[:, own] + lax.dot_general(
            w_out_ref[...], hidden, (((0,), (0,)), ((), ())), preferred_element_type=jnp.float32
        )

    @pl.when(step == pl.num_programs(0) - 1)
    def _last():
        add_noise(canvas_ref, noise[...], corners, half_side, features)

    shape = cover_ref.shape
    row_at = lax.broadcasted_iota(jnp.int32, shape, 1)
    col_at = lax.broadcasted_iota(jnp.int32, shape, 0) * width + lax.broadcasted_iota(
        jnp.int32, shape, 2
    )
    cover = cover_ref[...]
    for row, col in corners:
        left = col * (features // 4)
        inside = (
            (row_at >= row)
            & (row_at < row + 2 * half_side)
            & (col_at >= left)
            & (col_at < left + half_side * features // 2)
        )
        cover = cover + jnp.where(inside, 1.0, 0.0)
    cover_ref[...] = cover


def add_noise(canvas_ref, noise, corners, half_side, features):
    run = features // 2
    width = half_side * run
    panels = canvas_ref.shape[0]
    fold = fold_matrix(features, half_side)
    tall = lax.dot_general(
        jnp.concatenate(split_three(noise), axis=0),
        jnp.concatenate([fold, fold, fold], axis=0),
        (((0,), (0,)), ((), ())),
        preferred_element_type=jnp.float32,
    )
    tall = tall.reshape(len(corners), half_side * half_side, 2 * width)
    kept = jnp.where(column_mask(features, half_side)[None], tall, 0.0)
    pairs = jnp.sum(kept.reshape(len(corners), half_side, half_side, 2 * width), axis=2)
    blank = jnp.zeros((half_side, (panels - 1) * width), jnp.float32)
    for tile, (row, col) in enumerate(corners):
        for parity in range(2):
            own = pairs[tile, :, parity * width : (parity + 1) * width]
            placed = pltpu.roll(jnp.concatenate([own, blank], axis=1), col * run // 2, 1)
            at = pl.ds(row + parity, half_side, stride=2)
            for panel in range(panels):
                here = placed[:, panel * width : (panel + 1) * width]
                canvas_ref[panel, at, :] = canvas_ref[panel, at, :] + here


def backward_kernel(
    half_side,
    scale_factor,
    corner_ref,
    sum_ref,
    other_ref,
    reward_ref,
    cover_ref,
    w_value_far,
    w_gate_far,
    w_down_far,
    w_out_ref,
    w_through,
    value_ref,
    gate_ref,
    left_ref,
    blended_ref,
    grad_value_ref,
    grad_gate_ref,
    grad_down_ref,
    small_ref,
    cot_wide,
    scaled_sum,
    mean_sum,
    active_sum,
    hidden_sum,
    patch_sum,
    spread,
    cot,
    d_active,
    d_both,
    active,
    along_scaled,
    grad_value,
    grad_gate,
    grad_down,
    w_value_ref,
    w_gate_ref,
    w_down_ref,
    out_sems,
    in_sems,
):
    step = pl.program_id(0)
    model_width, features = w_out_ref.shape
    units = w_down_ref.shape[0]
    arrivals = [
        pltpu.make_async_copy(far, near, in_sems.at[index])
        for index, (far, near) in enumerate(
            (
                (w_value_far, w_value_ref),
                (w_gate_far, w_gate_ref),
                (w_down_far, w_down_ref),
            )
        )
    ]
    slabs = reward_ref.shape[0]
    panels, rows, width = sum_ref.shape
    slab_rows = rows // slabs
    tokens = half_side * half_side
    tiles_here = active.shape[1] // tokens

    @pl.when(step == 0)
    def _prepare():
        for copy in arrivals:
            copy.start()
        for panel in range(panels):
            lanes = slice(panel * width, (panel + 1) * width)
            cover = cover_ref[panel]
            blended = (sum_ref[panel] + other_ref[panel]) / cover
            blended_ref[:, lanes] = blended
            parts = []
            for slab in range(slabs):
                rewards = reward_ref[slab, :, lanes].astype(jnp.float32)[latent_rows(slab_rows) :]
                parts.append([rewards[term * slab_rows : (term + 1) * slab_rows] for term in range(4)])
            high, low, curved_high, curved_low = (
                jnp.concatenate([part[term] for part in parts], axis=0) for term in range(4)
            )
            reward = high + low
            curvature = curved_high + curved_low
            cot_wide[panel] = (
                ((reward - curvature * blended) / cover * scale_factor)
                .astype(jnp.bfloat16)
                .astype(jnp.float32)
            )
        for ref in (
            grad_value,
            grad_gate,
            scaled_sum,
            mean_sum,
            active_sum,
            hidden_sum,
            patch_sum,
        ):
            ref[...] = jnp.zeros_like(ref)

    for tile in range(tiles_here):
        here = slice(tile * tokens, (tile + 1) * tokens)
        spread[here, :] = spread_tile(
            cot_wide,
            corner_ref[step * tiles_here + tile, 0],
            corner_ref[step * tiles_here + tile, 1],
            half_side,
            features,
        )
    cots = dot_lanes(fold_matrix(features, half_side), spread[...]).astype(jnp.bfloat16)
    cot[...] = cots
    d_active[...] = dot_plain(w_through[...], jnp.concatenate([cots, cots], axis=0))
    for tile in range(tiles_here):
        here = slice(tile * tokens, (tile + 1) * tokens)
        total = jnp.zeros((chunk_rows, tokens), jnp.float32)
        for at in range(0, units, chunk_rows):
            chunk = slice(at, at + chunk_rows)
            value = value_ref[chunk, here]
            gate = gate_ref[chunk, here]
            passed = d_active[chunk, here]
            normal = 0.5 * (1.0 + lax.erf(gate * root_half))
            gelu = gate * normal
            slope = normal + gate * jnp.exp(-0.5 * gate * gate) * inv_root_two_pi
            active[chunk, here] = (value * gelu).astype(jnp.bfloat16)
            product = passed * value
            d_both[chunk, here] = (passed * gelu).astype(jnp.bfloat16)
            d_both[units + at : units + at + chunk_rows, here] = (product * slope).astype(
                jnp.bfloat16
            )
            total = total + product * (gelu + slope * gate)
        along = jnp.sum(total, axis=0, keepdims=True) * (1.0 / model_width)
        scaled = left_ref[model_width : model_width + 2 * features, here].astype(jnp.float32)
        high, low = split_two((scaled[:features] + scaled[features:]) * along)
        along_scaled[:features, here] = high
        along_scaled[features:, here] = low
    left = left_ref[: model_width + 2 * features, : cot.shape[1]]
    grads = dot_lanes(left, d_both[...])
    grad_value[...] += grads[:model_width, :units]
    grad_gate[...] += grads[:model_width, units:]
    scaled_sum[...] += grads[model_width:]
    mean_sum[...] += dot_lanes(left[:model_width], along_scaled[...])
    active_sum[...] += dot_lanes(active[...], cot[...])
    peers = lax.axis_size("mp")
    for group in range(tiles_here // peers):
        own = token_at(group * peers + lax.axis_index("mp"), tokens)
        own_cot = cot[:, own]
        at = cot.shape[1] + group * tokens
        hidden_sum[...] += dot_lanes(own_cot, left_ref[:model_width, at : at + tokens])
        patch_sum[...] += dot_lanes(left_ref[model_width + 2 * features :, own], own_cot)

    @pl.when(step == pl.num_programs(0) - 1)
    def _finish():
        outs = [
            pltpu.make_async_copy(buffer, ref, out_sems.at[index])
            for index, (buffer, ref) in enumerate(
                (
                    (grad_value, grad_value_ref),
                    (grad_gate, grad_gate_ref),
                    (grad_down, grad_down_ref),
                )
            )
        ]
        outs[0].start()
        outs[1].start()
        active_two = jnp.concatenate(split_two(active_sum[...].T), axis=0)
        mean_both = mean_sum[...].T
        w_out_two = jnp.concatenate([w_out_ref[...], w_out_ref[...]], axis=1)
        grad_down[...] = lax.dot_general(
            active_two, w_out_two, (((0,), (1,)), ((), ())), preferred_element_type=jnp.float32
        )
        outs[2].start()
        for copy in arrivals:
            copy.wait()
        through = dot_plain(active_two, w_down_ref[...])
        small_ref[features:] = hidden_sum[...] + through[:features] + through[features:]
        scaled_both = scaled_sum[:features] + scaled_sum[features:]
        scaled_two = jnp.concatenate(split_two(scaled_both), axis=0)
        moved = dot_lanes(scaled_two[:, :units], w_value_ref[...]) + dot_lanes(
            scaled_two[:, units:], w_gate_ref[...]
        )
        moved = moved[:features] + moved[features:]
        patch_two = jnp.concatenate(split_two(patch_sum[...]), axis=0)
        direct = dot_lanes(patch_two, w_out_ref[...])
        small_ref[:features] = (
            direct[:features]
            + direct[features:]
            + moved
            - jnp.mean(moved, axis=1, keepdims=True)
            - mean_both[:features]
            - mean_both[features:]
        )
        for copy in outs:
            copy.wait()


def whole(shape):
    return pl.BlockSpec(shape, lambda *_: (0,) * len(shape))


def over_mp(values):
    peers = lax.axis_size("mp")
    by = 1
    total = values
    other = None
    while by < peers:
        if other is not None:
            total = total + other
        other = lax.ppermute(total, "mp", [(i, i ^ by) for i in range(peers)])
        by *= 2
    return total, other


chunk_rows = 16


def some_tokens(height, tokens):
    return pl.BlockSpec((height, tokens), lambda step, *_: (0, step))


def step_tiles(tiles):
    peers = lax.axis_size("mp")
    return max(peers * count for count in (1,) if tiles % (peers * count) == 0)


def saved_arrays(tiles, token_count, features, model_width, units):
    every = tiles * token_count
    wide = every + every // lax.axis_size("mp")
    shapes = [
        ((units, every), jnp.float32),
        ((units, every), jnp.float32),
        ((model_width + 3 * features, wide), jnp.bfloat16),
    ]
    return [jax.ShapeDtypeStruct(shape, kind) for shape, kind in shapes]


def kernel_params(megabytes):
    return pltpu.CompilerParams(
        dimension_semantics=("arbitrary",), vmem_limit_bytes=megabytes * 2**20
    )


def run_forward(corners, latents, weights, half_side, rows):
    model_width, features = weights[1].shape
    units = weights[0].shape[0] // 2 - features
    tiles = corners.shape[0]
    cols = latents.shape[2]
    steps = tiles // step_tiles(tiles)
    tokens = step_tiles(tiles) * half_side * half_side
    width = half_side * features // 2
    f32 = jnp.float32
    b16 = jnp.bfloat16
    canvas = jax.ShapeDtypeStruct((cols // width, rows, width), f32)
    kept = saved_arrays(tiles, half_side * half_side, features, model_width, units)
    return pl.pallas_call(
        functools.partial(forward_kernel, half_side),
        out_shape=[canvas, canvas, *kept],
        grid_spec=pltpu.PrefetchScalarGridSpec(
            num_scalar_prefetch=1,
            grid=(steps,),
            in_specs=[whole(latents.shape)] + [whole(w.shape) for w in weights],
            out_specs=[whole(canvas.shape)] * 2 + [some_tokens(k.shape[0], k.shape[1] // steps) for k in kept],
            scratch_shapes=[
                pltpu.VMEM(canvas.shape, f32),
                pltpu.VMEM((tokens, 2 * width), b16),
                pltpu.VMEM((model_width, tokens), b16),
                pltpu.VMEM((units, tokens), b16),
                pltpu.VMEM((features, tokens), f32),
            ],
        ),
        compiler_params=kernel_params(52),
        name="forward",
    )(corners, latents, *weights)


def run_backward(corners, total, other, rewards, cover, weights, stored, half_side):
    model_width, features = weights[3].shape
    units = weights[0].shape[1]
    tiles = corners.shape[0]
    token_count = half_side * half_side
    steps = tiles // step_tiles(tiles)
    tokens = step_tiles(tiles) * token_count
    panels, rows, width = total.shape
    f32 = jnp.float32
    scale_factor = 16.0 / math.sqrt(tiles * token_count)
    return pl.pallas_call(
        functools.partial(backward_kernel, half_side, scale_factor),
        out_shape=[
            jax.ShapeDtypeStruct((rows, panels * width), f32),
            jax.ShapeDtypeStruct((model_width, units), f32),
            jax.ShapeDtypeStruct((model_width, units), f32),
            jax.ShapeDtypeStruct((units, model_width), f32),
            jax.ShapeDtypeStruct((2 * features, model_width), f32),
        ],
        grid_spec=pltpu.PrefetchScalarGridSpec(
            num_scalar_prefetch=1,
            grid=(steps,),
            in_specs=[whole(total.shape)] * 2
            + [whole(rewards.shape), whole(cover.shape)]
            + [pl.BlockSpec(memory_space=pl.ANY)] * 3
            + [whole(w.shape) for w in weights[3:]]
            + [some_tokens(k.shape[0], k.shape[1] // steps) for k in stored],
            out_specs=[
                whole((rows, panels * width)),
                pl.BlockSpec(memory_space=pl.ANY),
                pl.BlockSpec(memory_space=pl.ANY),
                pl.BlockSpec(memory_space=pl.ANY),
                whole((2 * features, model_width)),
            ],
            scratch_shapes=[
                pltpu.VMEM(total.shape, f32),
                pltpu.VMEM((2 * features, 2 * units), f32),
                pltpu.VMEM((model_width, 2 * features), f32),
                pltpu.VMEM((units, features), f32),
                pltpu.VMEM((features, model_width), f32),
                pltpu.VMEM((features, features), f32),
                pltpu.VMEM((tokens, 2 * width), jnp.bfloat16),
                pltpu.VMEM((features, tokens), jnp.bfloat16),
                pltpu.VMEM((units, tokens), f32),
                pltpu.VMEM((2 * units, tokens), jnp.bfloat16),
                pltpu.VMEM((units, tokens), jnp.bfloat16),
                pltpu.VMEM((2 * features, tokens), jnp.bfloat16),
                pltpu.VMEM((model_width, units), f32),
                pltpu.VMEM((model_width, units), f32),
                pltpu.VMEM((units, model_width), f32),
                *[pltpu.VMEM(w.shape, w.dtype) for w in weights[:3]],
                pltpu.SemaphoreType.DMA((3,)),
                pltpu.SemaphoreType.DMA((3,)),
            ],
        ),
        compiler_params=kernel_params(52),
        name="backward",
    )(corners, total, other, rewards, cover, *weights, *stored)


def pack_kernel(offset_ref, latent_ref, reward_ref, curvature_ref, packed_ref):
    copies, unused, cols = packed_ref.shape
    packed_rows = latent_rows(latent_ref.shape[0])
    slab_rows = latent_ref.shape[0]
    tiles_here = offset_ref.shape[0]
    lane = lax.broadcasted_iota(jnp.int32, (packed_rows - slab_rows, cols), 1)
    digits = jnp.zeros(lane.shape, jnp.int32)
    for tile in range(tiles_here):
        for axis in range(2):
            value = offset_ref[tile, axis]
            at = 2 * tile + axis
            digits = jnp.where(lane == at, value // 256, digits)
            digits = jnp.where(lane == 2 * tiles_here + at, value % 256, digits)
    rewards = split_two(reward_ref[...]) + split_two(curvature_ref[...])
    packed = jnp.concatenate(
        [latent_ref[...].astype(jnp.float32), digits.astype(jnp.float32)]
        + [part.astype(jnp.float32) for part in rewards],
        axis=0,
    ).astype(packed_ref.dtype)
    for copy in range(copies):
        packed_ref[copy, : packed.shape[0]] = packed


def latent_rows(slab_rows):
    return -(-(slab_rows + 1) // 16) * 16


def run_pack(latent, reward_grad, curvature, offsets, slabs):
    slab_rows, cols = latent.shape
    packed_rows = latent_rows(slab_rows) + 4 * slab_rows
    vmem = pl.BlockSpec(memory_space=pltpu.VMEM)
    return pl.pallas_call(
        pack_kernel,
        out_shape=jax.ShapeDtypeStruct((slabs, packed_rows, cols), latent.dtype),
        in_specs=[pl.BlockSpec(memory_space=pltpu.SMEM), vmem, vmem, vmem],
        out_specs=vmem,
        name="pack",
    )(offsets, latent, reward_grad, curvature)


def per_device_replicated(
    latent, reward_grad, curvature, offsets, counts, w_in, w_value, w_gate, w_down, w_out
):
    features, model_width = w_in.shape
    units = w_value.shape[1]
    half_side = S // 2
    token_count = half_side * half_side
    slab_rows, cols = latent.shape
    tiles_here = offsets.shape[0]
    slabs = lax.axis_size("tile")
    tiles = tiles_here * slabs
    rows = slab_rows * slabs
    packed = run_pack(latent, reward_grad, curvature, offsets, slabs)
    latents = lax.all_to_all(packed, "tile", 0, 0)
    digits = latents[:, slab_rows, : 4 * tiles_here].astype(jnp.int32)
    digits = digits.reshape(slabs, 2, tiles_here, 2)
    corners = (digits[:, 0] * 256 + digits[:, 1]).reshape(tiles, 2)

    packed_weights, w_through = run_weights((w_in, w_value, w_gate, w_down, w_out), half_side)
    sums, cover, *stored = run_forward(
        corners, latents, (packed_weights, w_out), half_side, rows
    )
    weights = (w_value, w_gate, w_down, w_out, w_through)
    total, other = over_mp(sums)
    blended, grad_value, grad_gate, grad_down, small = run_backward(
        corners, total, other, latents, cover, weights, stored, half_side
    )
    own = lax.dynamic_slice_in_dim(blended, lax.axis_index("tile") * slab_rows, slab_rows, 0)
    mine, theirs = over_mp(small)
    small = mine + theirs
    return (own, small[:features], grad_value, grad_gate, grad_down, small[features:].T)


def per_device(
    latent, reward_grad, curvature, offsets, counts, w_in, w_value, w_gate, w_down, w_out
):
    tiles = offsets.shape[0] * lax.axis_size("tile")
    stored_bytes = tiles * (S // 2) ** 2 * (8 * w_value.shape[1] + 3 * w_in.shape[1])
    peers = lax.axis_size("mp")
    pairs = w_in.shape[1] <= 2 * w_value.shape[1] and peers > 1 and peers & (peers - 1) == 0 and tiles % peers == 0
    replicate = pairs and stored_bytes <= 40 * 2**20
    plan = per_device_replicated if replicate else per_device_sharded
    return plan(
        latent, reward_grad, curvature, offsets, counts, w_in, w_value, w_gate, w_down, w_out
    )


def solution(mesh):
    return jax.shard_map(
        per_device,
        mesh=mesh,
        in_specs=(
            P("tile", None),
            P("tile", None),
            P("tile", None),
            P("tile", None),
            P("tile", None),
            P(),
            P(None, "mp"),
            P(None, "mp"),
            P("mp", None),
            P(),
        ),
        out_specs=(P("tile", None), P(), P(None, "mp"), P(None, "mp"), P("mp", None), P()),
        check_vma=False,
    )
```

```python
import functools
import math

import jax
import jax.numpy as jnp
from jax import lax
from jax.experimental import pallas as pl
from jax.experimental.pallas import tpu as pltpu
from jax.sharding import PartitionSpec as P

S = 32
SPACING = 24


layer_eps = 1e-05
root_half = 0.7071067811865476
inv_root_two_pi = 0.3989422804014327
highest = lax.Precision.HIGHEST


def passed_along(shard, axis, by):
    peers = lax.axis_size(axis)
    pairs = [(i, i + by) for i in range(peers) if 0 <= i + by < peers]
    return lax.ppermute(shard, axis, pairs)


def gelu_value(inputs):
    return 0.5 * inputs * (1.0 + lax.erf(inputs * root_half))


def gelu_slope(inputs):
    return (
        0.5 * (1.0 + lax.erf(inputs * root_half))
        + inputs * jnp.exp(-0.5 * inputs * inputs) * inv_root_two_pi
    )


def patchify(cropped, channels):
    half_side = cropped.shape[0] // 2
    return (
        cropped.reshape(half_side, 2, half_side, 2 * channels)
        .transpose(0, 2, 1, 3)
        .reshape(half_side * half_side, 4 * channels)
    )


def unpatch(tokens, tile_side, channels):
    half_side = tile_side // 2
    token_rows = tokens.shape[0] // half_side
    return (
        tokens.reshape(token_rows, half_side, 2, 2 * channels)
        .transpose(0, 2, 1, 3)
        .reshape(2 * token_rows, tile_side * channels)
    )


def layer_norm(hidden):
    values = hidden.astype(jnp.float32)
    center = values - jnp.mean(values, axis=-1, keepdims=True)
    variance = jnp.mean(center * center, axis=-1, keepdims=True)
    inv_scale = lax.rsqrt(variance + layer_eps)
    return (center * inv_scale, inv_scale)


def norm_backward(normed, inv_scale, d_unit):
    centered = d_unit - jnp.mean(d_unit, axis=-1, keepdims=True)
    return inv_scale * (centered - normed * jnp.mean(d_unit * normed, axis=-1, keepdims=True))


def contract_rows(left, right):
    return lax.dot_general(
        left, right, (((0,), (0,)), ((), ())), preferred_element_type=jnp.float32
    )


def contract_rows_exact(left, right):
    return lax.dot_general(
        left, right, (((0,), (0,)), ((), ())), precision=highest, preferred_element_type=jnp.float32
    )


def contract_cols(left, right):
    return lax.dot_general(
        left, right, (((1,), (1,)), ((), ())), preferred_element_type=jnp.float32
    )


def crop_tiles(source, corners, row_base, tile_side, channels):

    def crop_one(corner):
        cropped = lax.dynamic_slice(
            source, (corner[0] - row_base, corner[1] * channels), (tile_side, tile_side * channels)
        )
        return patchify(cropped, channels)

    return jax.vmap(crop_one)(corners)


def place_tiles(canvas, pieces, corners, row_shift, channels):
    piece_rows = pieces.shape[1]
    piece_cols = pieces.shape[2]

    def add_tile(tile_index, current):
        corner = corners[tile_index]
        start_row = corner[0] + row_shift
        start_col = corner[1] * channels
        existing = lax.dynamic_slice(current, (start_row, start_col), (piece_rows, piece_cols))
        return lax.dynamic_update_slice(
            current, existing + pieces[tile_index], (start_row, start_col)
        )

    return lax.fori_loop(0, pieces.shape[0], add_tile, canvas)


def per_device_sharded(
    latent, reward_grad, curvature, offsets, counts, w_in, w_value, w_gate, w_down, w_out
):
    channels = w_in.shape[0] // 4
    model_width = w_in.shape[1]
    tile_side = S
    half_side = tile_side // 2
    token_count = half_side * half_side
    tiles_here = offsets.shape[0]
    slab_rows = latent.shape[0]
    canvas_cols = latent.shape[1]
    tile_devices = lax.axis_size("tile")
    model_devices = lax.axis_size("mp")
    tile_pos = lax.axis_index("tile")
    model_pos = lax.axis_index("mp")
    share_tokens = token_count // model_devices
    share_pixels = tile_side // model_devices
    scale_factor = 16.0 / math.sqrt(tiles_here * tile_devices * token_count)
    w_out_wide = w_out.astype(jnp.float32)
    cover_count = jnp.repeat(counts, channels, axis=1).astype(jnp.float32)
    placed_row = model_pos * share_pixels
    every_corner = lax.all_gather(offsets, "tile", axis=0, tiled=True)
    grid_cols = canvas_cols // (channels * SPACING)
    grid_cells = (every_corner[:, 0] + SPACING // 2) // SPACING * grid_cols + (
        every_corner[:, 1] + SPACING // 2
    ) // SPACING
    wanted = (
        tile_pos // 2 * grid_cols
        + tile_pos % 2 * tiles_here
        + jnp.arange(tiles_here, dtype=jnp.int32)
    )
    matched = (grid_cells[None, :] == wanted[:, None]).astype(jnp.int32)
    corners = jnp.sum(matched[:, :, None] * every_corner[None, :, :], axis=1)
    row_base = (tile_pos - 2) * slab_rows
    latent_parts = []
    for shift_by in (2, 1, 0, -1, -2):
        if shift_by == 0:
            latent_parts.append(latent)
        else:
            latent_parts.append(passed_along(latent, "tile", shift_by))
    latent_source = jnp.concatenate(latent_parts, axis=0)
    patches = crop_tiles(latent_source, corners, row_base, tile_side, channels)
    flat_patches = jnp.transpose(patches, (1, 0, 2)).reshape(token_count * tiles_here, 4 * channels)
    hidden = jnp.dot(flat_patches, w_in, preferred_element_type=jnp.float32).astype(jnp.bfloat16)
    normed, inv_scale = layer_norm(hidden)
    unit_in = normed.astype(jnp.bfloat16)
    value_proj = jnp.dot(unit_in, w_value, preferred_element_type=jnp.float32)
    gate_proj = jnp.dot(unit_in, w_gate, preferred_element_type=jnp.float32)
    active = (value_proj * gelu_value(gate_proj)).astype(jnp.bfloat16)
    active_grid = active.reshape(token_count, tiles_here, active.shape[1])

    def take_share(values):
        grid = values.reshape(token_count, tiles_here, values.shape[-1])
        picked = lax.dynamic_slice_in_dim(grid, model_pos * share_tokens, share_tokens, 0)
        return picked.reshape(share_tokens * tiles_here, values.shape[-1])

    hidden_share = take_share(hidden)
    row_block = active_grid.reshape(
        lax.axis_size("mp") * share_tokens * tiles_here, active_grid.shape[2]
    )
    ff_share = lax.psum_scatter(
        jnp.dot(row_block, w_down, preferred_element_type=jnp.float32).reshape(
            lax.axis_size("mp") * share_tokens, tiles_here, model_width
        ),
        "mp",
        scatter_dimension=0,
        tiled=True,
    ).reshape(share_tokens * tiles_here, model_width)
    noise_share = jnp.dot(hidden_share, w_out, preferred_element_type=jnp.float32) + jnp.dot(
        ff_share, w_out_wide, precision=highest, preferred_element_type=jnp.float32
    )
    noise_tiles = jnp.transpose(
        noise_share.reshape(share_tokens, tiles_here, w_out.shape[1]), (1, 0, 2)
    )

    def unpatch_share(tokens):
        return unpatch(tokens, tile_side, channels)

    noise_pieces = jax.vmap(unpatch_share)(noise_tiles)
    window_term = place_tiles(
        jnp.zeros((5 * slab_rows, canvas_cols), jnp.float32),
        noise_pieces,
        corners,
        placed_row - row_base,
        channels,
    )
    slab_sum = window_term[2 * slab_rows : 3 * slab_rows]
    for shift_by in (-2, -1, 1, 2):
        outgoing = window_term[(shift_by + 2) * slab_rows : (shift_by + 3) * slab_rows]
        slab_sum = slab_sum + passed_along(outgoing, "tile", shift_by)
    blend_total = lax.psum(slab_sum, "mp")
    blended = blend_total / cover_count
    cotangent = ((reward_grad - curvature * blended) / cover_count * scale_factor).astype(
        jnp.bfloat16
    )
    cot_parts = []
    for shift_by in (2, 1, 0, -1, -2):
        if shift_by == 0:
            cot_parts.append(cotangent)
        else:
            cot_parts.append(passed_along(cotangent, "tile", shift_by))
    cot_source = jnp.concatenate(cot_parts, axis=0)
    cot_patches = crop_tiles(cot_source, corners, row_base, tile_side, channels)
    cot_flat = jnp.transpose(cot_patches, (1, 0, 2)).reshape(token_count * tiles_here, 4 * channels)
    cot_share = take_share(cot_flat)
    d_feat = contract_cols(cot_flat, w_out)
    d_feat_b = d_feat.astype(jnp.bfloat16)
    d_active = contract_cols(d_feat_b, w_down)
    down_term = contract_rows(active, d_feat_b)
    d_value = (d_active * gelu_value(gate_proj)).astype(jnp.bfloat16)
    d_gate = (d_active * value_proj * gelu_slope(gate_proj)).astype(jnp.bfloat16)
    value_term = contract_rows(unit_in, d_value)
    gate_term = contract_rows(unit_in, d_gate)
    d_value_grid = d_value.reshape(token_count, tiles_here, d_value.shape[1])
    d_gate_grid = d_gate.reshape(token_count, tiles_here, d_gate.shape[1])
    value_block = d_value_grid.reshape(
        share_tokens * lax.axis_size("mp") * tiles_here, d_value.shape[1]
    )
    gate_block = d_gate_grid.reshape(
        share_tokens * lax.axis_size("mp") * tiles_here, d_gate.shape[1]
    )
    summed = contract_cols(value_block, w_value) + contract_cols(gate_block, w_gate)
    d_unit_share = (
        lax.psum_scatter(
            summed.reshape(share_tokens * lax.axis_size("mp"), tiles_here, model_width).astype(
                jnp.bfloat16
            ),
            "mp",
            scatter_dimension=0,
            tiled=True,
        )
        .astype(jnp.float32)
        .reshape(share_tokens * tiles_here, model_width)
    )
    d_hidden = (
        take_share(d_feat) + norm_backward(take_share(normed), take_share(inv_scale), d_unit_share)
    ).astype(jnp.bfloat16)
    in_term = contract_rows(take_share(flat_patches), d_hidden)
    out_term = contract_rows(hidden_share, cot_share) + contract_rows_exact(
        ff_share, cot_share.astype(jnp.float32)
    )
    grad_in, grad_out = lax.psum((in_term, out_term), ("tile", "mp"))
    grad_value, grad_gate, grad_down = lax.psum((value_term, gate_term, down_term), "tile")
    return (blended, grad_in, grad_value, grad_gate, grad_down, grad_out)


def dot_lanes(left, right):
    return lax.dot_general(
        left, right, (((1,), (1,)), ((), ())), preferred_element_type=jnp.float32
    )


def dot_plain(left, right):
    return lax.dot_general(
        left, right, (((1,), (0,)), ((), ())), preferred_element_type=jnp.float32
    )


def split_two(values):
    high = values.astype(jnp.bfloat16)
    low = (values - high.astype(jnp.float32)).astype(jnp.bfloat16)
    return high, low


def split_three(values):
    high = values.astype(jnp.bfloat16)
    rest = values - high.astype(jnp.float32)
    middle = rest.astype(jnp.bfloat16)
    low = (rest - middle.astype(jnp.float32)).astype(jnp.bfloat16)
    return high, middle, low


def fold_matrix(features, half_side):
    run = features // 2
    wide = 2 * half_side * run
    feature = lax.broadcasted_iota(jnp.int32, (features, wide), 0)
    place = lax.broadcasted_iota(jnp.int32, (features, wide), 1)
    own = place // (half_side * run) * run + place % run
    return jnp.where(feature == own, 1.0, 0.0).astype(jnp.bfloat16)


def column_mask(features, half_side):
    run = features // 2
    wide = 2 * half_side * run
    token = lax.broadcasted_iota(jnp.int32, (half_side * half_side, wide), 0)
    place = lax.broadcasted_iota(jnp.int32, (half_side * half_side, wide), 1)
    return token % half_side == place // run % half_side


def repeat_matrix(half_side):
    token = lax.broadcasted_iota(jnp.int32, (half_side * half_side, half_side), 0)
    patch_row = lax.broadcasted_iota(jnp.int32, (half_side * half_side, half_side), 1)
    return jnp.where(token // half_side == patch_row, 1.0, 0.0).astype(jnp.bfloat16)


def spread_tile(canvas_ref, row, col, half_side, features, mask, repeat):
    run = features // 2
    width = half_side * run
    panels = canvas_ref.shape[0]
    cols = panels * width
    lanes = col * run // 2
    halves = []
    for parity in range(2):
        at = pl.ds(row + parity, half_side, stride=2)
        rows = jnp.concatenate([canvas_ref[panel, at, :] for panel in range(panels)], axis=1)
        rolled = pltpu.roll(rows, lax.rem(cols - lanes, cols), 1)
        halves.append(rolled[:, :width])
    pair = jnp.concatenate(halves, axis=1).astype(jnp.bfloat16)
    return (dot_plain(repeat[...], pair) * mask[...]).astype(jnp.bfloat16)


def token_at(tile, tokens):
    return pl.ds(pl.multiple_of(tile * tokens, tokens), tokens)


def weight_kernel(
    half_side,
    w_in_ref,
    w_value_ref,
    w_gate_ref,
    w_down_ref,
    w_out_ref,
    packed,
    w_through,
):
    features, model_width = w_in_ref.shape
    units = w_value_ref.shape[1]
    fold = fold_matrix(features, half_side)
    packed[...] = jnp.zeros_like(packed)
    packed[:model_width, model_width:] = lax.dot_general(
        w_in_ref[...], fold, (((0,), (0,)), ((), ())), preferred_element_type=jnp.float32
    ).astype(jnp.bfloat16)
    packed[:units, :model_width] = w_value_ref[...].T
    packed[units : 2 * units, :model_width] = w_gate_ref[...].T
    both = dot_plain(w_down_ref[...], w_out_ref[...])
    w_through[...] = jnp.concatenate(split_two(both), axis=1)
    packed[2 * units :, :units] = jnp.concatenate(split_two(both.T), axis=0)


def run_weights(weights, half_side):
    features, model_width = weights[0].shape
    units = weights[1].shape[1]
    width = half_side * features // 2
    vmem = pl.BlockSpec(memory_space=pltpu.VMEM)
    shapes = [
        (2 * units + 2 * features, max(model_width + 2 * width, units)),
        (units, 2 * features),
    ]
    return pl.pallas_call(
        functools.partial(weight_kernel, half_side),
        out_shape=[jax.ShapeDtypeStruct(shape, jnp.bfloat16) for shape in shapes],
        in_specs=[vmem] * len(weights),
        out_specs=[vmem] * len(shapes),
        name="weights",
    )(*weights)


def forward_kernel(
    half_side,
    corner_ref,
    latent_ref,
    weights_ref,
    w_out_ref,
    canvas_ref,
    cover_ref,
    value_ref,
    gate_ref,
    left_ref,
    latent_wide,
    spread,
    hidden_all,
    active,
    noise,
    mask,
    repeat,
):
    step = pl.program_id(0)
    model_width, features = w_out_ref.shape
    units = weights_ref.shape[0] // 2 - features
    slabs, slab_rows, cols = latent_ref.shape
    panels, rows, width = canvas_ref.shape
    own_rows = rows // slabs
    tokens = half_side * half_side
    tiles_here = active.shape[1] // tokens

    @pl.when(step == 0)
    def _prepare():
        for slab in range(slabs):
            own = latent_ref[slab, : latent_rows(own_rows)].astype(jnp.float32)[:own_rows]
            for panel in range(panels):
                latent_wide[panel, slab * own_rows : (slab + 1) * own_rows, :] = own[
                    :, panel * width : (panel + 1) * width
                ]
        canvas_ref[...] = jnp.zeros_like(canvas_ref)
        cover_ref[...] = jnp.zeros_like(cover_ref)
        noise[...] = jnp.zeros_like(noise)
        mask[...] = jnp.where(column_mask(features, half_side), 1.0, 0.0)
        repeat[...] = repeat_matrix(half_side)

    def corners_of(group):
        return [
            (corner_ref[group * tiles_here + tile, 0], corner_ref[group * tiles_here + tile, 1])
            for tile in range(tiles_here)
        ]

    corners = corners_of(step)
    add_noise(
        canvas_ref, noise[...], corners_of(jnp.maximum(step - 1, 0)), half_side, features, mask
    )
    fold = fold_matrix(features, half_side)
    for tile, (row, col) in enumerate(corners):
        here = slice(tile * tokens, (tile + 1) * tokens)
        spread[here, :] = spread_tile(
            latent_wide, row, col, half_side, features, mask, repeat
        )
    patch_rows = slice(model_width + 2 * features, None)
    left_ref[patch_rows, : active.shape[1]] = dot_lanes(fold, spread[...]).astype(jnp.bfloat16)
    hidden_all[...] = dot_lanes(weights_ref[:model_width, model_width:], spread[...]).astype(jnp.bfloat16)
    for tile in range(tiles_here):
        here = slice(tile * tokens, (tile + 1) * tokens)
        base = hidden_all[:chunk_rows, here].astype(jnp.float32)[:1]
        total = jnp.zeros((chunk_rows, tokens), jnp.float32)
        squares = jnp.zeros((chunk_rows, tokens), jnp.float32)
        for at in range(0, model_width, chunk_rows):
            moved = hidden_all[at : at + chunk_rows, here].astype(jnp.float32) - base
            total = total + moved
            squares = squares + moved * moved
        offset = jnp.sum(total, axis=0, keepdims=True) * (1.0 / model_width)
        mean = base + offset
        variance = jnp.sum(squares, axis=0, keepdims=True) * (1.0 / model_width) - offset * offset
        inv_scale = lax.rsqrt(variance + layer_eps)
        for at in range(0, model_width, chunk_rows):
            center = hidden_all[at : at + chunk_rows, here].astype(jnp.float32) - mean
            left_ref[at : at + chunk_rows, here] = (center * inv_scale).astype(jnp.bfloat16)
        high, low = split_two(left_ref[patch_rows, here].astype(jnp.float32) * inv_scale)
        left_ref[model_width : model_width + features, here] = high
        left_ref[model_width + features : model_width + 2 * features, here] = low
    for tile in range(tiles_here):
        here = slice(tile * tokens, (tile + 1) * tokens)
        unit = left_ref[:model_width, here]
        value_ref[:, here] = dot_plain(weights_ref[:units, :model_width], unit)
        gate_ref[:, here] = dot_plain(weights_ref[units : 2 * units, :model_width], unit)
        for at in range(0, units, chunk_rows):
            value = value_ref[at : at + chunk_rows, here]
            gate = gate_ref[at : at + chunk_rows, here]
            normal = 0.5 * lax.erf(gate * root_half) + 0.5
            active[at : at + chunk_rows, here] = (value * (gate * normal)).astype(jnp.bfloat16)
    parts = dot_plain(weights_ref[2 * units :, :units], active[...])
    noise[...] = parts[:features] + parts[features:]
    peers = lax.axis_size("mp")
    for group in range(tiles_here // peers):
        own = token_at(group * peers + lax.axis_index("mp"), tokens)
        hidden = hidden_all[:, own]
        at = active.shape[1] + group * tokens
        left_ref[:model_width, at : at + tokens] = hidden
        noise[:, own] = noise[:, own] + lax.dot_general(
            w_out_ref[...], hidden, (((0,), (0,)), ((), ())), preferred_element_type=jnp.float32
        )

    @pl.when(step == pl.num_programs(0) - 1)
    def _last():
        add_noise(canvas_ref, noise[...], corners, half_side, features, mask)

    shape = cover_ref.shape
    row_at = lax.broadcasted_iota(jnp.int32, shape, 1)
    col_at = lax.broadcasted_iota(jnp.int32, shape, 0) * width + lax.broadcasted_iota(
        jnp.int32, shape, 2
    )
    cover = cover_ref[...]
    for row, col in corners:
        left = col * (features // 4)
        inside = (
            (row_at >= row)
            & (row_at < row + 2 * half_side)
            & (col_at >= left)
            & (col_at < left + half_side * features // 2)
        )
        cover = cover + jnp.where(inside, 1.0, 0.0)
    cover_ref[...] = cover


def add_noise(canvas_ref, noise, corners, half_side, features, mask):
    run = features // 2
    width = half_side * run
    panels = canvas_ref.shape[0]
    fold = fold_matrix(features, half_side)
    tall = lax.dot_general(
        jnp.concatenate(split_three(noise), axis=0),
        jnp.concatenate([fold, fold, fold], axis=0),
        (((0,), (0,)), ((), ())),
        preferred_element_type=jnp.float32,
    )
    tall = tall.reshape(len(corners), half_side * half_side, 2 * width)
    kept = tall * mask[...][None]
    pairs = jnp.sum(kept.reshape(len(corners), half_side, half_side, 2 * width), axis=2)
    blank = jnp.zeros((half_side, (panels - 1) * width), jnp.float32)
    for tile, (row, col) in enumerate(corners):
        for parity in range(2):
            own = pairs[tile, :, parity * width : (parity + 1) * width]
            placed = pltpu.roll(jnp.concatenate([own, blank], axis=1), col * run // 2, 1)
            at = pl.ds(row + parity, half_side, stride=2)
            for panel in range(panels):
                here = placed[:, panel * width : (panel + 1) * width]
                canvas_ref[panel, at, :] = canvas_ref[panel, at, :] + here


def backward_kernel(
    half_side,
    scale_factor,
    corner_ref,
    sum_ref,
    other_ref,
    reward_ref,
    cover_ref,
    w_value_far,
    w_gate_far,
    w_down_far,
    w_out_ref,
    w_through,
    value_ref,
    gate_ref,
    left_ref,
    blended_ref,
    grad_value_ref,
    grad_gate_ref,
    grad_down_ref,
    small_ref,
    cot_wide,
    scaled_sum,
    mean_sum,
    active_sum,
    hidden_sum,
    patch_sum,
    spread,
    cot,
    d_active,
    d_both,
    active,
    along_scaled,
    grad_value,
    grad_gate,
    grad_down,
    w_value_ref,
    w_gate_ref,
    w_down_ref,
    mask,
    repeat,
    out_sems,
    in_sems,
):
    step = pl.program_id(0)
    model_width, features = w_out_ref.shape
    units = w_down_ref.shape[0]
    arrivals = [
        pltpu.make_async_copy(far, near, in_sems.at[index])
        for index, (far, near) in enumerate(
            (
                (w_value_far, w_value_ref),
                (w_gate_far, w_gate_ref),
                (w_down_far, w_down_ref),
            )
        )
    ]
    slabs = reward_ref.shape[0]
    panels, rows, width = sum_ref.shape
    slab_rows = rows // slabs
    tokens = half_side * half_side
    tiles_here = active.shape[1] // tokens

    @pl.when(step == 0)
    def _prepare():
        for copy in arrivals:
            copy.start()
        mask[...] = jnp.where(column_mask(features, half_side), 1.0, 0.0)
        repeat[...] = repeat_matrix(half_side)
        for panel in range(panels):
            lanes = slice(panel * width, (panel + 1) * width)
            cover = cover_ref[panel]
            blended = (sum_ref[panel] + other_ref[panel]) / cover
            blended_ref[:, lanes] = blended
            parts = []
            for slab in range(slabs):
                rewards = reward_ref[slab, :, lanes].astype(jnp.float32)[latent_rows(slab_rows) :]
                parts.append([rewards[term * slab_rows : (term + 1) * slab_rows] for term in range(4)])
            high, low, curved_high, curved_low = (
                jnp.concatenate([part[term] for part in parts], axis=0) for term in range(4)
            )
            reward = high + low
            curvature = curved_high + curved_low
            cot_wide[panel] = (
                ((reward - curvature * blended) / cover * scale_factor)
                .astype(jnp.bfloat16)
                .astype(jnp.float32)
            )
        for ref in (
            grad_value,
            grad_gate,
            scaled_sum,
            mean_sum,
            active_sum,
            hidden_sum,
            patch_sum,
        ):
            ref[...] = jnp.zeros_like(ref)

    for tile in range(tiles_here):
        here = slice(tile * tokens, (tile + 1) * tokens)
        spread[here, :] = spread_tile(
            cot_wide,
            corner_ref[step * tiles_here + tile, 0],
            corner_ref[step * tiles_here + tile, 1],
            half_side,
            features,
            mask,
            repeat,
        )
    cots = dot_lanes(fold_matrix(features, half_side), spread[...]).astype(jnp.bfloat16)
    cot[...] = cots
    d_active[...] = dot_plain(w_through[...], jnp.concatenate([cots, cots], axis=0))
    for tile in range(tiles_here):
        here = slice(tile * tokens, (tile + 1) * tokens)
        total = jnp.zeros((chunk_rows, tokens), jnp.float32)
        for at in range(0, units, chunk_rows):
            chunk = slice(at, at + chunk_rows)
            value = value_ref[chunk, here]
            gate = gate_ref[chunk, here]
            passed = d_active[chunk, here]
            normal = 0.5 * (1.0 + lax.erf(gate * root_half))
            gelu = gate * normal
            slope = normal + gate * jnp.exp(-0.5 * gate * gate) * inv_root_two_pi
            active[chunk, here] = (value * gelu).astype(jnp.bfloat16)
            product = passed * value
            d_both[chunk, here] = (passed * gelu).astype(jnp.bfloat16)
            d_both[units + at : units + at + chunk_rows, here] = (product * slope).astype(
                jnp.bfloat16
            )
            total = total + product * (gelu + slope * gate)
        along = jnp.sum(total, axis=0, keepdims=True) * (1.0 / model_width)
        scaled = left_ref[model_width : model_width + 2 * features, here].astype(jnp.float32)
        high, low = split_two((scaled[:features] + scaled[features:]) * along)
        along_scaled[:features, here] = high
        along_scaled[features:, here] = low
    left = left_ref[: model_width + 2 * features, : cot.shape[1]]
    grads = dot_lanes(left, d_both[...])
    grad_value[...] += grads[:model_width, :units]
    grad_gate[...] += grads[:model_width, units:]
    scaled_sum[...] += grads[model_width:]
    mean_sum[...] += dot_lanes(left[:model_width], along_scaled[...])
    active_sum[...] += dot_lanes(cot[...], active[...])
    peers = lax.axis_size("mp")
    for group in range(tiles_here // peers):
        own = token_at(group * peers + lax.axis_index("mp"), tokens)
        own_cot = cot[:, own]
        at = cot.shape[1] + group * tokens
        hidden_sum[...] += dot_lanes(own_cot, left_ref[:model_width, at : at + tokens])
        patch_sum[...] += dot_lanes(left_ref[model_width + 2 * features :, own], own_cot)

    @pl.when(step == pl.num_programs(0) - 1)
    def _finish():
        outs = [
            pltpu.make_async_copy(buffer, ref, out_sems.at[index])
            for index, (buffer, ref) in enumerate(
                (
                    (grad_value, grad_value_ref),
                    (grad_gate, grad_gate_ref),
                    (grad_down, grad_down_ref),
                )
            )
        ]
        outs[0].start()
        outs[1].start()
        active_two = jnp.concatenate(split_two(active_sum[...]), axis=0)
        mean_both = mean_sum[...].T
        w_out_two = jnp.concatenate([w_out_ref[...], w_out_ref[...]], axis=1)
        grad_down[...] = lax.dot_general(
            active_two, w_out_two, (((0,), (1,)), ((), ())), preferred_element_type=jnp.float32
        )
        outs[2].start()
        for copy in arrivals:
            copy.wait()
        through = dot_plain(active_two, w_down_ref[...])
        small_ref[features:] = hidden_sum[...] + through[:features] + through[features:]
        scaled_both = scaled_sum[:features] + scaled_sum[features:]
        scaled_two = jnp.concatenate(split_two(scaled_both), axis=0)
        moved = dot_lanes(scaled_two[:, :units], w_value_ref[...]) + dot_lanes(
            scaled_two[:, units:], w_gate_ref[...]
        )
        moved = moved[:features] + moved[features:]
        patch_two = jnp.concatenate(split_two(patch_sum[...]), axis=0)
        direct = dot_lanes(patch_two, w_out_ref[...])
        small_ref[:features] = (
            direct[:features]
            + direct[features:]
            + moved
            - jnp.mean(moved, axis=1, keepdims=True)
            - mean_both[:features]
            - mean_both[features:]
        )
        for copy in outs:
            copy.wait()


def whole(shape):
    return pl.BlockSpec(shape, lambda *_: (0,) * len(shape))


def over_mp(values):
    peers = lax.axis_size("mp")
    by = 1
    total = values
    other = None
    while by < peers:
        if other is not None:
            total = total + other
        other = lax.ppermute(total, "mp", [(i, i ^ by) for i in range(peers)])
        by *= 2
    return total, other


chunk_rows = 16


def some_tokens(height, tokens):
    return pl.BlockSpec((height, tokens), lambda step, *_: (0, step))


def step_tiles(tiles):
    peers = lax.axis_size("mp")
    return max(peers * count for count in (1,) if tiles % (peers * count) == 0)


def saved_arrays(tiles, token_count, features, model_width, units):
    every = tiles * token_count
    wide = every + every // lax.axis_size("mp")
    shapes = [
        ((units, every), jnp.float32),
        ((units, every), jnp.float32),
        ((model_width + 3 * features, wide), jnp.bfloat16),
    ]
    return [jax.ShapeDtypeStruct(shape, kind) for shape, kind in shapes]


def kernel_params(megabytes):
    return pltpu.CompilerParams(
        dimension_semantics=("arbitrary",), vmem_limit_bytes=megabytes * 2**20
    )


def run_forward(corners, latents, weights, half_side, rows):
    model_width, features = weights[1].shape
    units = weights[0].shape[0] // 2 - features
    tiles = corners.shape[0]
    cols = latents.shape[2]
    steps = tiles // step_tiles(tiles)
    tokens = step_tiles(tiles) * half_side * half_side
    width = half_side * features // 2
    f32 = jnp.float32
    b16 = jnp.bfloat16
    canvas = jax.ShapeDtypeStruct((cols // width, rows, width), f32)
    kept = saved_arrays(tiles, half_side * half_side, features, model_width, units)
    return pl.pallas_call(
        functools.partial(forward_kernel, half_side),
        out_shape=[canvas, canvas, *kept],
        grid_spec=pltpu.PrefetchScalarGridSpec(
            num_scalar_prefetch=1,
            grid=(steps,),
            in_specs=[whole(latents.shape)] + [whole(w.shape) for w in weights],
            out_specs=[whole(canvas.shape)] * 2 + [some_tokens(k.shape[0], k.shape[1] // steps) for k in kept],
            scratch_shapes=[
                pltpu.VMEM(canvas.shape, f32),
                pltpu.VMEM((tokens, 2 * width), b16),
                pltpu.VMEM((model_width, tokens), b16),
                pltpu.VMEM((units, tokens), b16),
                pltpu.VMEM((features, tokens), f32),
                pltpu.VMEM((half_side * half_side, 2 * width), f32),
                pltpu.VMEM((half_side * half_side, half_side), b16),
            ],
        ),
        compiler_params=kernel_params(52),
        name="forward",
    )(corners, latents, *weights)


def run_backward(corners, total, other, rewards, cover, weights, stored, half_side):
    model_width, features = weights[3].shape
    units = weights[0].shape[1]
    tiles = corners.shape[0]
    token_count = half_side * half_side
    steps = tiles // step_tiles(tiles)
    tokens = step_tiles(tiles) * token_count
    panels, rows, width = total.shape
    f32 = jnp.float32
    scale_factor = 16.0 / math.sqrt(tiles * token_count)
    return pl.pallas_call(
        functools.partial(backward_kernel, half_side, scale_factor),
        out_shape=[
            jax.ShapeDtypeStruct((rows, panels * width), f32),
            jax.ShapeDtypeStruct((model_width, units), f32),
            jax.ShapeDtypeStruct((model_width, units), f32),
            jax.ShapeDtypeStruct((units, model_width), f32),
            jax.ShapeDtypeStruct((2 * features, model_width), f32),
        ],
        grid_spec=pltpu.PrefetchScalarGridSpec(
            num_scalar_prefetch=1,
            grid=(steps,),
            in_specs=[whole(total.shape)] * 2
            + [whole(rewards.shape), whole(cover.shape)]
            + [pl.BlockSpec(memory_space=pl.ANY)] * 3
            + [whole(w.shape) for w in weights[3:]]
            + [some_tokens(k.shape[0], k.shape[1] // steps) for k in stored],
            out_specs=[
                whole((rows, panels * width)),
                pl.BlockSpec(memory_space=pl.ANY),
                pl.BlockSpec(memory_space=pl.ANY),
                pl.BlockSpec(memory_space=pl.ANY),
                whole((2 * features, model_width)),
            ],
            scratch_shapes=[
                pltpu.VMEM(total.shape, f32),
                pltpu.VMEM((2 * features, 2 * units), f32),
                pltpu.VMEM((model_width, 2 * features), f32),
                pltpu.VMEM((features, units), f32),
                pltpu.VMEM((features, model_width), f32),
                pltpu.VMEM((features, features), f32),
                pltpu.VMEM((tokens, 2 * width), jnp.bfloat16),
                pltpu.VMEM((features, tokens), jnp.bfloat16),
                pltpu.VMEM((units, tokens), f32),
                pltpu.VMEM((2 * units, tokens), jnp.bfloat16),
                pltpu.VMEM((units, tokens), jnp.bfloat16),
                pltpu.VMEM((2 * features, tokens), jnp.bfloat16),
                pltpu.VMEM((model_width, units), f32),
                pltpu.VMEM((model_width, units), f32),
                pltpu.VMEM((units, model_width), f32),
                *[pltpu.VMEM(w.shape, w.dtype) for w in weights[:3]],
                pltpu.VMEM((half_side * half_side, 2 * width), f32),
                pltpu.VMEM((half_side * half_side, half_side), jnp.bfloat16),
                pltpu.SemaphoreType.DMA((3,)),
                pltpu.SemaphoreType.DMA((3,)),
            ],
        ),
        compiler_params=kernel_params(52),
        name="backward",
    )(corners, total, other, rewards, cover, *weights, *stored)


def pack_kernel(offset_ref, latent_ref, reward_ref, curvature_ref, packed_ref):
    copies, unused, cols = packed_ref.shape
    packed_rows = latent_rows(latent_ref.shape[0])
    slab_rows = latent_ref.shape[0]
    tiles_here = offset_ref.shape[0]
    lane = lax.broadcasted_iota(jnp.int32, (packed_rows - slab_rows, cols), 1)
    digits = jnp.zeros(lane.shape, jnp.int32)
    for tile in range(tiles_here):
        for axis in range(2):
            value = offset_ref[tile, axis]
            at = 2 * tile + axis
            digits = jnp.where(lane == at, value // 256, digits)
            digits = jnp.where(lane == 2 * tiles_here + at, value % 256, digits)
    rewards = split_two(reward_ref[...]) + split_two(curvature_ref[...])
    packed = jnp.concatenate(
        [latent_ref[...].astype(jnp.float32), digits.astype(jnp.float32)]
        + [part.astype(jnp.float32) for part in rewards],
        axis=0,
    ).astype(packed_ref.dtype)
    for copy in range(copies):
        packed_ref[copy, : packed.shape[0]] = packed


def latent_rows(slab_rows):
    return -(-(slab_rows + 1) // 16) * 16


def run_pack(latent, reward_grad, curvature, offsets, slabs):
    slab_rows, cols = latent.shape
    packed_rows = latent_rows(slab_rows) + 4 * slab_rows
    vmem = pl.BlockSpec(memory_space=pltpu.VMEM)
    return pl.pallas_call(
        pack_kernel,
        out_shape=jax.ShapeDtypeStruct((slabs, packed_rows, cols), latent.dtype),
        in_specs=[pl.BlockSpec(memory_space=pltpu.SMEM), vmem, vmem, vmem],
        out_specs=vmem,
        name="pack",
    )(offsets, latent, reward_grad, curvature)


def per_device_replicated(
    latent, reward_grad, curvature, offsets, counts, w_in, w_value, w_gate, w_down, w_out
):
    features, model_width = w_in.shape
    units = w_value.shape[1]
    half_side = S // 2
    token_count = half_side * half_side
    slab_rows, cols = latent.shape
    tiles_here = offsets.shape[0]
    slabs = lax.axis_size("tile")
    tiles = tiles_here * slabs
    rows = slab_rows * slabs
    packed = run_pack(latent, reward_grad, curvature, offsets, slabs)
    latents = lax.all_to_all(packed, "tile", 0, 0)
    digits = latents[:, slab_rows, : 4 * tiles_here].astype(jnp.int32)
    digits = digits.reshape(slabs, 2, tiles_here, 2)
    corners = (digits[:, 0] * 256 + digits[:, 1]).reshape(tiles, 2)

    packed_weights, w_through = run_weights((w_in, w_value, w_gate, w_down, w_out), half_side)
    sums, cover, *stored = run_forward(
        corners, latents, (packed_weights, w_out), half_side, rows
    )
    weights = (w_value, w_gate, w_down, w_out, w_through)
    total, other = over_mp(sums)
    blended, grad_value, grad_gate, grad_down, small = run_backward(
        corners, total, other, latents, cover, weights, stored, half_side
    )
    own = lax.dynamic_slice_in_dim(blended, lax.axis_index("tile") * slab_rows, slab_rows, 0)
    mine, theirs = over_mp(small)
    small = mine + theirs
    return (own, small[:features], grad_value, grad_gate, grad_down, small[features:].T)


def per_device(
    latent, reward_grad, curvature, offsets, counts, w_in, w_value, w_gate, w_down, w_out
):
    tiles = offsets.shape[0] * lax.axis_size("tile")
    stored_bytes = tiles * (S // 2) ** 2 * (8 * w_value.shape[1] + 3 * w_in.shape[1])
    peers = lax.axis_size("mp")
    pairs = w_in.shape[1] <= 2 * w_value.shape[1] and peers > 1 and peers & (peers - 1) == 0 and tiles % peers == 0
    replicate = pairs and stored_bytes <= 40 * 2**20
    plan = per_device_replicated if replicate else per_device_sharded
    return plan(
        latent, reward_grad, curvature, offsets, counts, w_in, w_value, w_gate, w_down, w_out
    )


def solution(mesh):
    return jax.shard_map(
        per_device,
        mesh=mesh,
        in_specs=(
            P("tile", None),
            P("tile", None),
            P("tile", None),
            P("tile", None),
            P("tile", None),
            P(),
            P(None, "mp"),
            P(None, "mp"),
            P("mp", None),
            P(),
        ),
        out_specs=(P("tile", None), P(), P(None, "mp"), P(None, "mp"), P("mp", None), P()),
        check_vma=False,
    )
```

```python
import functools
import math

import jax
import jax.numpy as jnp
from jax import lax
from jax.experimental import pallas as pl
from jax.experimental.pallas import tpu as pltpu
from jax.sharding import PartitionSpec as P

S = 32
SPACING = 24


layer_eps = 1e-05
root_half = 0.7071067811865476
inv_root_two_pi = 0.3989422804014327
highest = lax.Precision.HIGHEST


def passed_along(shard, axis, by):
    peers = lax.axis_size(axis)
    pairs = [(i, i + by) for i in range(peers) if 0 <= i + by < peers]
    return lax.ppermute(shard, axis, pairs)


def gelu_value(inputs):
    return 0.5 * inputs * (1.0 + lax.erf(inputs * root_half))


def gelu_slope(inputs):
    return (
        0.5 * (1.0 + lax.erf(inputs * root_half))
        + inputs * jnp.exp(-0.5 * inputs * inputs) * inv_root_two_pi
    )


def patchify(cropped, channels):
    half_side = cropped.shape[0] // 2
    return (
        cropped.reshape(half_side, 2, half_side, 2 * channels)
        .transpose(0, 2, 1, 3)
        .reshape(half_side * half_side, 4 * channels)
    )


def unpatch(tokens, tile_side, channels):
    half_side = tile_side // 2
    token_rows = tokens.shape[0] // half_side
    return (
        tokens.reshape(token_rows, half_side, 2, 2 * channels)
        .transpose(0, 2, 1, 3)
        .reshape(2 * token_rows, tile_side * channels)
    )


def layer_norm(hidden):
    values = hidden.astype(jnp.float32)
    center = values - jnp.mean(values, axis=-1, keepdims=True)
    variance = jnp.mean(center * center, axis=-1, keepdims=True)
    inv_scale = lax.rsqrt(variance + layer_eps)
    return (center * inv_scale, inv_scale)


def norm_backward(normed, inv_scale, d_unit):
    centered = d_unit - jnp.mean(d_unit, axis=-1, keepdims=True)
    return inv_scale * (centered - normed * jnp.mean(d_unit * normed, axis=-1, keepdims=True))


def contract_rows(left, right):
    return lax.dot_general(
        left, right, (((0,), (0,)), ((), ())), preferred_element_type=jnp.float32
    )


def contract_rows_exact(left, right):
    return lax.dot_general(
        left, right, (((0,), (0,)), ((), ())), precision=highest, preferred_element_type=jnp.float32
    )


def contract_cols(left, right):
    return lax.dot_general(
        left, right, (((1,), (1,)), ((), ())), preferred_element_type=jnp.float32
    )


def crop_tiles(source, corners, row_base, tile_side, channels):

    def crop_one(corner):
        cropped = lax.dynamic_slice(
            source, (corner[0] - row_base, corner[1] * channels), (tile_side, tile_side * channels)
        )
        return patchify(cropped, channels)

    return jax.vmap(crop_one)(corners)


def place_tiles(canvas, pieces, corners, row_shift, channels):
    piece_rows = pieces.shape[1]
    piece_cols = pieces.shape[2]

    def add_tile(tile_index, current):
        corner = corners[tile_index]
        start_row = corner[0] + row_shift
        start_col = corner[1] * channels
        existing = lax.dynamic_slice(current, (start_row, start_col), (piece_rows, piece_cols))
        return lax.dynamic_update_slice(
            current, existing + pieces[tile_index], (start_row, start_col)
        )

    return lax.fori_loop(0, pieces.shape[0], add_tile, canvas)


def per_device_sharded(
    latent, reward_grad, curvature, offsets, counts, w_in, w_value, w_gate, w_down, w_out
):
    channels = w_in.shape[0] // 4
    model_width = w_in.shape[1]
    tile_side = S
    half_side = tile_side // 2
    token_count = half_side * half_side
    tiles_here = offsets.shape[0]
    slab_rows = latent.shape[0]
    canvas_cols = latent.shape[1]
    tile_devices = lax.axis_size("tile")
    model_devices = lax.axis_size("mp")
    tile_pos = lax.axis_index("tile")
    model_pos = lax.axis_index("mp")
    share_tokens = token_count // model_devices
    share_pixels = tile_side // model_devices
    scale_factor = 16.0 / math.sqrt(tiles_here * tile_devices * token_count)
    w_out_wide = w_out.astype(jnp.float32)
    cover_count = jnp.repeat(counts, channels, axis=1).astype(jnp.float32)
    placed_row = model_pos * share_pixels
    every_corner = lax.all_gather(offsets, "tile", axis=0, tiled=True)
    grid_cols = canvas_cols // (channels * SPACING)
    grid_cells = (every_corner[:, 0] + SPACING // 2) // SPACING * grid_cols + (
        every_corner[:, 1] + SPACING // 2
    ) // SPACING
    wanted = (
        tile_pos // 2 * grid_cols
        + tile_pos % 2 * tiles_here
        + jnp.arange(tiles_here, dtype=jnp.int32)
    )
    matched = (grid_cells[None, :] == wanted[:, None]).astype(jnp.int32)
    corners = jnp.sum(matched[:, :, None] * every_corner[None, :, :], axis=1)
    row_base = (tile_pos - 2) * slab_rows
    latent_parts = []
    for shift_by in (2, 1, 0, -1, -2):
        if shift_by == 0:
            latent_parts.append(latent)
        else:
            latent_parts.append(passed_along(latent, "tile", shift_by))
    latent_source = jnp.concatenate(latent_parts, axis=0)
    patches = crop_tiles(latent_source, corners, row_base, tile_side, channels)
    flat_patches = jnp.transpose(patches, (1, 0, 2)).reshape(token_count * tiles_here, 4 * channels)
    hidden = jnp.dot(flat_patches, w_in, preferred_element_type=jnp.float32).astype(jnp.bfloat16)
    normed, inv_scale = layer_norm(hidden)
    unit_in = normed.astype(jnp.bfloat16)
    value_proj = jnp.dot(unit_in, w_value, preferred_element_type=jnp.float32)
    gate_proj = jnp.dot(unit_in, w_gate, preferred_element_type=jnp.float32)
    active = (value_proj * gelu_value(gate_proj)).astype(jnp.bfloat16)
    active_grid = active.reshape(token_count, tiles_here, active.shape[1])

    def take_share(values):
        grid = values.reshape(token_count, tiles_here, values.shape[-1])
        picked = lax.dynamic_slice_in_dim(grid, model_pos * share_tokens, share_tokens, 0)
        return picked.reshape(share_tokens * tiles_here, values.shape[-1])

    hidden_share = take_share(hidden)
    row_block = active_grid.reshape(
        lax.axis_size("mp") * share_tokens * tiles_here, active_grid.shape[2]
    )
    ff_share = lax.psum_scatter(
        jnp.dot(row_block, w_down, preferred_element_type=jnp.float32).reshape(
            lax.axis_size("mp") * share_tokens, tiles_here, model_width
        ),
        "mp",
        scatter_dimension=0,
        tiled=True,
    ).reshape(share_tokens * tiles_here, model_width)
    noise_share = jnp.dot(hidden_share, w_out, preferred_element_type=jnp.float32) + jnp.dot(
        ff_share, w_out_wide, precision=highest, preferred_element_type=jnp.float32
    )
    noise_tiles = jnp.transpose(
        noise_share.reshape(share_tokens, tiles_here, w_out.shape[1]), (1, 0, 2)
    )

    def unpatch_share(tokens):
        return unpatch(tokens, tile_side, channels)

    noise_pieces = jax.vmap(unpatch_share)(noise_tiles)
    window_term = place_tiles(
        jnp.zeros((5 * slab_rows, canvas_cols), jnp.float32),
        noise_pieces,
        corners,
        placed_row - row_base,
        channels,
    )
    slab_sum = window_term[2 * slab_rows : 3 * slab_rows]
    for shift_by in (-2, -1, 1, 2):
        outgoing = window_term[(shift_by + 2) * slab_rows : (shift_by + 3) * slab_rows]
        slab_sum = slab_sum + passed_along(outgoing, "tile", shift_by)
    blend_total = lax.psum(slab_sum, "mp")
    blended = blend_total / cover_count
    cotangent = ((reward_grad - curvature * blended) / cover_count * scale_factor).astype(
        jnp.bfloat16
    )
    cot_parts = []
    for shift_by in (2, 1, 0, -1, -2):
        if shift_by == 0:
            cot_parts.append(cotangent)
        else:
            cot_parts.append(passed_along(cotangent, "tile", shift_by))
    cot_source = jnp.concatenate(cot_parts, axis=0)
    cot_patches = crop_tiles(cot_source, corners, row_base, tile_side, channels)
    cot_flat = jnp.transpose(cot_patches, (1, 0, 2)).reshape(token_count * tiles_here, 4 * channels)
    cot_share = take_share(cot_flat)
    d_feat = contract_cols(cot_flat, w_out)
    d_feat_b = d_feat.astype(jnp.bfloat16)
    d_active = contract_cols(d_feat_b, w_down)
    down_term = contract_rows(active, d_feat_b)
    d_value = (d_active * gelu_value(gate_proj)).astype(jnp.bfloat16)
    d_gate = (d_active * value_proj * gelu_slope(gate_proj)).astype(jnp.bfloat16)
    value_term = contract_rows(unit_in, d_value)
    gate_term = contract_rows(unit_in, d_gate)
    d_value_grid = d_value.reshape(token_count, tiles_here, d_value.shape[1])
    d_gate_grid = d_gate.reshape(token_count, tiles_here, d_gate.shape[1])
    value_block = d_value_grid.reshape(
        share_tokens * lax.axis_size("mp") * tiles_here, d_value.shape[1]
    )
    gate_block = d_gate_grid.reshape(
        share_tokens * lax.axis_size("mp") * tiles_here, d_gate.shape[1]
    )
    summed = contract_cols(value_block, w_value) + contract_cols(gate_block, w_gate)
    d_unit_share = (
        lax.psum_scatter(
            summed.reshape(share_tokens * lax.axis_size("mp"), tiles_here, model_width).astype(
                jnp.bfloat16
            ),
            "mp",
            scatter_dimension=0,
            tiled=True,
        )
        .astype(jnp.float32)
        .reshape(share_tokens * tiles_here, model_width)
    )
    d_hidden = (
        take_share(d_feat) + norm_backward(take_share(normed), take_share(inv_scale), d_unit_share)
    ).astype(jnp.bfloat16)
    in_term = contract_rows(take_share(flat_patches), d_hidden)
    out_term = contract_rows(hidden_share, cot_share) + contract_rows_exact(
        ff_share, cot_share.astype(jnp.float32)
    )
    grad_in, grad_out = lax.psum((in_term, out_term), ("tile", "mp"))
    grad_value, grad_gate, grad_down = lax.psum((value_term, gate_term, down_term), "tile")
    return (blended, grad_in, grad_value, grad_gate, grad_down, grad_out)


def dot_lanes(left, right):
    return lax.dot_general(
        left, right, (((1,), (1,)), ((), ())), preferred_element_type=jnp.float32
    )


def dot_plain(left, right):
    return lax.dot_general(
        left, right, (((1,), (0,)), ((), ())), preferred_element_type=jnp.float32
    )


def split_two(values):
    high = values.astype(jnp.bfloat16)
    low = (values - high.astype(jnp.float32)).astype(jnp.bfloat16)
    return high, low


def split_three(values):
    high = values.astype(jnp.bfloat16)
    rest = values - high.astype(jnp.float32)
    middle = rest.astype(jnp.bfloat16)
    low = (rest - middle.astype(jnp.float32)).astype(jnp.bfloat16)
    return high, middle, low


def fold_matrix(features, half_side):
    run = features // 2
    wide = 2 * half_side * run
    feature = lax.broadcasted_iota(jnp.int32, (features, wide), 0)
    place = lax.broadcasted_iota(jnp.int32, (features, wide), 1)
    own = place // (half_side * run) * run + place % run
    return jnp.where(feature == own, 1.0, 0.0).astype(jnp.bfloat16)


def column_mask(features, half_side):
    run = features // 2
    wide = 2 * half_side * run
    token = lax.broadcasted_iota(jnp.int32, (half_side * half_side, wide), 0)
    place = lax.broadcasted_iota(jnp.int32, (half_side * half_side, wide), 1)
    return token % half_side == place // run % half_side


def repeat_matrix(half_side):
    token = lax.broadcasted_iota(jnp.int32, (half_side * half_side, half_side), 0)
    patch_row = lax.broadcasted_iota(jnp.int32, (half_side * half_side, half_side), 1)
    return jnp.where(token // half_side == patch_row, 1.0, 0.0).astype(jnp.bfloat16)


def spread_tile(canvas_ref, row, col, half_side, features, mask, repeat):
    run = features // 2
    width = half_side * run
    panels = canvas_ref.shape[0]
    cols = panels * width
    lanes = col * run // 2
    halves = []
    for parity in range(2):
        at = pl.ds(row + parity, half_side, stride=2)
        rows = jnp.concatenate([canvas_ref[panel, at, :] for panel in range(panels)], axis=1)
        rolled = pltpu.roll(rows, lax.rem(cols - lanes, cols), 1)
        halves.append(rolled[:, :width])
    pair = jnp.concatenate(halves, axis=1).astype(jnp.bfloat16)
    return (dot_plain(repeat[...], pair) * mask[...]).astype(jnp.bfloat16)


def token_at(tile, tokens):
    return pl.ds(pl.multiple_of(tile * tokens, tokens), tokens)


def weight_kernel(
    half_side,
    w_in_ref,
    w_value_ref,
    w_gate_ref,
    w_down_ref,
    w_out_ref,
    packed,
    w_through,
):
    features, model_width = w_in_ref.shape
    units = w_value_ref.shape[1]
    fold = fold_matrix(features, half_side)
    packed[...] = jnp.zeros_like(packed)
    packed[:model_width, model_width:] = lax.dot_general(
        w_in_ref[...], fold, (((0,), (0,)), ((), ())), preferred_element_type=jnp.float32
    ).astype(jnp.bfloat16)
    packed[:units, :model_width] = w_value_ref[...].T
    packed[units : 2 * units, :model_width] = w_gate_ref[...].T
    both = dot_plain(w_down_ref[...], w_out_ref[...])
    w_through[...] = jnp.concatenate(split_two(both), axis=1)
    packed[2 * units :, :units] = jnp.concatenate(split_two(both.T), axis=0)


def run_weights(weights, half_side):
    features, model_width = weights[0].shape
    units = weights[1].shape[1]
    width = half_side * features // 2
    vmem = pl.BlockSpec(memory_space=pltpu.VMEM)
    shapes = [
        (2 * units + 2 * features, max(model_width + 2 * width, units)),
        (units, 2 * features),
    ]
    return pl.pallas_call(
        functools.partial(weight_kernel, half_side),
        out_shape=[jax.ShapeDtypeStruct(shape, jnp.bfloat16) for shape in shapes],
        in_specs=[vmem] * len(weights),
        out_specs=[vmem] * len(shapes),
        name="weights",
    )(*weights)


def forward_kernel(
    half_side,
    corner_ref,
    latent_ref,
    weights_ref,
    w_out_ref,
    canvas_ref,
    cover_ref,
    value_ref,
    gate_ref,
    left_ref,
    latent_wide,
    spread,
    hidden_all,
    active,
    noise,
    mask,
    repeat,
    canvas_sum,
):
    step = pl.program_id(0)
    model_width, features = w_out_ref.shape
    units = weights_ref.shape[0] // 2 - features
    slabs, slab_rows, cols = latent_ref.shape
    panels, rows, width = canvas_ref.shape
    own_rows = rows // slabs
    tokens = half_side * half_side
    tiles_here = active.shape[1] // tokens

    @pl.when(step == 0)
    def _prepare():
        for slab in range(slabs):
            own = latent_ref[slab, : latent_rows(own_rows)].astype(jnp.float32)[:own_rows]
            for panel in range(panels):
                latent_wide[panel, slab * own_rows : (slab + 1) * own_rows, :] = own[
                    :, panel * width : (panel + 1) * width
                ]
        canvas_sum[...] = jnp.zeros_like(canvas_sum)
        cover_ref[...] = jnp.zeros_like(cover_ref)
        noise[...] = jnp.zeros_like(noise)
        mask[...] = jnp.where(column_mask(features, half_side), 1.0, 0.0)
        repeat[...] = repeat_matrix(half_side)

    def corners_of(group):
        return [
            (corner_ref[group * tiles_here + tile, 0], corner_ref[group * tiles_here + tile, 1])
            for tile in range(tiles_here)
        ]

    corners = corners_of(step)
    add_noise(
        canvas_sum, noise[...], corners_of(jnp.maximum(step - 1, 0)), half_side, features, mask
    )
    fold = fold_matrix(features, half_side)
    for tile, (row, col) in enumerate(corners):
        here = slice(tile * tokens, (tile + 1) * tokens)
        spread[here, :] = spread_tile(
            latent_wide, row, col, half_side, features, mask, repeat
        )
    patch_rows = slice(model_width + 2 * features, None)
    left_ref[patch_rows, : active.shape[1]] = dot_lanes(fold, spread[...]).astype(jnp.bfloat16)
    hidden_all[...] = dot_lanes(weights_ref[:model_width, model_width:], spread[...]).astype(jnp.bfloat16)
    for tile in range(tiles_here):
        here = slice(tile * tokens, (tile + 1) * tokens)
        base = hidden_all[:chunk_rows, here].astype(jnp.float32)[:1]
        total = jnp.zeros((chunk_rows, tokens), jnp.float32)
        squares = jnp.zeros((chunk_rows, tokens), jnp.float32)
        for at in range(0, model_width, chunk_rows):
            moved = hidden_all[at : at + chunk_rows, here].astype(jnp.float32) - base
            total = total + moved
            squares = squares + moved * moved
        offset = jnp.sum(total, axis=0, keepdims=True) * (1.0 / model_width)
        mean = base + offset
        variance = jnp.sum(squares, axis=0, keepdims=True) * (1.0 / model_width) - offset * offset
        inv_scale = lax.rsqrt(variance + layer_eps)
        for at in range(0, model_width, chunk_rows):
            center = hidden_all[at : at + chunk_rows, here].astype(jnp.float32) - mean
            left_ref[at : at + chunk_rows, here] = (center * inv_scale).astype(jnp.bfloat16)
        high, low = split_two(left_ref[patch_rows, here].astype(jnp.float32) * inv_scale)
        left_ref[model_width : model_width + features, here] = high
        left_ref[model_width + features : model_width + 2 * features, here] = low
    for tile in range(tiles_here):
        here = slice(tile * tokens, (tile + 1) * tokens)
        unit = left_ref[:model_width, here]
        value_ref[:, here] = dot_plain(weights_ref[:units, :model_width], unit)
        gate_ref[:, here] = dot_plain(weights_ref[units : 2 * units, :model_width], unit)
        for at in range(0, units, chunk_rows):
            value = value_ref[at : at + chunk_rows, here]
            gate = gate_ref[at : at + chunk_rows, here]
            normal = 0.5 * lax.erf(gate * root_half) + 0.5
            active[at : at + chunk_rows, here] = (value * (gate * normal)).astype(jnp.bfloat16)
    parts = dot_plain(weights_ref[2 * units :, :units], active[...])
    noise[...] = parts[:features] + parts[features:]
    peers = lax.axis_size("mp")
    for group in range(tiles_here // peers):
        own = token_at(group * peers + lax.axis_index("mp"), tokens)
        hidden = hidden_all[:, own]
        at = active.shape[1] + group * tokens
        left_ref[:model_width, at : at + tokens] = hidden
        noise[:, own] = noise[:, own] + lax.dot_general(
            w_out_ref[...], hidden, (((0,), (0,)), ((), ())), preferred_element_type=jnp.float32
        )

    @pl.when(step == pl.num_programs(0) - 1)
    def _last():
        add_noise(canvas_sum, noise[...], corners, half_side, features, mask)
        canvas_ref[...] = canvas_sum[:, :rows, :]

    shape = cover_ref.shape
    row_at = lax.broadcasted_iota(jnp.int32, shape, 1)
    col_at = lax.broadcasted_iota(jnp.int32, shape, 0) * width + lax.broadcasted_iota(
        jnp.int32, shape, 2
    )
    cover = cover_ref[...]
    for row, col in corners:
        left = col * (features // 4)
        inside = (
            (row_at >= row)
            & (row_at < row + 2 * half_side)
            & (col_at >= left)
            & (col_at < left + half_side * features // 2)
        )
        cover = cover + jnp.where(inside, 1.0, 0.0)
    cover_ref[...] = cover


def add_noise(canvas_ref, noise, corners, half_side, features, mask):
    run = features // 2
    width = half_side * run
    panels = canvas_ref.shape[0]
    fold = fold_matrix(features, half_side)
    tall = lax.dot_general(
        jnp.concatenate(split_three(noise), axis=0),
        jnp.concatenate([fold, fold, fold], axis=0),
        (((0,), (0,)), ((), ())),
        preferred_element_type=jnp.float32,
    )
    tall = tall.reshape(len(corners), half_side * half_side, 2 * width)
    kept = tall * mask[...][None]
    pairs = jnp.sum(kept.reshape(len(corners), half_side, half_side, 2 * width), axis=2)
    blank = jnp.zeros((half_side, (panels - 1) * width), jnp.float32)
    for tile, (row, col) in enumerate(corners):
        for parity in range(2):
            own = pairs[tile, :, parity * width : (parity + 1) * width]
            placed = pltpu.roll(jnp.concatenate([own, blank], axis=1), col * run // 2, 1)
            at = pl.ds(row + parity, half_side, stride=2)
            for panel in range(panels):
                here = placed[:, panel * width : (panel + 1) * width]
                canvas_ref[panel, at, :] = canvas_ref[panel, at, :] + here


def backward_kernel(
    half_side,
    scale_factor,
    corner_ref,
    sum_ref,
    other_ref,
    reward_ref,
    cover_ref,
    w_value_far,
    w_gate_far,
    w_down_far,
    w_out_ref,
    w_through,
    value_ref,
    gate_ref,
    left_ref,
    blended_ref,
    grad_value_ref,
    grad_gate_ref,
    grad_down_ref,
    small_ref,
    cot_wide,
    scaled_sum,
    mean_sum,
    active_sum,
    hidden_sum,
    patch_sum,
    spread,
    cot,
    d_active,
    d_both,
    active,
    along_scaled,
    grad_value,
    grad_gate,
    grad_down,
    w_value_ref,
    w_gate_ref,
    w_down_ref,
    mask,
    repeat,
    out_sems,
    in_sems,
):
    step = pl.program_id(0)
    model_width, features = w_out_ref.shape
    units = w_down_ref.shape[0]
    arrivals = [
        pltpu.make_async_copy(far, near, in_sems.at[index])
        for index, (far, near) in enumerate(
            (
                (w_value_far, w_value_ref),
                (w_gate_far, w_gate_ref),
                (w_down_far, w_down_ref),
            )
        )
    ]
    slabs = reward_ref.shape[0]
    panels, rows, width = sum_ref.shape
    slab_rows = rows // slabs
    tokens = half_side * half_side
    tiles_here = active.shape[1] // tokens

    @pl.when(step == 0)
    def _prepare():
        for copy in arrivals:
            copy.start()
        mask[...] = jnp.where(column_mask(features, half_side), 1.0, 0.0)
        repeat[...] = repeat_matrix(half_side)
        for panel in range(panels):
            lanes = slice(panel * width, (panel + 1) * width)
            cover = cover_ref[panel]
            blended = (sum_ref[panel] + other_ref[panel]) / cover
            blended_ref[:, lanes] = blended
            parts = []
            for slab in range(slabs):
                rewards = reward_ref[slab, :, lanes].astype(jnp.float32)[latent_rows(slab_rows) :]
                parts.append([rewards[term * slab_rows : (term + 1) * slab_rows] for term in range(4)])
            high, low, curved_high, curved_low = (
                jnp.concatenate([part[term] for part in parts], axis=0) for term in range(4)
            )
            reward = high + low
            curvature = curved_high + curved_low
            cot_wide[panel, :rows] = (
                ((reward - curvature * blended) / cover * scale_factor)
                .astype(jnp.bfloat16)
                .astype(jnp.float32)
            )
        for ref in (
            grad_value,
            grad_gate,
            scaled_sum,
            mean_sum,
            active_sum,
            hidden_sum,
            patch_sum,
        ):
            ref[...] = jnp.zeros_like(ref)

    for tile in range(tiles_here):
        here = slice(tile * tokens, (tile + 1) * tokens)
        spread[here, :] = spread_tile(
            cot_wide,
            corner_ref[step * tiles_here + tile, 0],
            corner_ref[step * tiles_here + tile, 1],
            half_side,
            features,
            mask,
            repeat,
        )
    cots = dot_lanes(fold_matrix(features, half_side), spread[...]).astype(jnp.bfloat16)
    cot[...] = cots
    d_active[...] = dot_plain(w_through[...], jnp.concatenate([cots, cots], axis=0))
    for tile in range(tiles_here):
        here = slice(tile * tokens, (tile + 1) * tokens)
        total = jnp.zeros((chunk_rows, tokens), jnp.float32)
        for at in range(0, units, chunk_rows):
            chunk = slice(at, at + chunk_rows)
            value = value_ref[chunk, here]
            gate = gate_ref[chunk, here]
            passed = d_active[chunk, here]
            normal = 0.5 * (1.0 + lax.erf(gate * root_half))
            gelu = gate * normal
            slope = normal + gate * jnp.exp(-0.5 * gate * gate) * inv_root_two_pi
            active[chunk, here] = (value * gelu).astype(jnp.bfloat16)
            product = passed * value
            d_both[chunk, here] = (passed * gelu).astype(jnp.bfloat16)
            d_both[units + at : units + at + chunk_rows, here] = (product * slope).astype(
                jnp.bfloat16
            )
            total = total + product * (gelu + slope * gate)
        along = jnp.sum(total, axis=0, keepdims=True) * (1.0 / model_width)
        scaled = left_ref[model_width : model_width + 2 * features, here].astype(jnp.float32)
        high, low = split_two((scaled[:features] + scaled[features:]) * along)
        along_scaled[:features, here] = high
        along_scaled[features:, here] = low
    left = left_ref[: model_width + 2 * features, : cot.shape[1]]
    grads = dot_lanes(left, d_both[...])
    grad_value[...] += grads[:model_width, :units]
    grad_gate[...] += grads[:model_width, units:]
    scaled_sum[...] += grads[model_width:]
    mean_sum[...] += dot_lanes(left[:model_width], along_scaled[...])
    active_sum[...] += dot_lanes(cot[...], active[...])
    peers = lax.axis_size("mp")
    for group in range(tiles_here // peers):
        own = token_at(group * peers + lax.axis_index("mp"), tokens)
        own_cot = cot[:, own]
        at = cot.shape[1] + group * tokens
        hidden_sum[...] += dot_lanes(own_cot, left_ref[:model_width, at : at + tokens])
        patch_sum[...] += dot_lanes(left_ref[model_width + 2 * features :, own], own_cot)

    @pl.when(step == pl.num_programs(0) - 1)
    def _finish():
        outs = [
            pltpu.make_async_copy(buffer, ref, out_sems.at[index])
            for index, (buffer, ref) in enumerate(
                (
                    (grad_value, grad_value_ref),
                    (grad_gate, grad_gate_ref),
                    (grad_down, grad_down_ref),
                )
            )
        ]
        outs[0].start()
        outs[1].start()
        active_two = jnp.concatenate(split_two(active_sum[...]), axis=0)
        mean_both = mean_sum[...].T
        w_out_two = jnp.concatenate([w_out_ref[...], w_out_ref[...]], axis=1)
        grad_down[...] = lax.dot_general(
            active_two, w_out_two, (((0,), (1,)), ((), ())), preferred_element_type=jnp.float32
        )
        outs[2].start()
        for copy in arrivals:
            copy.wait()
        through = dot_plain(active_two, w_down_ref[...])
        small_ref[features:] = hidden_sum[...] + through[:features] + through[features:]
        scaled_both = scaled_sum[:features] + scaled_sum[features:]
        scaled_two = jnp.concatenate(split_two(scaled_both), axis=0)
        moved = dot_lanes(scaled_two[:, :units], w_value_ref[...]) + dot_lanes(
            scaled_two[:, units:], w_gate_ref[...]
        )
        moved = moved[:features] + moved[features:]
        patch_two = jnp.concatenate(split_two(patch_sum[...]), axis=0)
        direct = dot_lanes(patch_two, w_out_ref[...])
        small_ref[:features] = (
            direct[:features]
            + direct[features:]
            + moved
            - jnp.mean(moved, axis=1, keepdims=True)
            - mean_both[:features]
            - mean_both[features:]
        )
        for copy in outs:
            copy.wait()


def whole(shape):
    return pl.BlockSpec(shape, lambda *_: (0,) * len(shape))


def over_mp(values):
    peers = lax.axis_size("mp")
    by = 1
    total = values
    other = None
    while by < peers:
        if other is not None:
            total = total + other
        other = lax.ppermute(total, "mp", [(i, i ^ by) for i in range(peers)])
        by *= 2
    return total, other


chunk_rows = 16


def some_tokens(height, tokens):
    return pl.BlockSpec((height, tokens), lambda step, *_: (0, step))


def step_tiles(tiles):
    peers = lax.axis_size("mp")
    return max(peers * count for count in (1,) if tiles % (peers * count) == 0)


def saved_arrays(tiles, token_count, features, model_width, units):
    every = tiles * token_count
    wide = every + every // lax.axis_size("mp")
    shapes = [
        ((units, every), jnp.float32),
        ((units, every), jnp.float32),
        ((model_width + 3 * features, wide), jnp.bfloat16),
    ]
    return [jax.ShapeDtypeStruct(shape, kind) for shape, kind in shapes]


def kernel_params(megabytes):
    return pltpu.CompilerParams(
        dimension_semantics=("arbitrary",), vmem_limit_bytes=megabytes * 2**20
    )


def run_forward(corners, latents, weights, half_side, rows):
    model_width, features = weights[1].shape
    units = weights[0].shape[0] // 2 - features
    tiles = corners.shape[0]
    cols = latents.shape[2]
    steps = tiles // step_tiles(tiles)
    tokens = step_tiles(tiles) * half_side * half_side
    width = half_side * features // 2
    f32 = jnp.float32
    b16 = jnp.bfloat16
    canvas = jax.ShapeDtypeStruct((cols // width, rows, width), f32)
    kept = saved_arrays(tiles, half_side * half_side, features, model_width, units)
    return pl.pallas_call(
        functools.partial(forward_kernel, half_side),
        out_shape=[canvas, canvas, *kept],
        grid_spec=pltpu.PrefetchScalarGridSpec(
            num_scalar_prefetch=1,
            grid=(steps,),
            in_specs=[whole(latents.shape)] + [whole(w.shape) for w in weights],
            out_specs=[whole(canvas.shape)] * 2 + [some_tokens(k.shape[0], k.shape[1] // steps) for k in kept],
            scratch_shapes=[
                pltpu.VMEM((cols // width, rows + 8, width), f32),
                pltpu.VMEM((tokens, 2 * width), b16),
                pltpu.VMEM((model_width, tokens), b16),
                pltpu.VMEM((units, tokens), b16),
                pltpu.VMEM((features, tokens), f32),
                pltpu.VMEM((half_side * half_side, 2 * width), f32),
                pltpu.VMEM((half_side * half_side, half_side), b16),
                pltpu.VMEM((cols // width, rows + 8, width), f32),
            ],
        ),
        compiler_params=kernel_params(52),
        name="forward",
    )(corners, latents, *weights)


def run_backward(corners, total, other, rewards, cover, weights, stored, half_side):
    model_width, features = weights[3].shape
    units = weights[0].shape[1]
    tiles = corners.shape[0]
    token_count = half_side * half_side
    steps = tiles // step_tiles(tiles)
    tokens = step_tiles(tiles) * token_count
    panels, rows, width = total.shape
    f32 = jnp.float32
    scale_factor = 16.0 / math.sqrt(tiles * token_count)
    return pl.pallas_call(
        functools.partial(backward_kernel, half_side, scale_factor),
        out_shape=[
            jax.ShapeDtypeStruct((rows, panels * width), f32),
            jax.ShapeDtypeStruct((model_width, units), f32),
            jax.ShapeDtypeStruct((model_width, units), f32),
            jax.ShapeDtypeStruct((units, model_width), f32),
            jax.ShapeDtypeStruct((2 * features, model_width), f32),
        ],
        grid_spec=pltpu.PrefetchScalarGridSpec(
            num_scalar_prefetch=1,
            grid=(steps,),
            in_specs=[whole(total.shape)] * 2
            + [whole(rewards.shape), whole(cover.shape)]
            + [pl.BlockSpec(memory_space=pl.ANY)] * 3
            + [whole(w.shape) for w in weights[3:]]
            + [some_tokens(k.shape[0], k.shape[1] // steps) for k in stored],
            out_specs=[
                whole((rows, panels * width)),
                pl.BlockSpec(memory_space=pl.ANY),
                pl.BlockSpec(memory_space=pl.ANY),
                pl.BlockSpec(memory_space=pl.ANY),
                whole((2 * features, model_width)),
            ],
            scratch_shapes=[
                pltpu.VMEM((panels, rows + 8, width), f32),
                pltpu.VMEM((2 * features, 2 * units), f32),
                pltpu.VMEM((model_width, 2 * features), f32),
                pltpu.VMEM((features, units), f32),
                pltpu.VMEM((features, model_width), f32),
                pltpu.VMEM((features, features), f32),
                pltpu.VMEM((tokens, 2 * width), jnp.bfloat16),
                pltpu.VMEM((features, tokens), jnp.bfloat16),
                pltpu.VMEM((units, tokens), f32),
                pltpu.VMEM((2 * units, tokens), jnp.bfloat16),
                pltpu.VMEM((units, tokens), jnp.bfloat16),
                pltpu.VMEM((2 * features, tokens), jnp.bfloat16),
                pltpu.VMEM((model_width, units), f32),
                pltpu.VMEM((model_width, units), f32),
                pltpu.VMEM((units, model_width), f32),
                *[pltpu.VMEM(w.shape, w.dtype) for w in weights[:3]],
                pltpu.VMEM((half_side * half_side, 2 * width), f32),
                pltpu.VMEM((half_side * half_side, half_side), jnp.bfloat16),
                pltpu.SemaphoreType.DMA((3,)),
                pltpu.SemaphoreType.DMA((3,)),
            ],
        ),
        compiler_params=kernel_params(52),
        name="backward",
    )(corners, total, other, rewards, cover, *weights, *stored)


def pack_kernel(offset_ref, latent_ref, reward_ref, curvature_ref, packed_ref):
    copies, unused, cols = packed_ref.shape
    packed_rows = latent_rows(latent_ref.shape[0])
    slab_rows = latent_ref.shape[0]
    tiles_here = offset_ref.shape[0]
    lane = lax.broadcasted_iota(jnp.int32, (packed_rows - slab_rows, cols), 1)
    digits = jnp.zeros(lane.shape, jnp.int32)
    for tile in range(tiles_here):
        for axis in range(2):
            value = offset_ref[tile, axis]
            at = 2 * tile + axis
            digits = jnp.where(lane == at, value // 256, digits)
            digits = jnp.where(lane == 2 * tiles_here + at, value % 256, digits)
    rewards = split_two(reward_ref[...]) + split_two(curvature_ref[...])
    packed = jnp.concatenate(
        [latent_ref[...].astype(jnp.float32), digits.astype(jnp.float32)]
        + [part.astype(jnp.float32) for part in rewards],
        axis=0,
    ).astype(packed_ref.dtype)
    for copy in range(copies):
        packed_ref[copy, : packed.shape[0]] = packed


def latent_rows(slab_rows):
    return -(-(slab_rows + 1) // 16) * 16


def run_pack(latent, reward_grad, curvature, offsets, slabs):
    slab_rows, cols = latent.shape
    packed_rows = latent_rows(slab_rows) + 4 * slab_rows
    vmem = pl.BlockSpec(memory_space=pltpu.VMEM)
    return pl.pallas_call(
        pack_kernel,
        out_shape=jax.ShapeDtypeStruct((slabs, packed_rows, cols), latent.dtype),
        in_specs=[pl.BlockSpec(memory_space=pltpu.SMEM), vmem, vmem, vmem],
        out_specs=vmem,
        name="pack",
    )(offsets, latent, reward_grad, curvature)


def per_device_replicated(
    latent, reward_grad, curvature, offsets, counts, w_in, w_value, w_gate, w_down, w_out
):
    features, model_width = w_in.shape
    units = w_value.shape[1]
    half_side = S // 2
    token_count = half_side * half_side
    slab_rows, cols = latent.shape
    tiles_here = offsets.shape[0]
    slabs = lax.axis_size("tile")
    tiles = tiles_here * slabs
    rows = slab_rows * slabs
    packed = run_pack(latent, reward_grad, curvature, offsets, slabs)
    latents = lax.all_to_all(packed, "tile", 0, 0)
    digits = latents[:, slab_rows, : 4 * tiles_here].astype(jnp.int32)
    digits = digits.reshape(slabs, 2, tiles_here, 2)
    corners = (digits[:, 0] * 256 + digits[:, 1]).reshape(tiles, 2)

    packed_weights, w_through = run_weights((w_in, w_value, w_gate, w_down, w_out), half_side)
    sums, cover, *stored = run_forward(
        corners, latents, (packed_weights, w_out), half_side, rows
    )
    weights = (w_value, w_gate, w_down, w_out, w_through)
    total, other = over_mp(sums)
    blended, grad_value, grad_gate, grad_down, small = run_backward(
        corners, total, other, latents, cover, weights, stored, half_side
    )
    own = lax.dynamic_slice_in_dim(blended, lax.axis_index("tile") * slab_rows, slab_rows, 0)
    mine, theirs = over_mp(small)
    small = mine + theirs
    return (own, small[:features], grad_value, grad_gate, grad_down, small[features:].T)


def per_device(
    latent, reward_grad, curvature, offsets, counts, w_in, w_value, w_gate, w_down, w_out
):
    tiles = offsets.shape[0] * lax.axis_size("tile")
    stored_bytes = tiles * (S // 2) ** 2 * (8 * w_value.shape[1] + 3 * w_in.shape[1])
    peers = lax.axis_size("mp")
    pairs = w_in.shape[1] <= 2 * w_value.shape[1] and peers > 1 and peers & (peers - 1) == 0 and tiles % peers == 0
    replicate = pairs and stored_bytes <= 40 * 2**20
    plan = per_device_replicated if replicate else per_device_sharded
    return plan(
        latent, reward_grad, curvature, offsets, counts, w_in, w_value, w_gate, w_down, w_out
    )


def solution(mesh):
    return jax.shard_map(
        per_device,
        mesh=mesh,
        in_specs=(
            P("tile", None),
            P("tile", None),
            P("tile", None),
            P("tile", None),
            P("tile", None),
            P(),
            P(None, "mp"),
            P(None, "mp"),
            P("mp", None),
            P(),
        ),
        out_specs=(P("tile", None), P(), P(None, "mp"), P(None, "mp"), P("mp", None), P()),
        check_vma=False,
    )
```
